32 devices in a mesh: mem: 2 (over y), gx: 16 (over z, x, core).
Axes of the slice: x: 2, y: 2, z: 4, core: 2. Of those that a mesh axis runs over, the one named last changes fastest.
Arguments:
- density: float32 [32, 128, 256], P('mem', 'gx'), may hold values from 0.5 to 2
- momenta: float32 [32, 2, 128, 256], P('mem', None, 'gx'), may hold values from -1 to 1
- desired: float32 [2, 128, 256], P(None, 'gx'), may hold values from -1.5 to 1.5
- factor_x: float32 [128, 128], P('gx'), may hold values from -1 to 1, as said below
- factor_y: float32 [256, 128], replicated, may hold values from -1 to 1, as said below
- factor_m: float32 [32, 32], P('mem'), may hold values from -1 to 1, as said below
Outputs:
- core: float32 [32, 3, 128, 128], P('mem', None, 'gx')
The draws below stay inside these ranges and needn't reach their ends.
Inputs may be any that keep to these rules, and one draw needn't show every extreme that they name: `factor_x`: columns are orthonormal. `factor_y`: columns are orthonormal. `factor_m`: columns are orthonormal.
All inputs are finite; a program needn't handle non-finite values.
Results may differ from the reference program's by a relative error of at most 0.00013.
Values sent between devices are 32-bit elements; how exact they have to be, the bound alone decides.
No kernel may reach another device: no remote copies, remote signals or barrier semaphores. Data moves between devices by JAX's collectives and lax.ppermute only.
A program may use at most 64 MiB of HBM per device.

```python
import math
import jax
import jax.numpy as jnp
from jax import lax

MEM_DEV = 16
NY = 256
STEPS = 2
RX = 128
RY = 128
RM = 32
MEMBERS = 32
NX = 128


def draw_factor_x(key, part):
    raw = jax.random.normal(jax.random.fold_in(key, 11), (NX, RX), jnp.float32)
    return jnp.linalg.qr(raw)[0]


def draw_factor_y(key, part):
    raw = jax.random.normal(jax.random.fold_in(key, 12), (NY, RY), jnp.float32)
    return jnp.linalg.qr(raw)[0]


def draw_factor_m(key, part):
    raw = jax.random.normal(jax.random.fold_in(key, 13), (MEMBERS, RM), jnp.float32)
    return jnp.linalg.qr(raw)[0]


def shard_levels(rng, dims, split, low, top_value):
    def one(position, shards_of):
        steps = jax.random.uniform(jax.random.fold_in(jax.random.fold_in(rng, 6), position), (shards_of,), jnp.float32, low / len(split), top_value / len(split))
        return jnp.repeat(jnp.exp(steps), dims[position] // shards_of).reshape((-1,) + (1,) * (len(dims) - position - 1))

    level = one(*split[0])
    for cut in split[1:]:
        level = level * one(*cut)
    return level


def bell_draw(rng, extent, deviation, bound, split=(), dtype=jnp.bfloat16):
    loudness = shard_levels(rng, extent, split, -0.22, 0.18) if split else 1.0
    array = jax.random.normal(rng, extent, jnp.float32) * deviation * loudness
    return jnp.minimum(jnp.maximum(array, -bound), bound).astype(dtype)


def setup_inputs(seed: int = 0) -> dict:
    splits = jax.random.split(jax.random.key(seed), 7)
    density = jnp.clip(0.5 + 1.5 * jax.random.uniform(splits[0], (MEMBERS, NX, NY), jnp.float32) ** shard_levels(splits[0], (MEMBERS, NX, NY), ((0, 2), (1, 16)), -0.2, 0.2), 0.5, 2.0)
    momenta = bell_draw(splits[1], (MEMBERS, 2, NX, NY), 0.3, 1.0, ((0, 2), (2, 16)), jnp.float32)
    desired = bell_draw(splits[2], (2, NX, NY), 0.5, 1.5, ((1, 16),), jnp.float32)
    factor_x = draw_factor_x(jax.random.fold_in(splits[6], 71), 0)
    factor_y = draw_factor_y(jax.random.fold_in(splits[6], 71), 0)
    factor_m = draw_factor_m(jax.random.fold_in(splits[6], 71), 0)
    return dict(density=density, momenta=momenta, desired=desired, factor_x=factor_x, factor_y=factor_y, factor_m=factor_m)


STIFF = 1.0
RELAX = 1.0
DTIME = 0.2

def tendency(fields, desired):
    density = fields[:, 0]
    moment_x = fields[:, 1]
    moment_y = fields[:, 2]
    speed_x = moment_x / density
    speed_y = moment_y / density
    sound = jnp.sqrt(STIFF * density)
    pressure = 0.5 * STIFF * density * density
    conserved = (density, moment_x, moment_y)
    fluxes_x = (moment_x, moment_x * speed_x + pressure, moment_y * speed_x)
    fluxes_y = (moment_y, moment_x * speed_y, moment_y * speed_y + pressure)
    reach_x = jnp.abs(speed_x) + sound
    bound_x = jnp.maximum(reach_x[:, :-1], reach_x[:, 1:])
    reach_y = (jnp.abs(speed_y) + sound)[:, 1:-1]
    bound_y = jnp.maximum(reach_y, jnp.roll(reach_y, -1, axis=-1))
    changes = []
    for quantity, normal_flux, cross_flux in zip(conserved, fluxes_x, fluxes_y):
        face_x = 0.5 * (normal_flux[:, :-1] + normal_flux[:, 1:]) - 0.5 * bound_x * (quantity[:, 1:] - quantity[:, :-1])
        middle = quantity[:, 1:-1]
        cross_mid = cross_flux[:, 1:-1]
        face_y = 0.5 * (cross_mid + jnp.roll(cross_mid, -1, axis=-1)) - 0.5 * bound_y * (jnp.roll(middle, -1, axis=-1) - middle)
        changes.append(-(face_x[:, 1:] - face_x[:, :-1]) - (face_y - jnp.roll(face_y, 1, axis=-1)))
    centre = density[:, 1:-1]
    changes[1] = changes[1] + (centre * desired[0] - moment_x[:, 1:-1]) / RELAX
    changes[2] = changes[2] + (centre * desired[1] - moment_y[:, 1:-1]) / RELAX
    return jnp.stack(changes, axis=1)

def wrap_rows(fields):
    return jnp.concatenate([fields[:, :, -1:], fields, fields[:, :, :1]], axis=2)

def reference(density, momenta, desired, factor_x, factor_y, factor_m):
    block = math.gcd(MEM_DEV, 4)
    count = MEMBERS // block
    dens_blocks = density.reshape(count, block, NX, NY)
    mom_blocks = momenta.reshape(count, block, 2, NX, NY)
    fac_blocks = factor_m.reshape(count, block, RM)
    highest = lax.Precision.HIGHEST

    def advance(carry, inputs):
        dens_part, mom_part, fac_part = inputs
        fields = jnp.concatenate([dens_part[:, None], mom_part], axis=1)
        for repeat in range(STEPS):
            sectioned = fields + DTIME * tendency(wrap_rows(fields), desired)
            second = sectioned + DTIME * tendency(wrap_rows(sectioned), desired)
            fields = 0.5 * fields + 0.5 * second
        along_y = jnp.einsum('mcxy,yb->mcxb', fields, factor_y, precision=highest)
        along_x = jnp.einsum('mcxb,xa->mcab', along_y, factor_x, precision=highest)
        part = jnp.einsum('mcab,mk->kcab', along_x, fac_part, precision=highest)
        return (carry + part, None)
    start = jnp.zeros((RM, 3, RX, RY), jnp.float32)
    core, unused = lax.scan(advance, start, (dens_blocks, mom_blocks, fac_blocks))
    return core
```

```python
import functools

import jax
import jax.numpy as jnp
from jax import lax
from jax.experimental import pallas as pl
from jax.experimental.pallas import tpu as pltpu
from jax.sharding import PartitionSpec as P

STEPS = 2


STIFF = 1.0
RELAX = 1.0
DTIME = 0.2

HIGHEST = lax.Precision.HIGHEST
LANES = 128
SUBLANES = 8


def with_halo(cells, sides, width):
    for axis, dim in sides:
        count = lax.axis_size(axis)
        head = lax.slice_in_dim(cells, 0, width, axis=dim)
        tail = lax.slice_in_dim(cells, cells.shape[dim] - width, cells.shape[dim], axis=dim)
        cells = jnp.concatenate(
            [
                lax.ppermute(tail, axis, [(i, (i + 1) % count) for i in range(count)]),
                cells,
                lax.ppermute(head, axis, [((i + 1) % count, i) for i in range(count)]),
            ],
            axis=dim,
        )
    return cells


def tendency(fields, desired):
    density = fields[:, 0]
    moment_x = fields[:, 1]
    moment_y = fields[:, 2]
    speed_x = moment_x / density
    speed_y = moment_y / density
    sound = jnp.sqrt(STIFF * density)
    pressure = 0.5 * STIFF * density * density
    conserved = (density, moment_x, moment_y)
    fluxes_x = (moment_x, moment_x * speed_x + pressure, moment_y * speed_x)
    fluxes_y = (moment_y, moment_x * speed_y, moment_y * speed_y + pressure)
    reach_x = jnp.abs(speed_x) + sound
    bound_x = jnp.maximum(reach_x[:, :-1], reach_x[:, 1:])
    reach_y = (jnp.abs(speed_y) + sound)[:, 1:-1]
    bound_y = jnp.maximum(reach_y, jnp.roll(reach_y, -1, axis=-1))
    changes = []
    for quantity, normal_flux, cross_flux in zip(conserved, fluxes_x, fluxes_y):
        face_x = 0.5 * (normal_flux[:, :-1] + normal_flux[:, 1:]) - 0.5 * bound_x * (
            quantity[:, 1:] - quantity[:, :-1]
        )
        middle = quantity[:, 1:-1]
        cross_mid = cross_flux[:, 1:-1]
        face_y = 0.5 * (cross_mid + jnp.roll(cross_mid, -1, axis=-1)) - 0.5 * bound_y * (
            jnp.roll(middle, -1, axis=-1) - middle
        )
        changes.append(-(face_x[:, 1:] - face_x[:, :-1]) - (face_y - jnp.roll(face_y, 1, axis=-1)))
    centre = density[:, 1:-1]
    changes[1] = changes[1] + (centre * desired[0] - moment_x[:, 1:-1]) / RELAX
    changes[2] = changes[2] + (centre * desired[1] - moment_y[:, 1:-1]) / RELAX
    return jnp.stack(changes, axis=1)


def single_rims(fields):
    return with_halo(fields, (("gx", 2),), 1)


def plain(density, momenta, desired, factor_x, factor_y, factor_m):
    fields = jnp.concatenate([density[:, None], momenta], axis=1)
    for repeat in range(STEPS):
        sectioned = fields + DTIME * tendency(single_rims(fields), desired)
        second = sectioned + DTIME * tendency(single_rims(sectioned), desired)
        fields = 0.5 * fields + 0.5 * second
    along_y = jnp.einsum("mcxy,yb->mcxb", fields, factor_y, precision=HIGHEST)
    spread = lax.all_to_all(along_y, "gx", split_axis=3, concat_axis=2, tiled=True)
    projected = jnp.einsum(
        "mcxb,xa->mcab",
        spread,
        lax.all_gather(factor_x, "gx", axis=0, tiled=True),
        precision=HIGHEST,
    )
    returned = lax.all_to_all(projected, "gx", split_axis=2, concat_axis=3, tiled=True)
    member_terms = jnp.einsum("mcab,mk->kcab", returned, factor_m, precision=HIGHEST)
    return lax.psum_scatter(member_terms, "mem", scatter_dimension=0, tiled=True)


def cell_terms(q):
    rho, mx, my = q
    root = lax.rsqrt(rho)
    inverse = root * root
    sound = rho * root
    u = mx * inverse
    v = my * inverse
    pressure = (0.5 * STIFF) * (rho * rho)
    cross = my * u
    return dict(
        q=q,
        f=(mx, mx * u + pressure, cross),
        g=(my, cross, my * v + pressure),
        ax=jnp.abs(u) + sound,
        ay=jnp.abs(v) + sound,
    )


def x_face(low, high):
    bound = jnp.maximum(low["ax"], high["ax"])
    return tuple(
        fa + fb - bound * (b - a)
        for fa, fb, a, b in zip(low["f"], high["f"], low["q"], high["q"])
    )


def y_difference(row):
    axis = row["ay"].ndim - 1
    size = row["ay"].shape[axis]
    after = lambda a: pltpu.roll(a, size - 1, axis)
    before = lambda a: pltpu.roll(a, 1, axis)
    moved_q = tuple(after(a) for a in row["q"])
    moved_g = (moved_q[2], after(row["g"][1]), after(row["g"][2]))
    bound = jnp.maximum(row["ay"], after(row["ay"]))
    face = tuple(
        ga + gb - bound * (b - a)
        for ga, gb, a, b in zip(row["g"], moved_g, row["q"], moved_q)
    )
    return tuple(a - before(a) for a in face)


def section(row, low_face, high_face, wish):
    cross = y_difference(row)
    rho, mx, my = row["q"]
    half = 0.5 * DTIME
    spread = tuple(h - l + d for h, l, d in zip(high_face, low_face, cross))
    keep = 1.0 - DTIME / RELAX
    wished = (DTIME / RELAX) * rho
    return (
        rho - half * spread[0],
        keep * mx + wished * wish[0] - half * spread[1],
        keep * my + wished * wish[1] - half * spread[2],
    )


def advance_kernel(
    n_gx, left_d, own_d, left_m, own_m, left_w, own_w, fy, fx, fm, out, state, *tiled
):
    rows = own_w.shape[0] // 2
    members = own_d.shape[0] // rows
    tiles = own_d.shape[1] // LANES
    for whole, cut in zip((left_d, own_d, left_m, own_m), tiled):
        for t in range(tiles):
            cut[t] = whole[:, t * LANES : (t + 1) * LANES]
    left_d, own_d, left_m, own_m = tiled

    def every(ref, first, stride):
        return jnp.concatenate(
            [ref[t, pl.ds(first, SUBLANES, stride=stride), :] for t in range(tiles)], axis=1
        )

    count = 2 * rows
    sections = 2 * STEPS
    for group in range(members // SUBLANES):
        def load(x):
            d, m = (left_d, left_m) if x < rows else (own_d, own_m)
            at = x % rows
            first = group * SUBLANES
            return (
                every(d, first * rows + at, rows),
                every(m, first * 2 * rows + at, 2 * rows),
                every(m, (first * 2 + 1) * rows + at, 2 * rows),
            )

        def wish(x):
            w = left_w if x < rows else own_w
            at = x % rows
            return tuple(
                jnp.broadcast_to(w[pl.ds(c * rows + at, 1), :], (SUBLANES, w.shape[1]))
                for c in range(2)
            )

        cells = [{} for _ in range(sections + 1)]
        faces = [{} for _ in range(sections)]
        for t in range(count):
            cells[0][t] = cell_terms(load(t))
            if t:
                faces[0][t - 1] = x_face(cells[0][t - 1], cells[0][t])
            for s in range(1, sections + 1):
                x = t - s
                if x < s:
                    break
                new = section(cells[s - 1][x], faces[s - 1][x - 1], faces[s - 1][x], wish(x))
                if s % 2 == 0:
                    old = cells[s - 2][x]["q"]
                    new = tuple(0.5 * a + 0.5 * b for a, b in zip(old, new))
                if s < sections:
                    cells[s][x] = cell_terms(new)
                    if x > s:
                        faces[s][x - 1] = x_face(cells[s][x - 1], cells[s][x])
                else:
                    at = (x - sections) * members + group * SUBLANES
                    for c in range(3):
                        state[pl.ds(c * rows * members + at, SUBLANES), :] = new[c]
    devices = 2 * n_gx
    shares = fy.shape[1] // devices
    height = out.shape[0] // devices
    for c in range(3):
        block = state[pl.ds(c * rows * members, rows * members), :]
        along = jnp.dot(block, fy[...], precision=HIGHEST, preferred_element_type=jnp.float32)
        turned = along.T
        for r in range(shares):
            out[pl.ds(c * shares + r, devices, stride=height), :] = turned[
                r * devices : (r + 1) * devices
            ]
    mem, gx = lax.axis_index("mem"), lax.axis_index("gx")
    half = rows // 2
    for r in range(half):
        line = fx[pl.ds(mem * half + r, 1), :]
        out[pl.ds(3 * shares + r, devices, stride=height), :] = jnp.broadcast_to(
            line, (devices, line.shape[1])
        )
    line = fm[pl.ds(gx, 1), :]
    line = jnp.concatenate([line] * (LANES // line.shape[1]), axis=1)
    out[pl.ds(3 * shares + half, devices, stride=height), :] = jnp.broadcast_to(
        line, (devices, LANES)
    )


def project_kernel(n_gx, rows, shares, rm, inp, out, blocks, tall):
    devices = 2 * n_gx
    members = n_gx
    height = inp.shape[0] // devices
    half = rows // 2
    pieces = 3 * shares
    columns = [inp[pl.ds(j, devices, stride=height), :] for j in range(pieces)]
    lhs = jnp.concatenate(
        [
            jnp.concatenate([d[:n_gx] for d in columns], axis=0),
            jnp.concatenate([d[n_gx:] for d in columns], axis=0),
        ],
        axis=1,
    )
    fm = inp[pl.ds(pieces + half, devices, stride=height), :]
    group = lax.broadcasted_iota(jnp.int32, (members, LANES), 1) // rm
    per = LANES // rm
    zero = jnp.zeros((members, LANES), jnp.float32)
    lines = []
    for mem in range(2):
        part = fm[mem * members : (mem + 1) * members]
        for x in range(rows):
            kept = jnp.where(group == x % per, part, 0.0)
            lines.append(
                jnp.concatenate(
                    [kept if x // per == t else zero for t in range(rows // per)], axis=1
                )
            )
    diagonal = jnp.concatenate(lines, axis=0)
    mixed = jnp.dot(lhs, diagonal, precision=HIGHEST, preferred_element_type=jnp.float32)
    lows = rm // 2
    orders = (range(pieces), [j % pieces for j in range(pieces - shares, 2 * pieces - shares)])
    for x in range(rows):
        for k in range(2):
            blocks[pl.ds(x * n_gx, n_gx), pl.ds(k * pieces * lows, pieces * lows)] = jnp.concatenate(
                [
                    mixed[j * n_gx : (j + 1) * n_gx, x * rm + k * lows : x * rm + (k + 1) * lows]
                    for j in orders[k]
                ],
                axis=1,
            )
    halves = [inp[pl.ds(pieces + r, devices, stride=height), :] for r in range(half)]
    lines = []
    for r in range(half):
        late = halves[r][n_gx:]
        lines.append(pltpu.roll(late, 1, 0))
    for r in range(half):
        lines.append(halves[r][:n_gx])
    fx = jnp.concatenate(lines, axis=0)
    core = jnp.dot(fx.T, blocks[...], precision=HIGHEST, preferred_element_type=jnp.float32)
    high = out.shape[0] // devices
    for t in range(3):
        tall[t] = core[:, t * LANES : (t + 1) * LANES]
    lane = lax.broadcasted_iota(jnp.int32, (n_gx, LANES), 1)
    for a in range(SUBLANES):
        for k in range(2):
            out[pl.ds(k * n_gx * high + a, n_gx, stride=high), :] = tall[
                2 * k, pl.ds(a, n_gx, stride=SUBLANES), :
            ]
    for i in range(SUBLANES // 2):
        upper = tall[1, pl.ds(i, n_gx, stride=SUBLANES), :]
        lower = tall[1, pl.ds(i + SUBLANES // 2, n_gx, stride=SUBLANES), :]
        first = jnp.where(lane < LANES // 2, upper, pltpu.roll(lower, LANES // 2, 1))
        second = jnp.where(lane < LANES // 2, pltpu.roll(upper, LANES // 2, 1), lower)
        out[pl.ds(SUBLANES + i, n_gx, stride=high), :] = first
        out[pl.ds(n_gx * high + SUBLANES + i, n_gx, stride=high), :] = second


def gather_kernel(shares, lows, inp, out):
    devices = LANES // shares
    high = inp.shape[0] // devices
    quarter = SUBLANES // 2
    step = out.shape[0] // lows

    def turn(first):
        return jnp.concatenate(
            [inp[pl.ds(first + i, devices, stride=high), :] for i in range(quarter)], axis=0
        ).T

    def place(turned, base, c, a0):
        for i in range(quarter):
            line = jnp.concatenate(
                [
                    turned[base + r * lows : base + (r + 1) * lows, i * devices : (i + 1) * devices]
                    for r in range(shares)
                ],
                axis=1,
            )
            out[pl.ds(c * SUBLANES + a0 + i, lows, stride=step), :] = line

    for h in range(2):
        turned = turn(h * quarter)
        for c in range(2):
            place(turned, c * shares * lows, c, h * quarter)
    turned = turn(SUBLANES)
    for h in range(2):
        place(turned, h * shares * lows, 2, h * quarter)


def exchange(chunks, devices):
    block = chunks.reshape(devices, chunks.shape[0] // devices, 1, chunks.shape[1])
    moved = lax.all_to_all(block, ("mem", "gx"), split_axis=0, concat_axis=0, tiled=True)
    return moved.reshape(chunks.shape)


def laid_out(density, factor_x, factor_y, factor_m):
    members, rows, cells_y = density.shape
    n_mem, n_gx = lax.axis_size("mem"), lax.axis_size("gx")
    rx, ry, rm = factor_x.shape[1], factor_y.shape[1], factor_m.shape[1]
    shares = ry // (n_mem * n_gx)
    return (
        n_mem == 2
        and rows == 4 * STEPS == SUBLANES
        and members == n_gx
        and members * rows == LANES
        and members % SUBLANES == 0
        and cells_y % LANES == 0
        and rx == LANES == n_gx * SUBLANES
        and ry == LANES == shares * n_mem * n_gx
        and shares * rm == LANES
        and shares * rm // 2 * 2 == LANES
        and rows * rm == 2 * LANES
    )


def on_device(density, momenta, desired, factor_x, factor_y, factor_m):
    if not laid_out(density, factor_x, factor_y, factor_m):
        return plain(density, momenta, desired, factor_x, factor_y, factor_m)
    members, rows, cells_y = density.shape
    n_gx = lax.axis_size("gx")
    devices = 2 * n_gx
    rx, ry, rm = factor_x.shape[1], factor_y.shape[1], factor_m.shape[1]
    shares = ry // devices
    forward = [(i, (i + 1) % n_gx) for i in range(n_gx)]
    own = (density, momenta, desired)
    left = [lax.ppermute(a, "gx", forward) for a in own]
    flat = [a.reshape(-1, cells_y) for pair in zip(left, own) for a in pair]
    params = pltpu.CompilerParams(vmem_limit_bytes=32 * 1024 * 1024)
    height = 3 * shares + rows // 2 + 1
    sent = pl.pallas_call(
        functools.partial(advance_kernel, n_gx),
        out_shape=jax.ShapeDtypeStruct((devices * height, LANES), jnp.float32),
        scratch_shapes=[pltpu.VMEM((3 * rows * members, cells_y), jnp.float32)]
        + [pltpu.VMEM((cells_y // LANES, a.shape[0], LANES), jnp.float32) for a in flat[:4]],
        compiler_params=params,
        name="advance",
    )(*flat, factor_y, factor_x, factor_m)
    got = exchange(sent, devices)
    lows = rm // 2
    high = 3 * shares * lows * SUBLANES // LANES
    sent = pl.pallas_call(
        functools.partial(project_kernel, n_gx, rows, shares, rm),
        out_shape=jax.ShapeDtypeStruct((devices * high, LANES), jnp.float32),
        scratch_shapes=[
            pltpu.VMEM((rows * n_gx, 3 * shares * rm), jnp.float32),
            pltpu.VMEM((3, rx, LANES), jnp.float32),
        ],
        compiler_params=params,
        name="project",
    )(got)
    got = exchange(sent, devices)
    core = pl.pallas_call(
        functools.partial(gather_kernel, shares, lows),
        out_shape=jax.ShapeDtypeStruct((lows * 3 * SUBLANES, LANES), jnp.float32),
        compiler_params=params,
        name="gather",
    )(got)
    return core.reshape(lows, 3, SUBLANES, ry)


def solution(mesh):
    return jax.shard_map(
        on_device,
        mesh=mesh,
        in_specs=(
            P("mem", "gx", None),
            P("mem", None, "gx", None),
            P(None, "gx", None),
            P("gx", None),
            P(),
            P("mem", None),
        ),
        out_specs=P("mem", None, "gx", None),
        check_vma=False,
    )
```

```python
import functools

import jax
import jax.numpy as jnp
from jax import lax
from jax.experimental import pallas as pl
from jax.experimental.pallas import tpu as pltpu
from jax.sharding import PartitionSpec as P

STEPS = 2


STIFF = 1.0
RELAX = 1.0
DTIME = 0.2

HIGHEST = lax.Precision.HIGHEST
LANES = 128
SUBLANES = 8


def with_halo(cells, sides, width):
    for axis, dim in sides:
        count = lax.axis_size(axis)
        head = lax.slice_in_dim(cells, 0, width, axis=dim)
        tail = lax.slice_in_dim(cells, cells.shape[dim] - width, cells.shape[dim], axis=dim)
        cells = jnp.concatenate(
            [
                lax.ppermute(tail, axis, [(i, (i + 1) % count) for i in range(count)]),
                cells,
                lax.ppermute(head, axis, [((i + 1) % count, i) for i in range(count)]),
            ],
            axis=dim,
        )
    return cells


def tendency(fields, desired):
    density = fields[:, 0]
    moment_x = fields[:, 1]
    moment_y = fields[:, 2]
    speed_x = moment_x / density
    speed_y = moment_y / density
    sound = jnp.sqrt(STIFF * density)
    pressure = 0.5 * STIFF * density * density
    conserved = (density, moment_x, moment_y)
    fluxes_x = (moment_x, moment_x * speed_x + pressure, moment_y * speed_x)
    fluxes_y = (moment_y, moment_x * speed_y, moment_y * speed_y + pressure)
    reach_x = jnp.abs(speed_x) + sound
    bound_x = jnp.maximum(reach_x[:, :-1], reach_x[:, 1:])
    reach_y = (jnp.abs(speed_y) + sound)[:, 1:-1]
    bound_y = jnp.maximum(reach_y, jnp.roll(reach_y, -1, axis=-1))
    changes = []
    for quantity, normal_flux, cross_flux in zip(conserved, fluxes_x, fluxes_y):
        face_x = 0.5 * (normal_flux[:, :-1] + normal_flux[:, 1:]) - 0.5 * bound_x * (
            quantity[:, 1:] - quantity[:, :-1]
        )
        middle = quantity[:, 1:-1]
        cross_mid = cross_flux[:, 1:-1]
        face_y = 0.5 * (cross_mid + jnp.roll(cross_mid, -1, axis=-1)) - 0.5 * bound_y * (
            jnp.roll(middle, -1, axis=-1) - middle
        )
        changes.append(-(face_x[:, 1:] - face_x[:, :-1]) - (face_y - jnp.roll(face_y, 1, axis=-1)))
    centre = density[:, 1:-1]
    changes[1] = changes[1] + (centre * desired[0] - moment_x[:, 1:-1]) / RELAX
    changes[2] = changes[2] + (centre * desired[1] - moment_y[:, 1:-1]) / RELAX
    return jnp.stack(changes, axis=1)


def single_rims(fields):
    return with_halo(fields, (("gx", 2),), 1)


def plain(density, momenta, desired, factor_x, factor_y, factor_m):
    fields = jnp.concatenate([density[:, None], momenta], axis=1)
    for repeat in range(STEPS):
        sectioned = fields + DTIME * tendency(single_rims(fields), desired)
        second = sectioned + DTIME * tendency(single_rims(sectioned), desired)
        fields = 0.5 * fields + 0.5 * second
    along_y = jnp.einsum("mcxy,yb->mcxb", fields, factor_y, precision=HIGHEST)
    spread = lax.all_to_all(along_y, "gx", split_axis=3, concat_axis=2, tiled=True)
    projected = jnp.einsum(
        "mcxb,xa->mcab",
        spread,
        lax.all_gather(factor_x, "gx", axis=0, tiled=True),
        precision=HIGHEST,
    )
    returned = lax.all_to_all(projected, "gx", split_axis=2, concat_axis=3, tiled=True)
    member_terms = jnp.einsum("mcab,mk->kcab", returned, factor_m, precision=HIGHEST)
    return lax.psum_scatter(member_terms, "mem", scatter_dimension=0, tiled=True)


def cell_terms(q):
    rho, mx, my = q
    root = lax.rsqrt(rho)
    inverse = root * root
    sound = rho * root
    u = mx * inverse
    v = my * inverse
    pressure = (0.5 * STIFF) * (rho * rho)
    cross = my * u
    return dict(
        q=q,
        f=(mx, mx * u + pressure, cross),
        g=(my, cross, my * v + pressure),
        ax=jnp.abs(u) + sound,
        ay=jnp.abs(v) + sound,
    )


def x_face(low, high):
    bound = jnp.maximum(low["ax"], high["ax"])
    return tuple(
        fa + fb - bound * (b - a)
        for fa, fb, a, b in zip(low["f"], high["f"], low["q"], high["q"])
    )


def y_difference(row):
    axis = row["ay"].ndim - 1
    size = row["ay"].shape[axis]
    after = lambda a: pltpu.roll(a, size - 1, axis)
    before = lambda a: pltpu.roll(a, 1, axis)
    moved_q = tuple(after(a) for a in row["q"])
    moved_g = (moved_q[2], after(row["g"][1]), after(row["g"][2]))
    bound = jnp.maximum(row["ay"], after(row["ay"]))
    face = tuple(
        ga + gb - bound * (b - a)
        for ga, gb, a, b in zip(row["g"], moved_g, row["q"], moved_q)
    )
    return tuple(a - before(a) for a in face)


def section(row, low_face, high_face, wish):
    cross = y_difference(row)
    rho, mx, my = row["q"]
    half = 0.5 * DTIME
    spread = tuple(h - l + d for h, l, d in zip(high_face, low_face, cross))
    keep = 1.0 - DTIME / RELAX
    wished = (DTIME / RELAX) * rho
    return (
        rho - half * spread[0],
        keep * mx + wished * wish[0] - half * spread[1],
        keep * my + wished * wish[1] - half * spread[2],
    )


def start_kernel(d, m, w, fy, own_d, own_m, own_w, own_fy, near, far, sems):
    tiles = own_d.shape[0]
    copies = []
    for whole, cut in ((d, own_d), (m, own_m), (w, own_w)):
        for t in range(tiles):
            copies.append((whole.at[:, pl.ds(t * LANES, LANES)], cut.at[t]))
    copies.append((fy, own_fy))
    copies = [
        pltpu.make_async_copy(source, target, sems.at[i])
        for i, (source, target) in enumerate(copies)
    ]
    for copy in copies:
        copy.start()
    odd = lax.rem(lax.axis_index("gx"), 2)
    rows = own_w.shape[1] // 2
    half = rows // 2
    for copy in copies:
        copy.wait()
    for target, first in ((near, half * (1 - odd)), (far, half * odd)):
        for t in range(tiles):
            base = 0
            for cut in (own_d, own_m, own_w):
                lines = cut.shape[1] // rows
                for i in range(half):
                    target[t, pl.ds(base + i, lines, stride=half), :] = cut[
                        t, pl.ds(first + i, lines, stride=rows), :
                    ]
                base += lines * half


class Strip:
    def __init__(self, group, own, near, far):
        self.group, self.own, self.near, self.far = group, own, near, far
        self.rows = own[2].shape[1] // 2
        self.half = self.rows // 2
        self.members = own[0].shape[1] // self.rows
        self.tiles = own[0].shape[0]
        self.odd = lax.rem(lax.axis_index("gx"), 2)
        self.sign = (1 - 2 * self.odd).astype(jnp.float32)

    def every(self, ref, first, count, stride):
        parts = [ref[t, pl.ds(first, count, stride=stride), :] for t in range(self.tiles)]
        return jnp.concatenate(parts, axis=1)

    def place(self, x):
        if x < self.half:
            ref, at, lines = self.far, x, self.half
        elif x < self.half + self.rows:
            ref, at, lines = self.own, x - self.half, self.rows
        else:
            ref, at, lines = self.near, x - self.half - self.rows, self.half
        return ref, self.odd * (lines - 1) + (1 - 2 * self.odd) * at, lines

    def load(self, x):
        ref, at, lines = self.place(x)
        if ref is self.own:
            d, m = ref[0], ref[1]
            base = 0
        else:
            d = m = ref
            base = self.members * lines
        first = self.group * SUBLANES
        rho = self.every(d, first * lines + at, SUBLANES, lines)
        mx = self.every(m, base + first * 2 * lines + at, SUBLANES, 2 * lines)
        my = self.every(m, base + (first * 2 + 1) * lines + at, SUBLANES, 2 * lines)
        return rho, self.sign * mx, my

    def wish(self, x):
        ref, at, lines = self.place(x)
        if ref is self.own:
            ref, base = ref[2], 0
        else:
            base = 3 * self.members * lines
        line = [self.every(ref, base + c * lines + at, 1, 1) for c in range(2)]
        line[0] = self.sign * line[0]
        return tuple(jnp.broadcast_to(a, (SUBLANES, a.shape[1])) for a in line)


def march(count, computed, fetch, wish, emit):
    sections = len(computed) - 1
    known, terms, faces = {}, {}, {}

    def value(s, x):
        if (s, x) not in known:
            if x in computed[s]:
                new = section(
                    cell(s - 1, x), face(s - 1, x - 1), face(s - 1, x), wish(x)
                )
                if s % 2 == 0:
                    new = tuple(0.5 * a + 0.5 * b for a, b in zip(value(s - 2, x), new))
                emit(s, x, new)
            else:
                new = fetch(s, x)
            known[s, x] = new
        return known[s, x]

    def cell(s, x):
        if (s, x) not in terms:
            terms[s, x] = cell_terms(value(s, x))
        return terms[s, x]

    def face(s, x):
        if (s, x) not in faces:
            faces[s, x] = x_face(cell(s, x), cell(s, x + 1))
        return faces[s, x]

    for t in range(count):
        for s in range(1, sections + 1):
            if t - s in computed[s]:
                value(s, t - s)


def edge_line(s, x, half, members):
    return ((s - 1) * 2 + x - half - s) * 3 * members


def turn_projected(state, fy, members, c, count):
    lines = count * members
    block = state[pl.ds(c * lines, lines), :]
    along = jnp.dot(block, fy[...], precision=HIGHEST, preferred_element_type=jnp.float32)
    return along.T


def inner_kernel(own_d, own_m, own_w, near, fy, edges, turned, state):
    rows = own_w.shape[1] // 2
    half = rows // 2
    members = own_d.shape[1] // rows
    sections = 2 * STEPS
    count = 2 * rows
    for group in range(members // SUBLANES):
        strip = Strip(group, (own_d, own_m, own_w), near, None)

        def emit(s, x, q):
            if s == sections:
                for c in range(3):
                    at = (c * half + x - rows) * members + group * SUBLANES
                    state[pl.ds(at, SUBLANES), :] = q[c]
            elif x - half - s in (0, 1):
                for c in range(3):
                    at = edge_line(s, x, half, members) + c * members + group * SUBLANES
                    edges[pl.ds(at, SUBLANES), :] = q[c]

        computed = [range(0)] + [range(half + s, count - s) for s in range(1, sections + 1)]
        march(count, computed, lambda s, x: strip.load(x), strip.wish, emit)
    for c in range(3):
        part = turn_projected(state, fy, members, c, half)
        turned[c] = jnp.concatenate([jnp.zeros_like(part), part], axis=1)


def outer_kernel(
    n_gx, own_d, own_m, own_w, far, fy, edges, turned, fx, fm, out, state
):
    rows = own_w.shape[1] // 2
    half = rows // 2
    members = own_d.shape[1] // rows
    sections = 2 * STEPS
    for group in range(members // SUBLANES):
        strip = Strip(group, (own_d, own_m, own_w), None, far)

        def fetch(s, x):
            if s == 0:
                return strip.load(x)
            at = edge_line(s, x, half, members) + group * SUBLANES
            return tuple(edges[pl.ds(at + c * members, SUBLANES), :] for c in range(3))

        def emit(s, x, q):
            if s == sections:
                for c in range(3):
                    at = (c * half + x - half) * members + group * SUBLANES
                    state[pl.ds(at, SUBLANES), :] = q[c]

        computed = [range(0)] + [range(s, half + s) for s in range(1, sections + 1)]
        march(rows + sections, computed, fetch, strip.wish, emit)
    devices = 2 * n_gx
    shares = fy.shape[1] // devices
    height = out.shape[0] // devices
    odd = lax.rem(lax.axis_index("gx"), 2)
    sign = (1 - 2 * odd).astype(jnp.float32)
    for c in range(3):
        part = turn_projected(state, fy, members, c, half)
        whole = jnp.concatenate([part, turned[c][:, half * members :]], axis=1)
        if c == 1:
            whole = sign * whole
        for r in range(shares):
            out[pl.ds(c * shares + r, devices, stride=height), :] = whole[
                r * devices : (r + 1) * devices
            ]
    mem, gx = lax.axis_index("mem"), lax.axis_index("gx")
    for r in range(half):
        line = fx[pl.ds(mem * half + r, 1), :]
        out[pl.ds(3 * shares + r, devices, stride=height), :] = jnp.broadcast_to(
            line, (devices, line.shape[1])
        )
    line = fm[pl.ds(gx, 1), :]
    line = jnp.concatenate([line] * (LANES // line.shape[1]), axis=1)
    out[pl.ds(3 * shares + half, devices, stride=height), :] = jnp.broadcast_to(
        line, (devices, LANES)
    )


def project_kernel(n_gx, rows, shares, rm, inp, out, blocks, tall):
    devices = 2 * n_gx
    members = n_gx
    height = inp.shape[0] // devices
    half = rows // 2
    pieces = 3 * shares
    columns = [inp[pl.ds(j, devices, stride=height), :] for j in range(pieces)]
    lhs = jnp.concatenate(
        [
            jnp.concatenate([d[:n_gx] for d in columns], axis=0),
            jnp.concatenate([d[n_gx:] for d in columns], axis=0),
        ],
        axis=1,
    )
    fm = inp[pl.ds(pieces + half, devices, stride=height), :]
    group = lax.broadcasted_iota(jnp.int32, (members, LANES), 1) // rm
    per = LANES // rm
    zero = jnp.zeros((members, LANES), jnp.float32)
    lines = []
    for mem in range(2):
        part = fm[mem * members : (mem + 1) * members]
        for x in range(rows):
            kept = jnp.where(group == x % per, part, 0.0)
            lines.append(
                jnp.concatenate(
                    [kept if x // per == t else zero for t in range(rows // per)], axis=1
                )
            )
    diagonal = jnp.concatenate(lines, axis=0)
    mixed = jnp.dot(lhs, diagonal, precision=HIGHEST, preferred_element_type=jnp.float32)
    lows = rm // 2
    orders = (range(pieces), [j % pieces for j in range(pieces - shares, 2 * pieces - shares)])
    for x in range(rows):
        for k in range(2):
            blocks[pl.ds(x * n_gx, n_gx), pl.ds(k * pieces * lows, pieces * lows)] = jnp.concatenate(
                [
                    mixed[j * n_gx : (j + 1) * n_gx, x * rm + k * lows : x * rm + (k + 1) * lows]
                    for j in orders[k]
                ],
                axis=1,
            )
    halves = [inp[pl.ds(pieces + r, devices, stride=height), :] for r in range(half)]
    lines = [a[:n_gx] for a in halves] + [a[n_gx:] for a in halves]
    odd = lax.broadcasted_iota(jnp.int32, (n_gx, LANES), 0) % 2 == 1
    lines = [jnp.where(odd, lines[rows - 1 - r], lines[r]) for r in range(rows)]
    fx = jnp.concatenate(lines, axis=0)
    core = jnp.dot(fx.T, blocks[...], precision=HIGHEST, preferred_element_type=jnp.float32)
    high = out.shape[0] // devices
    for t in range(3):
        tall[t] = core[:, t * LANES : (t + 1) * LANES]
    lane = lax.broadcasted_iota(jnp.int32, (n_gx, LANES), 1)
    for a in range(SUBLANES):
        for k in range(2):
            out[pl.ds(k * n_gx * high + a, n_gx, stride=high), :] = tall[
                2 * k, pl.ds(a, n_gx, stride=SUBLANES), :
            ]
    for i in range(SUBLANES // 2):
        upper = tall[1, pl.ds(i, n_gx, stride=SUBLANES), :]
        lower = tall[1, pl.ds(i + SUBLANES // 2, n_gx, stride=SUBLANES), :]
        first = jnp.where(lane < LANES // 2, upper, pltpu.roll(lower, LANES // 2, 1))
        second = jnp.where(lane < LANES // 2, pltpu.roll(upper, LANES // 2, 1), lower)
        out[pl.ds(SUBLANES + i, n_gx, stride=high), :] = first
        out[pl.ds(n_gx * high + SUBLANES + i, n_gx, stride=high), :] = second


def gather_kernel(shares, lows, inp, out):
    devices = LANES // shares
    high = inp.shape[0] // devices
    quarter = SUBLANES // 2
    step = out.shape[0] // lows

    def turn(first):
        return jnp.concatenate(
            [inp[pl.ds(first + i, devices, stride=high), :] for i in range(quarter)], axis=0
        ).T

    def place(turned, base, c, a0):
        for i in range(quarter):
            line = jnp.concatenate(
                [
                    turned[base + r * lows : base + (r + 1) * lows, i * devices : (i + 1) * devices]
                    for r in range(shares)
                ],
                axis=1,
            )
            out[pl.ds(c * SUBLANES + a0 + i, lows, stride=step), :] = line

    for h in range(2):
        turned = turn(h * quarter)
        for c in range(2):
            place(turned, c * shares * lows, c, h * quarter)
    turned = turn(SUBLANES)
    for h in range(2):
        place(turned, h * shares * lows, 2, h * quarter)


def exchange(chunks, devices):
    block = chunks.reshape(devices, chunks.shape[0] // devices, 1, chunks.shape[1])
    moved = lax.all_to_all(block, ("mem", "gx"), split_axis=0, concat_axis=0, tiled=True)
    return moved.reshape(chunks.shape)


def laid_out(density, factor_x, factor_y, factor_m):
    members, rows, cells_y = density.shape
    n_mem, n_gx = lax.axis_size("mem"), lax.axis_size("gx")
    rx, ry, rm = factor_x.shape[1], factor_y.shape[1], factor_m.shape[1]
    shares = ry // (n_mem * n_gx)
    return (
        n_mem == 2
        and rows == 4 * STEPS == SUBLANES
        and members == n_gx
        and n_gx % 2 == 0
        and members * rows == LANES
        and members % SUBLANES == 0
        and cells_y % LANES == 0
        and rx == LANES == n_gx * SUBLANES
        and ry == LANES == shares * n_mem * n_gx
        and shares * rm == LANES
        and shares * rm // 2 * 2 == LANES
        and rows * rm == 2 * LANES
    )


def on_device(density, momenta, desired, factor_x, factor_y, factor_m):
    if not laid_out(density, factor_x, factor_y, factor_m):
        return plain(density, momenta, desired, factor_x, factor_y, factor_m)
    members, rows, cells_y = density.shape
    n_gx = lax.axis_size("gx")
    devices = 2 * n_gx
    rx, ry, rm = factor_x.shape[1], factor_y.shape[1], factor_m.shape[1]
    shares = ry // devices
    params = pltpu.CompilerParams(vmem_limit_bytes=32 * 1024 * 1024)
    vmem = pl.BlockSpec(memory_space=pltpu.VMEM)
    anywhere = pl.BlockSpec(memory_space=pltpu.HBM)
    tiles = cells_y // LANES
    half = rows // 2
    own = [a.reshape(-1, cells_y) for a in (density, momenta, desired)]
    lines = [a.shape[0] for a in own]
    shape = lambda *dims: jax.ShapeDtypeStruct(dims, jnp.float32)
    *own, fy, near, far = pl.pallas_call(
        start_kernel,
        out_shape=[shape(tiles, n, LANES) for n in lines]
        + [shape(*factor_y.shape)]
        + [shape(tiles, sum(lines) // 2, LANES)] * 2,
        in_specs=[anywhere] * 4,
        out_specs=[vmem] * 6,
        scratch_shapes=[pltpu.SemaphoreType.DMA((3 * tiles + 1,))],
        compiler_params=params,
        name="start",
    )(*[pltpu.with_memory_space_constraint(a, pltpu.HBM) for a in (*own, factor_y)])
    near = lax.ppermute(near, "gx", [(i, i ^ 1) for i in range(n_gx)])
    far = lax.ppermute(far, "gx", [(i, (i - 1 + i % 2 * 2) % n_gx) for i in range(n_gx)])
    sections = 2 * STEPS
    edges, turned = pl.pallas_call(
        inner_kernel,
        out_shape=[
            shape((sections - 1) * 2 * 3 * members, cells_y),
            shape(3, ry, LANES),
        ],
        scratch_shapes=[pltpu.VMEM((3 * half * members, cells_y), jnp.float32)],
        compiler_params=params,
        name="inner",
    )(*own, near, fy)
    height = 3 * shares + half + 1
    sent = pl.pallas_call(
        functools.partial(outer_kernel, n_gx),
        out_shape=shape(devices * height, LANES),
        scratch_shapes=[pltpu.VMEM((3 * half * members, cells_y), jnp.float32)],
        compiler_params=params,
        name="outer",
    )(*own, far, fy, edges, turned, factor_x, factor_m)
    got = exchange(sent, devices)
    lows = rm // 2
    high = 3 * shares * lows * SUBLANES // LANES
    sent = pl.pallas_call(
        functools.partial(project_kernel, n_gx, rows, shares, rm),
        out_shape=jax.ShapeDtypeStruct((devices * high, LANES), jnp.float32),
        scratch_shapes=[
            pltpu.VMEM((rows * n_gx, 3 * shares * rm), jnp.float32),
            pltpu.VMEM((3, rx, LANES), jnp.float32),
        ],
        compiler_params=params,
        name="project",
    )(got)
    got = exchange(sent, devices)
    core = pl.pallas_call(
        functools.partial(gather_kernel, shares, lows),
        out_shape=jax.ShapeDtypeStruct((lows * 3 * SUBLANES, LANES), jnp.float32),
        compiler_params=params,
        name="gather",
    )(got)
    return core.reshape(lows, 3, SUBLANES, ry)


def solution(mesh):
    return jax.shard_map(
        on_device,
        mesh=mesh,
        in_specs=(
            P("mem", "gx", None),
            P("mem", None, "gx", None),
            P(None, "gx", None),
            P("gx", None),
            P(),
            P("mem", None),
        ),
        out_specs=P("mem", None, "gx", None),
        check_vma=False,
    )
```

```python
import functools

import jax
import jax.numpy as jnp
from jax import lax
from jax.experimental import pallas as pl
from jax.experimental.pallas import tpu as pltpu
from jax.sharding import PartitionSpec as P

STEPS = 2


STIFF = 1.0
RELAX = 1.0
DTIME = 0.2

HIGHEST = lax.Precision.HIGHEST
HIGH = lax.Precision.HIGH
LANES = 128
SUBLANES = 8


def with_halo(cells, sides, width):
    for axis, dim in sides:
        count = lax.axis_size(axis)
        head = lax.slice_in_dim(cells, 0, width, axis=dim)
        tail = lax.slice_in_dim(cells, cells.shape[dim] - width, cells.shape[dim], axis=dim)
        cells = jnp.concatenate(
            [
                lax.ppermute(tail, axis, [(i, (i + 1) % count) for i in range(count)]),
                cells,
                lax.ppermute(head, axis, [((i + 1) % count, i) for i in range(count)]),
            ],
            axis=dim,
        )
    return cells


def tendency(fields, desired):
    density = fields[:, 0]
    moment_x = fields[:, 1]
    moment_y = fields[:, 2]
    speed_x = moment_x / density
    speed_y = moment_y / density
    sound = jnp.sqrt(STIFF * density)
    pressure = 0.5 * STIFF * density * density
    conserved = (density, moment_x, moment_y)
    fluxes_x = (moment_x, moment_x * speed_x + pressure, moment_y * speed_x)
    fluxes_y = (moment_y, moment_x * speed_y, moment_y * speed_y + pressure)
    reach_x = jnp.abs(speed_x) + sound
    bound_x = jnp.maximum(reach_x[:, :-1], reach_x[:, 1:])
    reach_y = (jnp.abs(speed_y) + sound)[:, 1:-1]
    bound_y = jnp.maximum(reach_y, jnp.roll(reach_y, -1, axis=-1))
    changes = []
    for quantity, normal_flux, cross_flux in zip(conserved, fluxes_x, fluxes_y):
        face_x = 0.5 * (normal_flux[:, :-1] + normal_flux[:, 1:]) - 0.5 * bound_x * (
            quantity[:, 1:] - quantity[:, :-1]
        )
        middle = quantity[:, 1:-1]
        cross_mid = cross_flux[:, 1:-1]
        face_y = 0.5 * (cross_mid + jnp.roll(cross_mid, -1, axis=-1)) - 0.5 * bound_y * (
            jnp.roll(middle, -1, axis=-1) - middle
        )
        changes.append(-(face_x[:, 1:] - face_x[:, :-1]) - (face_y - jnp.roll(face_y, 1, axis=-1)))
    centre = density[:, 1:-1]
    changes[1] = changes[1] + (centre * desired[0] - moment_x[:, 1:-1]) / RELAX
    changes[2] = changes[2] + (centre * desired[1] - moment_y[:, 1:-1]) / RELAX
    return jnp.stack(changes, axis=1)


def single_rims(fields):
    return with_halo(fields, (("gx", 2),), 1)


def plain(density, momenta, desired, factor_x, factor_y, factor_m):
    fields = jnp.concatenate([density[:, None], momenta], axis=1)
    for repeat in range(STEPS):
        sectioned = fields + DTIME * tendency(single_rims(fields), desired)
        second = sectioned + DTIME * tendency(single_rims(sectioned), desired)
        fields = 0.5 * fields + 0.5 * second
    along_y = jnp.einsum("mcxy,yb->mcxb", fields, factor_y, precision=HIGHEST)
    spread = lax.all_to_all(along_y, "gx", split_axis=3, concat_axis=2, tiled=True)
    projected = jnp.einsum(
        "mcxb,xa->mcab",
        spread,
        lax.all_gather(factor_x, "gx", axis=0, tiled=True),
        precision=HIGHEST,
    )
    returned = lax.all_to_all(projected, "gx", split_axis=2, concat_axis=3, tiled=True)
    member_terms = jnp.einsum("mcab,mk->kcab", returned, factor_m, precision=HIGHEST)
    return lax.psum_scatter(member_terms, "mem", scatter_dimension=0, tiled=True)


def cell_terms(q):
    rho, mx, my = q
    root = lax.rsqrt(rho)
    inverse = root * root
    sound = rho * root
    u = mx * inverse
    v = my * inverse
    pressure = (0.5 * STIFF) * (rho * rho)
    cross = my * u
    return dict(
        q=q,
        f=(mx, mx * u + pressure, cross),
        g=(my, cross, my * v + pressure),
        ax=jnp.abs(u) + sound,
        ay=jnp.abs(v) + sound,
    )


def x_face(low, high):
    bound = jnp.maximum(low["ax"], high["ax"])
    return tuple(
        fa + fb - bound * (b - a)
        for fa, fb, a, b in zip(low["f"], high["f"], low["q"], high["q"])
    )


def y_difference(row):
    axis = row["ay"].ndim - 1
    size = row["ay"].shape[axis]
    after = lambda a: pltpu.roll(a, size - 1, axis)
    before = lambda a: pltpu.roll(a, 1, axis)
    moved_q = tuple(after(a) for a in row["q"])
    moved_g = (moved_q[2], after(row["g"][1]), after(row["g"][2]))
    bound = jnp.maximum(row["ay"], after(row["ay"]))
    face = tuple(
        ga + gb - bound * (b - a)
        for ga, gb, a, b in zip(row["g"], moved_g, row["q"], moved_q)
    )
    return tuple(a - before(a) for a in face)


def section(row, low_face, high_face, wish):
    cross = y_difference(row)
    rho, mx, my = row["q"]
    half = 0.5 * DTIME
    spread = tuple(h - l + d for h, l, d in zip(high_face, low_face, cross))
    keep = 1.0 - DTIME / RELAX
    wished = (DTIME / RELAX) * rho
    return (
        rho - half * spread[0],
        keep * mx + wished * wish[0] - half * spread[1],
        keep * my + wished * wish[1] - half * spread[2],
    )


def start_kernel(d, m, w, fy, own_d, own_m, own_w, own_fy, far, near, sems):
    tiles = own_d.shape[0]
    odd = lax.rem(lax.axis_index("gx"), 2)
    rows = own_w.shape[1] // 2
    half = rows // 2
    pairs = []
    for whole, cut in ((d, own_d), (m, own_m), (w, own_w)):
        for t in range(tiles):
            pairs.append((whole.at[:, pl.ds(t * LANES, LANES)], cut.at[t]))
    pairs.append((fy, own_fy))
    copies = [
        pltpu.make_async_copy(source, target, sems.at[i])
        for i, (source, target) in enumerate(pairs)
    ]
    for copy in copies:
        copy.start()
    base = 0
    for n, cut in enumerate((own_d, own_m, own_w)):
        lines = cut.shape[1] // rows
        for t in range(tiles):
            copies[n * tiles + t].wait()
            for target, first in ((far.at[t], half * odd), (near[t], half * (1 - odd))):
                for i in range(half):
                    target[pl.ds(base + i, lines, stride=half), :] = cut[
                        t, pl.ds(first + i, lines, stride=rows), :
                    ]
        base += lines * half
    copies[-1].wait()


class Strip:
    def __init__(self, group, own, near, far):
        self.rows = own[2].shape[1] // 2
        self.half = self.rows // 2
        self.members = own[0].shape[1] // self.rows
        self.tiles = own[0].shape[0]
        cut = lambda ref: [ref.at[t] for t in range(self.tiles)]
        self.group, self.own = group, tuple(cut(a) for a in own)
        self.near = near
        self.far = None if far is None else cut(far)
        self.odd = lax.rem(lax.axis_index("gx"), 2)
        self.sign = (1 - 2 * self.odd).astype(jnp.float32)

    def every(self, ref, first, count, stride):
        parts = [ref[t][pl.ds(first, count, stride=stride), :] for t in range(self.tiles)]
        return jnp.concatenate(parts, axis=1)

    def place(self, x):
        if x < self.half:
            ref, at, lines = self.far, x, self.half
        elif x < self.half + self.rows:
            ref, at, lines = self.own, x - self.half, self.rows
        else:
            ref, at, lines = self.near, x - self.half - self.rows, self.half
        return ref, self.odd * (lines - 1) + (1 - 2 * self.odd) * at, lines

    def load(self, x):
        ref, at, lines = self.place(x)
        if ref is self.own:
            d, m = ref[0], ref[1]
            base = 0
        else:
            d = m = ref
            base = self.members * lines
        first = self.group * SUBLANES
        rho = self.every(d, first * lines + at, SUBLANES, lines)
        mx = self.every(m, base + first * 2 * lines + at, SUBLANES, 2 * lines)
        my = self.every(m, base + (first * 2 + 1) * lines + at, SUBLANES, 2 * lines)
        return rho, self.sign * mx, my

    def wish(self, x):
        ref, at, lines = self.place(x)
        if ref is self.own:
            ref, base = ref[2], 0
        else:
            base = 3 * self.members * lines
        line = [self.every(ref, base + c * lines + at, 1, 1) for c in range(2)]
        line[0] = self.sign * line[0]
        return tuple(jnp.broadcast_to(a, (SUBLANES, a.shape[1])) for a in line)


def march(count, computed, fetch, wish, emit):
    sections = len(computed) - 1
    known, terms, faces = {}, {}, {}

    def value(s, x):
        if (s, x) not in known:
            if x in computed[s]:
                new = section(
                    cell(s - 1, x), face(s - 1, x - 1), face(s - 1, x), wish(x)
                )
                if s % 2 == 0:
                    new = tuple(0.5 * a + 0.5 * b for a, b in zip(value(s - 2, x), new))
                emit(s, x, new)
            else:
                new = fetch(s, x)
            known[s, x] = new
        return known[s, x]

    def cell(s, x):
        if (s, x) not in terms:
            terms[s, x] = cell_terms(value(s, x))
        return terms[s, x]

    def face(s, x):
        if (s, x) not in faces:
            faces[s, x] = x_face(cell(s, x), cell(s, x + 1))
        return faces[s, x]

    for t in range(count):
        for s in range(1, sections + 1):
            if t - s in computed[s]:
                value(s, t - s)


def edge_line(s, x, half, members):
    return ((s - 1) * 2 + x - half - s) * 3 * members


def turn_projected(state, fy, members, c, count):
    lines = count * members
    block = state[pl.ds(c * lines, lines), :]
    along = jnp.dot(block, fy[...], precision=HIGH, preferred_element_type=jnp.float32)
    return along.T


def inner_kernel(own_d, own_m, own_w, fy, *rest):
    *near, edges, turned, state = rest
    rows = own_w.shape[1] // 2
    half = rows // 2
    members = own_d.shape[1] // rows
    sections = 2 * STEPS
    count = 2 * rows
    for group in range(members // SUBLANES):
        strip = Strip(group, (own_d, own_m, own_w), near, None)

        def emit(s, x, q):
            if s == sections:
                for c in range(3):
                    at = (c * half + x - rows) * members + group * SUBLANES
                    state[pl.ds(at, SUBLANES), :] = q[c]
            elif x - half - s in (0, 1):
                for c in range(3):
                    at = edge_line(s, x, half, members) + c * members + group * SUBLANES
                    edges[pl.ds(at, SUBLANES), :] = q[c]

        computed = [range(0)] + [range(half + s, count - s) for s in range(1, sections + 1)]
        march(count, computed, lambda s, x: strip.load(x), strip.wish, emit)
    for c in range(3):
        part = turn_projected(state, fy, members, c, half)
        turned[c] = jnp.concatenate([jnp.zeros_like(part), part], axis=1)


def outer_kernel(
    n_gx, own_d, own_m, own_w, far, fy, edges, turned, fx, fm, out, state
):
    rows = own_w.shape[1] // 2
    half = rows // 2
    members = own_d.shape[1] // rows
    sections = 2 * STEPS
    for group in range(members // SUBLANES):
        strip = Strip(group, (own_d, own_m, own_w), None, far)

        def fetch(s, x):
            if s == 0:
                return strip.load(x)
            at = edge_line(s, x, half, members) + group * SUBLANES
            return tuple(edges[pl.ds(at + c * members, SUBLANES), :] for c in range(3))

        def emit(s, x, q):
            if s == sections:
                for c in range(3):
                    at = (c * half + x - half) * members + group * SUBLANES
                    state[pl.ds(at, SUBLANES), :] = q[c]

        computed = [range(0)] + [range(s, half + s) for s in range(1, sections + 1)]
        march(rows + sections, computed, fetch, strip.wish, emit)
    devices = 2 * n_gx
    shares = fy.shape[1] // devices
    height = out.shape[0] // devices
    odd = lax.rem(lax.axis_index("gx"), 2)
    sign = (1 - 2 * odd).astype(jnp.float32)
    for c in range(3):
        part = turn_projected(state, fy, members, c, half)
        whole = jnp.concatenate([part, turned[c][:, half * members :]], axis=1)
        if c == 1:
            whole = sign * whole
        for r in range(shares):
            out[pl.ds(c * shares + r, devices, stride=height), :] = whole[
                r * devices : (r + 1) * devices
            ]
    mem, gx = lax.axis_index("mem"), lax.axis_index("gx")
    for r in range(half):
        line = fx[pl.ds(mem * half + r, 1), :]
        out[pl.ds(3 * shares + r, devices, stride=height), :] = jnp.broadcast_to(
            line, (devices, line.shape[1])
        )
    line = fm[pl.ds(gx, 1), :]
    line = jnp.concatenate([line] * (LANES // line.shape[1]), axis=1)
    out[pl.ds(3 * shares + half, devices, stride=height), :] = jnp.broadcast_to(
        line, (devices, LANES)
    )


def project_kernel(n_gx, rows, shares, rm, inp, out, blocks, tall):
    devices = 2 * n_gx
    members = n_gx
    height = inp.shape[0] // devices
    half = rows // 2
    pieces = 3 * shares
    columns = [inp[pl.ds(j, devices, stride=height), :] for j in range(pieces)]
    lhs = jnp.concatenate(
        [
            jnp.concatenate([d[:n_gx] for d in columns], axis=0),
            jnp.concatenate([d[n_gx:] for d in columns], axis=0),
        ],
        axis=1,
    )
    fm = inp[pl.ds(pieces + half, devices, stride=height), :]
    group = lax.broadcasted_iota(jnp.int32, (members, LANES), 1) // rm
    per = LANES // rm
    zero = jnp.zeros((members, LANES), jnp.float32)
    lines = []
    for mem in range(2):
        part = fm[mem * members : (mem + 1) * members]
        for x in range(rows):
            kept = jnp.where(group == x % per, part, 0.0)
            lines.append(
                jnp.concatenate(
                    [kept if x // per == t else zero for t in range(rows // per)], axis=1
                )
            )
    diagonal = jnp.concatenate(lines, axis=0)
    mixed = jnp.dot(lhs, diagonal, precision=HIGH, preferred_element_type=jnp.float32)
    lows = rm // 2
    orders = (range(pieces), [j % pieces for j in range(pieces - shares, 2 * pieces - shares)])
    for x in range(rows):
        for k in range(2):
            blocks[pl.ds(x * n_gx, n_gx), pl.ds(k * pieces * lows, pieces * lows)] = jnp.concatenate(
                [
                    mixed[j * n_gx : (j + 1) * n_gx, x * rm + k * lows : x * rm + (k + 1) * lows]
                    for j in orders[k]
                ],
                axis=1,
            )
    halves = [inp[pl.ds(pieces + r, devices, stride=height), :] for r in range(half)]
    lines = [a[:n_gx] for a in halves] + [a[n_gx:] for a in halves]
    odd = lax.broadcasted_iota(jnp.int32, (n_gx, LANES), 0) % 2 == 1
    lines = [jnp.where(odd, lines[rows - 1 - r], lines[r]) for r in range(rows)]
    fx = jnp.concatenate(lines, axis=0)
    core = jnp.dot(fx.T, blocks[...], precision=HIGH, preferred_element_type=jnp.float32)
    high = out.shape[0] // devices
    for t in range(3):
        tall[t] = core[:, t * LANES : (t + 1) * LANES]
    lane = lax.broadcasted_iota(jnp.int32, (n_gx, LANES), 1)
    for a in range(SUBLANES):
        for k in range(2):
            out[pl.ds(k * n_gx * high + a, n_gx, stride=high), :] = tall[
                2 * k, pl.ds(a, n_gx, stride=SUBLANES), :
            ]
    for i in range(SUBLANES // 2):
        upper = tall[1, pl.ds(i, n_gx, stride=SUBLANES), :]
        lower = tall[1, pl.ds(i + SUBLANES // 2, n_gx, stride=SUBLANES), :]
        first = jnp.where(lane < LANES // 2, upper, pltpu.roll(lower, LANES // 2, 1))
        second = jnp.where(lane < LANES // 2, pltpu.roll(upper, LANES // 2, 1), lower)
        out[pl.ds(SUBLANES + i, n_gx, stride=high), :] = first
        out[pl.ds(n_gx * high + SUBLANES + i, n_gx, stride=high), :] = second


def gather_kernel(shares, lows, inp, out):
    devices = LANES // shares
    high = inp.shape[0] // devices
    quarter = SUBLANES // 2
    step = out.shape[0] // lows

    def turn(first):
        return jnp.concatenate(
            [inp[pl.ds(first + i, devices, stride=high), :] for i in range(quarter)], axis=0
        ).T

    def place(turned, base, c, a0):
        for i in range(quarter):
            line = jnp.concatenate(
                [
                    turned[base + r * lows : base + (r + 1) * lows, i * devices : (i + 1) * devices]
                    for r in range(shares)
                ],
                axis=1,
            )
            out[pl.ds(c * SUBLANES + a0 + i, lows, stride=step), :] = line

    for h in range(2):
        turned = turn(h * quarter)
        for c in range(2):
            place(turned, c * shares * lows, c, h * quarter)
    turned = turn(SUBLANES)
    for h in range(2):
        place(turned, h * shares * lows, 2, h * quarter)


def exchange(chunks, devices):
    block = chunks.reshape(devices, chunks.shape[0] // devices, 1, chunks.shape[1])
    moved = lax.all_to_all(block, ("mem", "gx"), split_axis=0, concat_axis=0, tiled=True)
    return moved.reshape(chunks.shape)


def laid_out(density, factor_x, factor_y, factor_m):
    members, rows, cells_y = density.shape
    n_mem, n_gx = lax.axis_size("mem"), lax.axis_size("gx")
    rx, ry, rm = factor_x.shape[1], factor_y.shape[1], factor_m.shape[1]
    shares = ry // (n_mem * n_gx)
    return (
        n_mem == 2
        and rows == 4 * STEPS == SUBLANES
        and members == n_gx
        and n_gx % 2 == 0
        and members * rows == LANES
        and members % SUBLANES == 0
        and cells_y % LANES == 0
        and rx == LANES == n_gx * SUBLANES
        and ry == LANES == shares * n_mem * n_gx
        and shares * rm == LANES
        and shares * rm // 2 * 2 == LANES
        and rows * rm == 2 * LANES
    )


def on_device(density, momenta, desired, factor_x, factor_y, factor_m):
    if not laid_out(density, factor_x, factor_y, factor_m):
        return plain(density, momenta, desired, factor_x, factor_y, factor_m)
    members, rows, cells_y = density.shape
    n_gx = lax.axis_size("gx")
    devices = 2 * n_gx
    rx, ry, rm = factor_x.shape[1], factor_y.shape[1], factor_m.shape[1]
    shares = ry // devices
    params = pltpu.CompilerParams(vmem_limit_bytes=32 * 1024 * 1024)
    vmem = pl.BlockSpec(memory_space=pltpu.VMEM)
    anywhere = pl.BlockSpec(memory_space=pl.ANY)
    tiles = cells_y // LANES
    half = rows // 2
    own = [a.reshape(-1, cells_y) for a in (density, momenta, desired)]
    lines = [a.shape[0] for a in own]
    shape = lambda *dims: jax.ShapeDtypeStruct(dims, jnp.float32)
    packed = (sum(lines) // 2, LANES)
    *own, fy, far, near = pl.pallas_call(
        start_kernel,
        out_shape=[shape(tiles, n, LANES) for n in lines]
        + [shape(*factor_y.shape), shape(tiles, *packed), [shape(*packed)] * tiles],
        in_specs=[anywhere] * 4,
        out_specs=[vmem] * 5 + [[vmem] * tiles],
        scratch_shapes=[pltpu.SemaphoreType.DMA((3 * tiles + 1,))],
        compiler_params=params,
        name="start",
    )(*[pltpu.with_memory_space_constraint(a, pltpu.HBM) for a in (*own, factor_y)])
    far = lax.ppermute(far, "gx", [(i, (i - 1 + i % 2 * 2) % n_gx) for i in range(n_gx)])
    near = [lax.ppermute(a, "gx", [(i, i ^ 1) for i in range(n_gx)]) for a in near]
    sections = 2 * STEPS
    edges, turned = pl.pallas_call(
        inner_kernel,
        out_shape=[
            shape((sections - 1) * 2 * 3 * members, cells_y),
            shape(3, ry, LANES),
        ],
        scratch_shapes=[pltpu.VMEM((3 * half * members, cells_y), jnp.float32)],
        compiler_params=params,
        name="inner",
    )(*own, fy, *near)
    height = 3 * shares + half + 1
    sent = pl.pallas_call(
        functools.partial(outer_kernel, n_gx),
        out_shape=shape(devices * height, LANES),
        scratch_shapes=[pltpu.VMEM((3 * half * members, cells_y), jnp.float32)],
        compiler_params=params,
        name="outer",
    )(*own, far, fy, edges, turned, factor_x, factor_m)
    got = exchange(sent, devices)
    lows = rm // 2
    high = 3 * shares * lows * SUBLANES // LANES
    sent = pl.pallas_call(
        functools.partial(project_kernel, n_gx, rows, shares, rm),
        out_shape=jax.ShapeDtypeStruct((devices * high, LANES), jnp.float32),
        scratch_shapes=[
            pltpu.VMEM((rows * n_gx, 3 * shares * rm), jnp.float32),
            pltpu.VMEM((3, rx, LANES), jnp.float32),
        ],
        compiler_params=params,
        name="project",
    )(got)
    got = exchange(sent, devices)
    core = pl.pallas_call(
        functools.partial(gather_kernel, shares, lows),
        out_shape=jax.ShapeDtypeStruct((lows * 3 * SUBLANES, LANES), jnp.float32),
        compiler_params=params,
        name="gather",
    )(got)
    return core.reshape(lows, 3, SUBLANES, ry)


def solution(mesh):
    return jax.shard_map(
        on_device,
        mesh=mesh,
        in_specs=(
            P("mem", "gx", None),
            P("mem", None, "gx", None),
            P(None, "gx", None),
            P("gx", None),
            P(),
            P("mem", None),
        ),
        out_specs=P("mem", None, "gx", None),
        check_vma=False,
    )
```

```python
import functools

import jax
import jax.numpy as jnp
from jax import lax
from jax.experimental import pallas as pl
from jax.experimental.pallas import tpu as pltpu
from jax.sharding import PartitionSpec as P

STEPS = 2


STIFF = 1.0
RELAX = 1.0
DTIME = 0.2

HIGHEST = lax.Precision.HIGHEST
HIGH = lax.Precision.HIGH
LANES = 128
SUBLANES = 8


def with_halo(cells, sides, width):
    for axis, dim in sides:
        count = lax.axis_size(axis)
        head = lax.slice_in_dim(cells, 0, width, axis=dim)
        tail = lax.slice_in_dim(cells, cells.shape[dim] - width, cells.shape[dim], axis=dim)
        cells = jnp.concatenate(
            [
                lax.ppermute(tail, axis, [(i, (i + 1) % count) for i in range(count)]),
                cells,
                lax.ppermute(head, axis, [((i + 1) % count, i) for i in range(count)]),
            ],
            axis=dim,
        )
    return cells


def tendency(fields, desired):
    density = fields[:, 0]
    moment_x = fields[:, 1]
    moment_y = fields[:, 2]
    speed_x = moment_x / density
    speed_y = moment_y / density
    sound = jnp.sqrt(STIFF * density)
    pressure = 0.5 * STIFF * density * density
    conserved = (density, moment_x, moment_y)
    fluxes_x = (moment_x, moment_x * speed_x + pressure, moment_y * speed_x)
    fluxes_y = (moment_y, moment_x * speed_y, moment_y * speed_y + pressure)
    reach_x = jnp.abs(speed_x) + sound
    bound_x = jnp.maximum(reach_x[:, :-1], reach_x[:, 1:])
    reach_y = (jnp.abs(speed_y) + sound)[:, 1:-1]
    bound_y = jnp.maximum(reach_y, jnp.roll(reach_y, -1, axis=-1))
    changes = []
    for quantity, normal_flux, cross_flux in zip(conserved, fluxes_x, fluxes_y):
        face_x = 0.5 * (normal_flux[:, :-1] + normal_flux[:, 1:]) - 0.5 * bound_x * (
            quantity[:, 1:] - quantity[:, :-1]
        )
        middle = quantity[:, 1:-1]
        cross_mid = cross_flux[:, 1:-1]
        face_y = 0.5 * (cross_mid + jnp.roll(cross_mid, -1, axis=-1)) - 0.5 * bound_y * (
            jnp.roll(middle, -1, axis=-1) - middle
        )
        changes.append(-(face_x[:, 1:] - face_x[:, :-1]) - (face_y - jnp.roll(face_y, 1, axis=-1)))
    centre = density[:, 1:-1]
    changes[1] = changes[1] + (centre * desired[0] - moment_x[:, 1:-1]) / RELAX
    changes[2] = changes[2] + (centre * desired[1] - moment_y[:, 1:-1]) / RELAX
    return jnp.stack(changes, axis=1)


def single_rims(fields):
    return with_halo(fields, (("gx", 2),), 1)


def plain(density, momenta, desired, factor_x, factor_y, factor_m):
    fields = jnp.concatenate([density[:, None], momenta], axis=1)
    for repeat in range(STEPS):
        sectioned = fields + DTIME * tendency(single_rims(fields), desired)
        second = sectioned + DTIME * tendency(single_rims(sectioned), desired)
        fields = 0.5 * fields + 0.5 * second
    along_y = jnp.einsum("mcxy,yb->mcxb", fields, factor_y, precision=HIGHEST)
    spread = lax.all_to_all(along_y, "gx", split_axis=3, concat_axis=2, tiled=True)
    projected = jnp.einsum(
        "mcxb,xa->mcab",
        spread,
        lax.all_gather(factor_x, "gx", axis=0, tiled=True),
        precision=HIGHEST,
    )
    returned = lax.all_to_all(projected, "gx", split_axis=2, concat_axis=3, tiled=True)
    member_terms = jnp.einsum("mcab,mk->kcab", returned, factor_m, precision=HIGHEST)
    return lax.psum_scatter(member_terms, "mem", scatter_dimension=0, tiled=True)


def cell_terms(q):
    rho, mx, my = q
    root = lax.rsqrt(rho)
    inverse = root * root
    sound = rho * root
    u = mx * inverse
    v = my * inverse
    pressure = (0.5 * STIFF) * (rho * rho)
    cross = my * u
    return dict(
        q=q,
        f=(mx, mx * u + pressure, cross),
        g=(my, cross, my * v + pressure),
        ax=jnp.abs(u) + sound,
        ay=jnp.abs(v) + sound,
    )


def x_face(low, high):
    bound = jnp.maximum(low["ax"], high["ax"])
    return tuple(
        fa + fb - bound * (b - a)
        for fa, fb, a, b in zip(low["f"], high["f"], low["q"], high["q"])
    )


def y_difference(row):
    axis = row["ay"].ndim - 1
    size = row["ay"].shape[axis]
    after = lambda a: pltpu.roll(a, size - 1, axis)
    before = lambda a: pltpu.roll(a, 1, axis)
    moved_q = tuple(after(a) for a in row["q"])
    moved_g = (moved_q[2], after(row["g"][1]), after(row["g"][2]))
    bound = jnp.maximum(row["ay"], after(row["ay"]))
    face = tuple(
        ga + gb - bound * (b - a)
        for ga, gb, a, b in zip(row["g"], moved_g, row["q"], moved_q)
    )
    return tuple(a - before(a) for a in face)


def section(row, low_face, high_face, wish):
    cross = y_difference(row)
    rho, mx, my = row["q"]
    half = 0.5 * DTIME
    spread = tuple(h + d for h, d in zip(high_face, cross))
    if low_face is not None:
        spread = tuple(a - l for a, l in zip(spread, low_face))
    keep = 1.0 - DTIME / RELAX
    wished = (DTIME / RELAX) * rho
    return (
        rho - half * spread[0],
        keep * mx + wished * wish[0] - half * spread[1],
        keep * my + wished * wish[1] - half * spread[2],
    )


def start_kernel(d, m, w, fy, own_d, own_m, own_w, own_fy, far, near, sems):
    tiles = own_d.shape[0]
    odd = lax.rem(lax.axis_index("gx"), 2)
    rows = own_w.shape[1] // 2
    half = rows // 2
    pairs = []
    for whole, cut in ((d, own_d), (m, own_m), (w, own_w)):
        for t in range(tiles):
            pairs.append((whole.at[:, pl.ds(t * LANES, LANES)], cut.at[t]))
    pairs.append((fy, own_fy))
    copies = [
        pltpu.make_async_copy(source, target, sems.at[i])
        for i, (source, target) in enumerate(pairs)
    ]
    for copy in copies:
        copy.start()
    base = 0
    for n, cut in enumerate((own_d, own_m, own_w)):
        lines = cut.shape[1] // rows
        for t in range(tiles):
            copies[n * tiles + t].wait()
            for target, first in ((far.at[t], half * odd), (near[t], half * (1 - odd))):
                for i in range(half):
                    target[pl.ds(base + i, lines, stride=half), :] = cut[
                        t, pl.ds(first + i, lines, stride=rows), :
                    ]
        base += lines * half
    copies[-1].wait()


class Strip:
    def __init__(self, group, own, near, far):
        self.rows = own[2].shape[1] // 2
        self.half = self.rows // 2
        self.members = own[0].shape[1] // self.rows
        self.tiles = own[0].shape[0]
        cut = lambda ref: [ref.at[t] for t in range(self.tiles)]
        self.group, self.own = group, tuple(cut(a) for a in own)
        self.near = near
        self.far = None if far is None else cut(far)
        self.odd = lax.rem(lax.axis_index("gx"), 2)
        self.sign = (1 - 2 * self.odd).astype(jnp.float32)

    def every(self, ref, first, count, stride):
        parts = [ref[t][pl.ds(first, count, stride=stride), :] for t in range(self.tiles)]
        return jnp.concatenate(parts, axis=1)

    def place(self, x):
        if x < self.half:
            ref, at, lines = self.far, x, self.half
        elif x < self.half + self.rows:
            ref, at, lines = self.own, x - self.half, self.rows
        else:
            ref, at, lines = self.near, x - self.half - self.rows, self.half
        return ref, self.odd * (lines - 1) + (1 - 2 * self.odd) * at, lines

    def load(self, x):
        ref, at, lines = self.place(x)
        if ref is self.own:
            d, m = ref[0], ref[1]
            base = 0
        else:
            d = m = ref
            base = self.members * lines
        first = self.group * SUBLANES
        rho = self.every(d, first * lines + at, SUBLANES, lines)
        mx = self.every(m, base + first * 2 * lines + at, SUBLANES, 2 * lines)
        my = self.every(m, base + (first * 2 + 1) * lines + at, SUBLANES, 2 * lines)
        return rho, self.sign * mx, my

    def wish(self, x):
        ref, at, lines = self.place(x)
        if ref is self.own:
            ref, base = ref[2], 0
        else:
            base = 3 * self.members * lines
        line = [self.every(ref, base + c * lines + at, 1, 1) for c in range(2)]
        line[0] = self.sign * line[0]
        return tuple(jnp.broadcast_to(a, (SUBLANES, a.shape[1])) for a in line)

    def keep(self, state, x, q):
        for c, a in enumerate((q[0], self.sign * q[1], q[2])):
            at = (3 * x + c) * self.members + self.group * SUBLANES
            state[pl.ds(at, SUBLANES), :] = a


def march(computed, fetch, wish, emit, hook=None, bound=None):
    sections = len(computed) - 1
    known, terms, faces = {}, {}, {}

    def value(s, x):
        if (s, x) not in known:
            if x not in computed[s]:
                new = fetch(s, x)
            elif bound is not None and x == computed[s][-1]:
                share = 0.5 * DTIME * (0.5 if s % 2 == 0 else 1.0)
                new = tuple(
                    a + share * b for a, b in zip(bound(s - 1, x)["next"], face(s - 1, x - 1))
                )
            else:
                new = advanced(s, x, face(s - 1, x - 1))
            if x in computed[s]:
                emit(s, x, new)
            known[s, x] = new
        return known[s, x]

    def advanced(s, x, low):
        new = section(cell(s - 1, x), low, face(s - 1, x), wish(x))
        if s % 2 == 0:
            new = tuple(0.5 * a + 0.5 * b for a, b in zip(value(s - 2, x), new))
        return new

    def cell(s, x):
        if (s, x) not in terms:
            if bound is not None and x == computed[s + 1][-1]:
                terms[s, x] = bound(s, x)
            else:
                terms[s, x] = cell_terms(value(s, x))
        return terms[s, x]

    def face(s, x):
        if (s, x) not in faces:
            faces[s, x] = x_face(cell(s, x), cell(s, x + 1))
        return faces[s, x]

    for t in range(computed[1][0], computed[-1][-1] + sections + 1):
        for s in range(1, sections + 1):
            if t - s in computed[s]:
                value(s, t - s)
        if hook is not None:
            for s in range(sections):
                hook(s, t - s - 1, cell, advanced)


def edge_line(s, members):
    return s * 9 * members


def deal_columns(state, fy, devices, members, lines):
    along = jnp.dot(state[...], fy[...], precision=HIGH, preferred_element_type=jnp.float32)
    turned = along.T
    shares = fy.shape[1] // devices
    firsts, thirds = [], []
    for x in range(lines):
        at = 3 * x * members
        cut = lambda low, high: jnp.concatenate(
            [
                turned[r * devices : (r + 1) * devices, at + low : at + high]
                for r in range(shares)
            ],
            axis=1,
        )
        firsts.append(cut(0, 2 * members))
        thirds.append(cut(2 * members, 3 * members))
    return firsts, thirds


def member_kernel(near, fm, out):
    out[...] = jnp.concatenate([fm[...]] * (LANES // fm.shape[1]), axis=1)


def inner_kernel(own_d, own_m, own_w, fy, *rest):
    *near, edges, early, state = rest
    rows = own_w.shape[1] // 2
    half = rows // 2
    members = own_d.shape[1] // rows
    sections = 2 * STEPS
    count = 2 * rows
    for group in range(members // SUBLANES):
        strip = Strip(group, (own_d, own_m, own_w), near, None)

        def emit(s, x, q):
            if s == sections:
                strip.keep(state, x - rows, q)

        def hook(s, x, cell, advanced):
            if x == half + s:
                row = cell(s, x)
                arrays = (*row["q"], *row["f"][1:], row["ax"], *advanced(s + 1, x, None))
                for c, a in enumerate(arrays):
                    at = edge_line(s, members) + c * members + group * SUBLANES
                    edges[pl.ds(at, SUBLANES), :] = a

        computed = [range(0)] + [range(half + s, count - s) for s in range(1, sections + 1)]
        march(computed, lambda s, x: strip.load(x), strip.wish, emit, hook)
    devices = early.shape[0] // (2 * half)
    firsts, thirds = deal_columns(state, fy, devices, members, half)
    for i in range(half):
        early[pl.ds(i * devices, devices), :] = firsts[i]
        early[pl.ds((half + i) * devices, devices), :] = jnp.concatenate([thirds[i]] * 2, axis=1)


def outer_kernel(
    n_gx, own_d, own_m, own_w, far, fy, edges, early, fx, other_fm, out, state
):
    rows = own_w.shape[1] // 2
    half = rows // 2
    members = own_d.shape[1] // rows
    sections = 2 * STEPS
    for group in range(members // SUBLANES):
        strip = Strip(group, (own_d, own_m, own_w), None, far)

        @functools.cache
        def bound(s, x):
            at = edge_line(s, members) + group * SUBLANES
            a = [edges[pl.ds(at + c * members, SUBLANES), :] for c in range(9)]
            return dict(q=tuple(a[:3]), f=(a[1], a[3], a[4]), ax=a[5], next=tuple(a[6:]))

        def fetch(s, x):
            return strip.load(x) if s == 0 else bound(s, x)["q"]

        def emit(s, x, q):
            if s == sections:
                strip.keep(state, x - half, q)

        computed = [range(0)] + [range(s, half + s) for s in range(1, sections + 1)]
        march(computed, fetch, strip.wish, emit, bound=bound)
    devices = 2 * n_gx
    height = out.shape[0] // devices
    firsts, thirds = deal_columns(state, fy, devices, members, half)
    middle = LANES // 2
    for i in range(half):
        out[pl.ds(i, devices, stride=height), :] = firsts[i]
        out[pl.ds(half + i, devices, stride=height), :] = early[pl.ds(i * devices, devices), :]
        other = early[pl.ds((half + i) * devices, devices), :]
        out[pl.ds(rows + i, devices, stride=height), :] = jnp.concatenate(
            [thirds[i], other[:, middle:]], axis=1
        )
    mem = lax.axis_index("mem")
    for r in range(half):
        line = fx[pl.ds(mem * half + r, 1), :]
        out[pl.ds(rows + half + r, devices, stride=height), :] = jnp.broadcast_to(
            line, (devices, line.shape[1])
        )


def project_kernel(n_gx, rows, rm, inp, own_fm, other_fm, out, tall):
    devices = 2 * n_gx
    members = n_gx
    height = inp.shape[0] // devices
    half = rows // 2
    middle = LANES // 2
    low_rank = rm // 2
    line = lambda j: inp[pl.ds(j, devices, stride=height), :]
    swap = lambda a: pltpu.roll(a, middle, 1)
    lane = lax.broadcasted_iota(jnp.int32, (members, LANES), 1)
    firsts = [line(x) for x in range(rows)]
    firsts = jnp.concatenate(
        [
            jnp.concatenate([a[mem * n_gx : (mem + 1) * n_gx] for a in firsts], axis=0)
            for mem in range(2)
        ],
        axis=1,
    )
    thirds = [line(rows + i) for i in range(half)]
    pairs = [(a[:n_gx], a[n_gx:]) for a in thirds]
    thirds = jnp.concatenate(
        [jnp.where(lane < middle, a, swap(b)) for a, b in pairs]
        + [jnp.where(lane < middle, swap(a), b) for a, b in pairs],
        axis=0,
    )
    first = lax.axis_index("mem") == 0
    a, b = own_fm[...], other_fm[...]
    fm = jnp.concatenate([jnp.where(first, a, b), jnp.where(first, b, a)], axis=0)
    wide = lax.broadcasted_iota(jnp.int32, fm.shape, 1)
    first_half = wide % rm < low_rank
    repeated = (
        jnp.where(first_half, fm, pltpu.roll(fm, low_rank, 1)),
        jnp.where(first_half, pltpu.roll(fm, LANES - low_rank, 1), fm),
    )
    block = lane // low_rank
    part = lambda k, mem: repeated[k][mem * members : (mem + 1) * members]
    count = LANES // members
    diagonal = jnp.concatenate(
        [
            jnp.concatenate(
                [jnp.where(block == p, part(k, mem), 0.0) for mem in range(2) for p in range(count)],
                axis=0,
            )
            for k in range(2)
        ],
        axis=1,
    )
    small = jnp.concatenate(
        [
            jnp.where(
                block == p,
                part(0, mem),
                jnp.where(block == count // 2 + p, part(1, mem), 0.0),
            )
            for mem in range(2)
            for p in range(count // 2)
        ],
        axis=0,
    )
    product = functools.partial(jnp.dot, precision=HIGH, preferred_element_type=jnp.float32)
    firsts = product(firsts, diagonal)
    thirds = product(thirds, small)
    blocks = jnp.concatenate([firsts[:, :LANES], thirds, firsts[:, LANES:]], axis=1)
    halves = [line(rows + half + r) for r in range(half)]
    lines = [a[:n_gx] for a in halves] + [a[n_gx:] for a in halves]
    odd = lax.broadcasted_iota(jnp.int32, (n_gx, LANES), 0) % 2 == 1
    lines = [jnp.where(odd, lines[rows - 1 - r], lines[r]) for r in range(rows)]
    fx = jnp.concatenate(lines, axis=0)
    core = product(fx.T, blocks)
    high = out.shape[0] // devices
    for t in range(3):
        tall[t] = core[:, t * LANES : (t + 1) * LANES]
    lane = lax.broadcasted_iota(jnp.int32, (n_gx, LANES), 1)
    for a in range(SUBLANES):
        for k in range(2):
            out[pl.ds(k * n_gx * high + a, n_gx, stride=high), :] = tall[
                2 * k, pl.ds(a, n_gx, stride=SUBLANES), :
            ]
    for i in range(SUBLANES // 2):
        upper = tall[1, pl.ds(i, n_gx, stride=SUBLANES), :]
        lower = tall[1, pl.ds(i + SUBLANES // 2, n_gx, stride=SUBLANES), :]
        first = jnp.where(lane < LANES // 2, upper, pltpu.roll(lower, LANES // 2, 1))
        second = jnp.where(lane < LANES // 2, pltpu.roll(upper, LANES // 2, 1), lower)
        out[pl.ds(SUBLANES + i, n_gx, stride=high), :] = first
        out[pl.ds(n_gx * high + SUBLANES + i, n_gx, stride=high), :] = second


def gather_kernel(shares, lows, inp, out):
    devices = LANES // shares
    high = inp.shape[0] // devices
    quarter = SUBLANES // 2
    step = out.shape[0] // lows

    def turn(first):
        return jnp.concatenate(
            [inp[pl.ds(first + i, devices, stride=high), :] for i in range(quarter)], axis=0
        ).T

    def place(turned, base, apart, c, a0):
        for i in range(quarter):
            line = jnp.concatenate(
                [
                    turned[base + r * apart : base + r * apart + lows, i * devices : (i + 1) * devices]
                    for r in range(shares)
                ],
                axis=1,
            )
            out[pl.ds(c * SUBLANES + a0 + i, lows, stride=step), :] = line

    for h in range(2):
        turned = turn(h * quarter)
        for c in range(2):
            place(turned, c * lows, 2 * lows, c, h * quarter)
    turned = turn(SUBLANES)
    for h in range(2):
        place(turned, h * shares * lows, lows, 2, h * quarter)


def exchange(chunks, devices):
    block = chunks.reshape(devices, chunks.shape[0] // devices, 1, chunks.shape[1])
    moved = lax.all_to_all(block, ("mem", "gx"), split_axis=0, concat_axis=0, tiled=True)
    return moved.reshape(chunks.shape)


def laid_out(density, factor_x, factor_y, factor_m):
    members, rows, cells_y = density.shape
    n_mem, n_gx = lax.axis_size("mem"), lax.axis_size("gx")
    rx, ry, rm = factor_x.shape[1], factor_y.shape[1], factor_m.shape[1]
    shares = ry // (n_mem * n_gx)
    return (
        n_mem == 2
        and rows == 4 * STEPS == SUBLANES
        and members == n_gx
        and n_gx % 2 == 0
        and members * rows == LANES
        and members % SUBLANES == 0
        and cells_y % LANES == 0
        and rx == LANES == n_gx * SUBLANES
        and ry == LANES == shares * n_mem * n_gx
        and shares * rm == LANES
        and shares * rm // 2 * 2 == LANES
        and 2 * shares * members == LANES
        and 2 * members == rm
    )


def on_device(density, momenta, desired, factor_x, factor_y, factor_m):
    if not laid_out(density, factor_x, factor_y, factor_m):
        return plain(density, momenta, desired, factor_x, factor_y, factor_m)
    members, rows, cells_y = density.shape
    n_gx = lax.axis_size("gx")
    devices = 2 * n_gx
    rx, ry, rm = factor_x.shape[1], factor_y.shape[1], factor_m.shape[1]
    shares = ry // devices
    params = pltpu.CompilerParams(vmem_limit_bytes=32 * 1024 * 1024)
    vmem = pl.BlockSpec(memory_space=pltpu.VMEM)
    anywhere = pl.BlockSpec(memory_space=pl.ANY)
    tiles = cells_y // LANES
    half = rows // 2
    own = [a.reshape(-1, cells_y) for a in (density, momenta, desired)]
    lines = [a.shape[0] for a in own]
    shape = lambda *dims: jax.ShapeDtypeStruct(dims, jnp.float32)
    packed = (sum(lines) // 2, LANES)
    *own, fy, far, near = pl.pallas_call(
        start_kernel,
        out_shape=[shape(tiles, n, LANES) for n in lines]
        + [shape(*factor_y.shape), shape(tiles, *packed), [shape(*packed)] * tiles],
        in_specs=[anywhere] * 4,
        out_specs=[vmem] * 5 + [[vmem] * tiles],
        scratch_shapes=[pltpu.SemaphoreType.DMA((3 * tiles + 1,))],
        compiler_params=params,
        name="start",
    )(*[pltpu.with_memory_space_constraint(a, pltpu.HBM) for a in (*own, factor_y)])
    far = lax.ppermute(far, "gx", [(i, (i - 1 + i % 2 * 2) % n_gx) for i in range(n_gx)])
    near = [lax.ppermute(a, "gx", [(i, i ^ 1) for i in range(n_gx)]) for a in near]
    own_fm = pl.pallas_call(
        member_kernel,
        out_shape=shape(members, LANES),
        in_specs=[anywhere, vmem],
        out_specs=vmem,
        compiler_params=params,
        name="member",
    )(near[-1], factor_m)
    other_fm = lax.ppermute(own_fm, "mem", [(0, 1), (1, 0)])
    sections = 2 * STEPS
    edges, early = pl.pallas_call(
        inner_kernel,
        out_shape=[
            shape(sections * 9 * members, cells_y),
            shape(2 * half * devices, LANES),
        ],
        scratch_shapes=[pltpu.VMEM((3 * half * members, cells_y), jnp.float32)],
        compiler_params=params,
        name="inner",
    )(*own, fy, *near)
    height = rows + 2 * half
    sent = pl.pallas_call(
        functools.partial(outer_kernel, n_gx),
        out_shape=shape(devices * height, LANES),
        in_specs=[vmem] * 8 + [anywhere],
        out_specs=vmem,
        scratch_shapes=[pltpu.VMEM((3 * half * members, cells_y), jnp.float32)],
        compiler_params=params,
        name="outer",
    )(*own, far, fy, edges, early, factor_x, other_fm)
    got = exchange(sent, devices)
    lows = rm // 2
    high = 3 * shares * lows * SUBLANES // LANES
    sent = pl.pallas_call(
        functools.partial(project_kernel, n_gx, rows, rm),
        out_shape=jax.ShapeDtypeStruct((devices * high, LANES), jnp.float32),
        scratch_shapes=[pltpu.VMEM((3, rx, LANES), jnp.float32)],
        compiler_params=params,
        name="project",
    )(got, own_fm, other_fm)
    got = exchange(sent, devices)
    core = pl.pallas_call(
        functools.partial(gather_kernel, shares, lows),
        out_shape=jax.ShapeDtypeStruct((lows * 3 * SUBLANES, LANES), jnp.float32),
        compiler_params=params,
        name="gather",
    )(got)
    return core.reshape(lows, 3, SUBLANES, ry)


def solution(mesh):
    return jax.shard_map(
        on_device,
        mesh=mesh,
        in_specs=(
            P("mem", "gx", None),
            P("mem", None, "gx", None),
            P(None, "gx", None),
            P("gx", None),
            P(),
            P("mem", None),
        ),
        out_specs=P("mem", None, "gx", None),
        check_vma=False,
    )
```

```python
import functools

import jax
import jax.numpy as jnp
from jax import lax
from jax.experimental import pallas as pl
from jax.experimental.pallas import tpu as pltpu
from jax.sharding import PartitionSpec as P

STEPS = 2


STIFF = 1.0
RELAX = 1.0
DTIME = 0.2

HIGHEST = lax.Precision.HIGHEST
HIGH = lax.Precision.HIGH
LANES = 128
SUBLANES = 8


def with_halo(cells, sides, width):
    for axis, dim in sides:
        count = lax.axis_size(axis)
        head = lax.slice_in_dim(cells, 0, width, axis=dim)
        tail = lax.slice_in_dim(cells, cells.shape[dim] - width, cells.shape[dim], axis=dim)
        cells = jnp.concatenate(
            [
                lax.ppermute(tail, axis, [(i, (i + 1) % count) for i in range(count)]),
                cells,
                lax.ppermute(head, axis, [((i + 1) % count, i) for i in range(count)]),
            ],
            axis=dim,
        )
    return cells


def tendency(fields, desired):
    density = fields[:, 0]
    moment_x = fields[:, 1]
    moment_y = fields[:, 2]
    speed_x = moment_x / density
    speed_y = moment_y / density
    sound = jnp.sqrt(STIFF * density)
    pressure = 0.5 * STIFF * density * density
    conserved = (density, moment_x, moment_y)
    fluxes_x = (moment_x, moment_x * speed_x + pressure, moment_y * speed_x)
    fluxes_y = (moment_y, moment_x * speed_y, moment_y * speed_y + pressure)
    reach_x = jnp.abs(speed_x) + sound
    bound_x = jnp.maximum(reach_x[:, :-1], reach_x[:, 1:])
    reach_y = (jnp.abs(speed_y) + sound)[:, 1:-1]
    bound_y = jnp.maximum(reach_y, jnp.roll(reach_y, -1, axis=-1))
    changes = []
    for quantity, normal_flux, cross_flux in zip(conserved, fluxes_x, fluxes_y):
        face_x = 0.5 * (normal_flux[:, :-1] + normal_flux[:, 1:]) - 0.5 * bound_x * (
            quantity[:, 1:] - quantity[:, :-1]
        )
        middle = quantity[:, 1:-1]
        cross_mid = cross_flux[:, 1:-1]
        face_y = 0.5 * (cross_mid + jnp.roll(cross_mid, -1, axis=-1)) - 0.5 * bound_y * (
            jnp.roll(middle, -1, axis=-1) - middle
        )
        changes.append(-(face_x[:, 1:] - face_x[:, :-1]) - (face_y - jnp.roll(face_y, 1, axis=-1)))
    centre = density[:, 1:-1]
    changes[1] = changes[1] + (centre * desired[0] - moment_x[:, 1:-1]) / RELAX
    changes[2] = changes[2] + (centre * desired[1] - moment_y[:, 1:-1]) / RELAX
    return jnp.stack(changes, axis=1)


def single_rims(fields):
    return with_halo(fields, (("gx", 2),), 1)


def plain(density, momenta, desired, factor_x, factor_y, factor_m):
    fields = jnp.concatenate([density[:, None], momenta], axis=1)
    for repeat in range(STEPS):
        sectioned = fields + DTIME * tendency(single_rims(fields), desired)
        second = sectioned + DTIME * tendency(single_rims(sectioned), desired)
        fields = 0.5 * fields + 0.5 * second
    along_y = jnp.einsum("mcxy,yb->mcxb", fields, factor_y, precision=HIGHEST)
    spread = lax.all_to_all(along_y, "gx", split_axis=3, concat_axis=2, tiled=True)
    projected = jnp.einsum(
        "mcxb,xa->mcab",
        spread,
        lax.all_gather(factor_x, "gx", axis=0, tiled=True),
        precision=HIGHEST,
    )
    returned = lax.all_to_all(projected, "gx", split_axis=2, concat_axis=3, tiled=True)
    member_terms = jnp.einsum("mcab,mk->kcab", returned, factor_m, precision=HIGHEST)
    return lax.psum_scatter(member_terms, "mem", scatter_dimension=0, tiled=True)


def cell_terms(q):
    rho, mx, my = q
    root = lax.rsqrt(rho)
    inverse = root * root
    sound = rho * root
    u = mx * inverse
    v = my * inverse
    pressure = (0.5 * STIFF) * (rho * rho)
    cross = my * u
    return dict(
        q=q,
        f=(mx, mx * u + pressure, cross),
        g=(my, cross, my * v + pressure),
        ax=jnp.abs(u) + sound,
        ay=jnp.abs(v) + sound,
    )


def x_face(low, high):
    bound = jnp.maximum(low["ax"], high["ax"])
    return tuple(
        fa + fb - bound * (b - a)
        for fa, fb, a, b in zip(low["f"], high["f"], low["q"], high["q"])
    )


def y_difference(row):
    axis = row["ay"].ndim - 1
    size = row["ay"].shape[axis]
    after = lambda a: pltpu.roll(a, size - 1, axis)
    before = lambda a: pltpu.roll(a, 1, axis)
    moved_q = tuple(after(a) for a in row["q"])
    moved_g = (moved_q[2], after(row["g"][1]), after(row["g"][2]))
    bound = jnp.maximum(row["ay"], after(row["ay"]))
    face = tuple(
        ga + gb - bound * (b - a)
        for ga, gb, a, b in zip(row["g"], moved_g, row["q"], moved_q)
    )
    return tuple(a - before(a) for a in face)


def section(row, low_face, high_face, wish):
    cross = y_difference(row)
    rho, mx, my = row["q"]
    half = 0.5 * DTIME
    spread = tuple(h + d for h, d in zip(high_face, cross))
    if low_face is not None:
        spread = tuple(a - l for a, l in zip(spread, low_face))
    keep = 1.0 - DTIME / RELAX
    return (
        rho - half * spread[0],
        keep * mx + rho * wish[0] - half * spread[1],
        keep * my + rho * wish[1] - half * spread[2],
    )


def half_copies(arrays, targets, odd, upper, sems):
    kinds = []
    for low in range(2):
        copies = []
        for t, target in enumerate(targets):
            base = 0
            for whole in arrays:
                lines, rows = whole.shape[:2]
                source = whole.at[:, pl.ds(low * (rows // 2), rows // 2), pl.ds(t * LANES, LANES)]
                copies.append((source, target.at[pl.ds(base, lines)]))
                base += lines
        kinds.append([
            pltpu.make_async_copy(source, target, sems.at[i])
            for i, (source, target) in enumerate(copies)
        ])
    for kind in range(2):

        @pl.when(odd == kind)
        def _():
            for copy in kinds[kind if upper else 1 - kind]:
                copy.start()

    return kinds[0]


def far_kernel(d, m, w, far, sems):
    odd = lax.rem(lax.axis_index("gx"), 2)
    targets = [far.at[t] for t in range(far.shape[0])]
    for copy in half_copies((d, m, w), targets, odd, 1, sems):
        copy.wait()


def own_kernel(d, m, w, fy, fx, far, own_d, own_m, own_w, own_fy, own_fx, near, half_sems, sems):
    tiles = own_d.shape[0]
    odd = lax.rem(lax.axis_index("gx"), 2)
    copies = half_copies((d, m, w), near, odd, 0, half_sems)
    wholes = []
    for whole, cut in ((d, own_d), (m, own_m), (w, own_w)):
        for t in range(tiles):
            wholes.append((whole.at[:, :, pl.ds(t * LANES, LANES)], cut.at[t]))
    wholes += [(fy, own_fy), (fx, own_fx)]
    wholes = [
        pltpu.make_async_copy(source, target, sems.at[i])
        for i, (source, target) in enumerate(wholes)
    ]
    for copy in wholes:
        copy.start()
    for copy in copies + wholes:
        copy.wait()


class Strip:
    def __init__(self, group, own, near, far):
        self.rows = own[2].shape[1] // 2
        self.half = self.rows // 2
        self.members = own[0].shape[1] // self.rows
        self.tiles = own[0].shape[0]
        cut = lambda ref: [ref.at[t] for t in range(self.tiles)]
        self.first, self.own = pl.multiple_of(group * SUBLANES, SUBLANES), tuple(cut(a) for a in own)
        self.near = near
        self.far = None if far is None else cut(far)
        self.odd = lax.rem(lax.axis_index("gx"), 2)
        self.sign = (1 - 2 * self.odd).astype(jnp.float32)

    def every(self, ref, first, count, stride):
        parts = [ref[t][pl.ds(first, count, stride=stride), :] for t in range(self.tiles)]
        return jnp.concatenate(parts, axis=1)

    def place(self, x):
        if x < self.half:
            ref, at, lines = self.far, x, self.half
        elif x < self.half + self.rows:
            ref, at, lines = self.own, x - self.half, self.rows
        else:
            ref, at, lines = self.near, x - self.half - self.rows, self.half
        return ref, self.odd * (lines - 1) + (1 - 2 * self.odd) * at, lines

    def load(self, x):
        ref, at, lines = self.place(x)
        if ref is self.own:
            d, m = ref[0], ref[1]
            base = 0
        else:
            d = m = ref
            base = self.members * lines
        first = self.first
        rho = self.every(d, first * lines + at, SUBLANES, lines)
        mx = self.every(m, base + first * 2 * lines + at, SUBLANES, 2 * lines)
        my = self.every(m, base + (first * 2 + 1) * lines + at, SUBLANES, 2 * lines)
        return rho, self.sign * mx, my

    def wish(self, x):
        ref, at, lines = self.place(x)
        if ref is self.own:
            ref, base = ref[2], 0
        else:
            base = 3 * self.members * lines
        line = [self.every(ref, base + c * lines + at, 1, 1) for c in range(2)]
        rate = DTIME / RELAX
        line = [(rate * self.sign) * line[0], rate * line[1]]
        return tuple(jnp.broadcast_to(a, (SUBLANES, a.shape[1])) for a in line)

    def keep(self, state, x, q):
        for c, a in enumerate((q[0], self.sign * q[1], q[2])):
            at = (3 * x + c) * self.members + self.first
            state[pl.ds(at, SUBLANES), :] = a


def march(computed, fetch, wish, emit, hook=None, bound=None):
    sections = len(computed) - 1
    known, terms, faces = {}, {}, {}

    def value(s, x):
        if (s, x) not in known:
            if x not in computed[s]:
                new = fetch(s, x)
            elif bound is not None and x == computed[s][-1]:
                share = 0.5 * DTIME * (0.5 if s % 2 == 0 else 1.0)
                new = tuple(
                    a + share * b for a, b in zip(bound(s - 1, x)["next"], face(s - 1, x - 1))
                )
            else:
                new = advanced(s, x, face(s - 1, x - 1))
            if x in computed[s]:
                emit(s, x, new)
            known[s, x] = new
        return known[s, x]

    def advanced(s, x, low):
        new = section(cell(s - 1, x), low, face(s - 1, x), wish(x))
        if s % 2 == 0:
            new = tuple(0.5 * (a + b) for a, b in zip(value(s - 2, x), new))
        return new

    def cell(s, x):
        if (s, x) not in terms:
            if bound is not None and x == computed[s + 1][-1]:
                terms[s, x] = bound(s, x)
            else:
                terms[s, x] = cell_terms(value(s, x))
        return terms[s, x]

    def face(s, x):
        if (s, x) not in faces:
            faces[s, x] = x_face(cell(s, x), cell(s, x + 1))
        return faces[s, x]

    for t in range(computed[1][0], computed[-1][-1] + sections + 1):
        for s in range(1, sections + 1):
            if t - s in computed[s]:
                value(s, t - s)
        if hook is not None:
            for s in range(sections):
                hook(s, t - s - 1, cell, advanced)


def edge_line(s, members):
    return s * 9 * members


def deal_columns(state, turned_fy, devices, members, lines):
    turned = lax.dot_general(
        turned_fy,
        state[...],
        (((1,), (1,)), ((), ())),
        precision=HIGH,
        preferred_element_type=jnp.float32,
    )
    shares = turned_fy.shape[0] // devices
    firsts, thirds = [], []
    for x in range(lines):
        at = 3 * x * members
        cut = lambda low, high: jnp.concatenate(
            [
                turned[r * devices : (r + 1) * devices, at + low : at + high]
                for r in range(shares)
            ],
            axis=1,
        )
        firsts.append(cut(0, 2 * members))
        thirds.append(cut(2 * members, 3 * members))
    return firsts, thirds


def member_kernel(near, fm, out):
    out[...] = jnp.concatenate([fm[...]] * (LANES // fm.shape[1]), axis=1)


def inner_kernel(own_d, own_m, own_w, fy, *rest):
    *near, edges, early, fy_out, state = rest
    rows = own_w.shape[1] // 2
    half = rows // 2
    members = own_d.shape[1] // rows
    sections = 2 * STEPS
    count = 2 * rows

    @pl.loop(0, members // SUBLANES)
    def _(group):
        strip = Strip(group, (own_d, own_m, own_w), near, None)

        def emit(s, x, q):
            if s == sections:
                strip.keep(state, x - rows, q)

        def hook(s, x, cell, advanced):
            if x == half + s:
                row = cell(s, x)
                arrays = (*row["q"], *row["f"][1:], row["ax"], *advanced(s + 1, x, None))
                for c, a in enumerate(arrays):
                    at = edge_line(s, members) + c * members + strip.first
                    edges[pl.ds(at, SUBLANES), :] = a

        computed = [range(0)] + [range(half + s, count - s) for s in range(1, sections + 1)]
        march(computed, lambda s, x: strip.load(x), strip.wish, emit, hook)

    devices = early.shape[0] // (2 * half)
    fy_out[...] = fy[...].T
    firsts, thirds = deal_columns(state, fy_out[...], devices, members, half)
    for i in range(half):
        early[pl.ds(i * devices, devices), :] = firsts[i]
        early[pl.ds((half + i) * devices, devices), :] = jnp.concatenate([thirds[i]] * 2, axis=1)


def outer_kernel(
    n_gx, own_d, own_m, own_w, far, fy, edges, early, fx, other_fm, out, state
):
    rows = own_w.shape[1] // 2
    half = rows // 2
    members = own_d.shape[1] // rows
    sections = 2 * STEPS
    for group in range(members // SUBLANES):
        strip = Strip(group, (own_d, own_m, own_w), None, far)

        @functools.cache
        def bound(s, x):
            at = edge_line(s, members) + strip.first
            a = [edges[pl.ds(at + c * members, SUBLANES), :] for c in range(9)]
            return dict(q=tuple(a[:3]), f=(a[1], a[3], a[4]), ax=a[5], next=tuple(a[6:]))

        def fetch(s, x):
            return strip.load(x) if x < half else bound(s, x)["q"]

        def emit(s, x, q):
            if s == sections:
                strip.keep(state, x - half, q)

        computed = [range(0)] + [range(s, half + s) for s in range(1, sections + 1)]
        march(computed, fetch, strip.wish, emit, bound=bound)

    devices = 2 * n_gx
    height = out.shape[0] // devices
    firsts, thirds = deal_columns(state, fy[...], devices, members, half)
    middle = LANES // 2
    for i in range(half):
        out[pl.ds(i, devices, stride=height), :] = firsts[i]
        out[pl.ds(half + i, devices, stride=height), :] = early[pl.ds(i * devices, devices), :]
        other = early[pl.ds((half + i) * devices, devices), :]
        out[pl.ds(rows + i, devices, stride=height), :] = jnp.concatenate(
            [thirds[i], other[:, middle:]], axis=1
        )
    mem = lax.axis_index("mem")
    for r in range(half):
        line = fx[pl.ds(mem * half + r, 1), :]
        out[pl.ds(rows + half + r, devices, stride=height), :] = jnp.broadcast_to(
            line, (devices, line.shape[1])
        )


def project_kernel(n_gx, rows, rm, inp, own_fm, other_fm, out, tall):
    devices = 2 * n_gx
    members = n_gx
    height = inp.shape[0] // devices
    half = rows // 2
    middle = LANES // 2
    low_rank = rm // 2
    line = lambda j: inp[pl.ds(j, devices, stride=height), :]
    swap = lambda a: pltpu.roll(a, middle, 1)
    lane = lax.broadcasted_iota(jnp.int32, (members, LANES), 1)
    firsts = [line(x) for x in range(rows)]
    firsts = jnp.concatenate(
        [
            jnp.concatenate([a[mem * n_gx : (mem + 1) * n_gx] for a in firsts], axis=0)
            for mem in range(2)
        ],
        axis=1,
    )
    thirds = [line(rows + i) for i in range(half)]
    pairs = [(a[:n_gx], a[n_gx:]) for a in thirds]
    thirds = jnp.concatenate(
        [jnp.where(lane < middle, a, swap(b)) for a, b in pairs]
        + [jnp.where(lane < middle, swap(a), b) for a, b in pairs],
        axis=0,
    )
    first = lax.axis_index("mem") == 0
    a, b = own_fm[...], other_fm[...]
    fm = jnp.concatenate([jnp.where(first, a, b), jnp.where(first, b, a)], axis=0)
    wide = lax.broadcasted_iota(jnp.int32, fm.shape, 1)
    first_half = wide % rm < low_rank
    repeated = (
        jnp.where(first_half, fm, pltpu.roll(fm, low_rank, 1)),
        jnp.where(first_half, pltpu.roll(fm, LANES - low_rank, 1), fm),
    )
    block = lane // low_rank
    part = lambda k, mem: repeated[k][mem * members : (mem + 1) * members]
    count = LANES // members
    diagonal = jnp.concatenate(
        [
            jnp.concatenate(
                [jnp.where(block == p, part(k, mem), 0.0) for mem in range(2) for p in range(count)],
                axis=0,
            )
            for k in range(2)
        ],
        axis=1,
    )
    small = jnp.concatenate(
        [
            jnp.where(
                block == p,
                part(0, mem),
                jnp.where(block == count // 2 + p, part(1, mem), 0.0),
            )
            for mem in range(2)
            for p in range(count // 2)
        ],
        axis=0,
    )
    product = functools.partial(jnp.dot, precision=HIGH, preferred_element_type=jnp.float32)
    firsts = product(firsts, diagonal)
    thirds = product(thirds, small)
    blocks = jnp.concatenate([firsts[:, :LANES], thirds, firsts[:, LANES:]], axis=1)
    halves = [line(rows + half + r) for r in range(half)]
    lines = [a[:n_gx] for a in halves] + [a[n_gx:] for a in halves]
    odd = lax.broadcasted_iota(jnp.int32, (n_gx, LANES), 0) % 2 == 1
    lines = [jnp.where(odd, lines[rows - 1 - r], lines[r]) for r in range(rows)]
    fx = jnp.concatenate(lines, axis=0)
    core = product(fx.T, blocks)
    high = out.shape[0] // devices
    for t in range(3):
        tall[t] = core[:, t * LANES : (t + 1) * LANES]
    lane = lax.broadcasted_iota(jnp.int32, (n_gx, LANES), 1)
    for a in range(SUBLANES):
        for k in range(2):
            out[pl.ds(k * n_gx * high + a, n_gx, stride=high), :] = tall[
                2 * k, pl.ds(a, n_gx, stride=SUBLANES), :
            ]
    for i in range(SUBLANES // 2):
        upper = tall[1, pl.ds(i, n_gx, stride=SUBLANES), :]
        lower = tall[1, pl.ds(i + SUBLANES // 2, n_gx, stride=SUBLANES), :]
        first = jnp.where(lane < LANES // 2, upper, pltpu.roll(lower, LANES // 2, 1))
        second = jnp.where(lane < LANES // 2, pltpu.roll(upper, LANES // 2, 1), lower)
        out[pl.ds(SUBLANES + i, n_gx, stride=high), :] = first
        out[pl.ds(n_gx * high + SUBLANES + i, n_gx, stride=high), :] = second


def gather_kernel(shares, lows, inp, core, out, sems):
    devices = LANES // shares
    high = inp.shape[0] // devices
    quarter = SUBLANES // 2

    def turn(first):
        return jnp.concatenate(
            [inp[pl.ds(first + i, devices, stride=high), :] for i in range(quarter)], axis=0
        ).T

    def place(turned, base, apart, c, a0):
        for i in range(quarter):
            line = jnp.concatenate(
                [
                    turned[base + r * apart : base + r * apart + lows, i * devices : (i + 1) * devices]
                    for r in range(shares)
                ],
                axis=1,
            )
            out[c, pl.ds(a0 + i, lows, stride=SUBLANES), :] = line

    def send(c):
        source = out.at[c].reshape(lows, SUBLANES, LANES)
        return pltpu.make_async_copy(source, core.at[:, c], sems.at[c])

    turned = [turn(h * quarter) for h in range(2)]
    for c in range(2):
        for h in range(2):
            place(turned[h], c * lows, 2 * lows, c, h * quarter)
        send(c).start()
    turned = turn(SUBLANES)
    for h in range(2):
        place(turned, h * shares * lows, lows, 2, h * quarter)
    send(2).start()
    for c in range(3):
        send(c).wait()


def exchange(chunks, devices):
    block = chunks.reshape(devices, chunks.shape[0] // devices, 1, chunks.shape[1])
    moved = lax.all_to_all(block, ("mem", "gx"), split_axis=0, concat_axis=0, tiled=True)
    return moved.reshape(chunks.shape)


def laid_out(density, factor_x, factor_y, factor_m):
    members, rows, cells_y = density.shape
    n_mem, n_gx = lax.axis_size("mem"), lax.axis_size("gx")
    rx, ry, rm = factor_x.shape[1], factor_y.shape[1], factor_m.shape[1]
    shares = ry // (n_mem * n_gx)
    return (
        n_mem == 2
        and rows == 4 * STEPS == SUBLANES
        and members == n_gx
        and n_gx % 2 == 0
        and members * rows == LANES
        and members % SUBLANES == 0
        and cells_y % LANES == 0
        and rx == LANES == n_gx * SUBLANES
        and ry == LANES == shares * n_mem * n_gx
        and shares * rm == LANES
        and shares * rm // 2 * 2 == LANES
        and 2 * shares * members == LANES
        and 2 * members == rm
    )


def on_device(density, momenta, desired, factor_x, factor_y, factor_m):
    if not laid_out(density, factor_x, factor_y, factor_m):
        return plain(density, momenta, desired, factor_x, factor_y, factor_m)
    members, rows, cells_y = density.shape
    n_gx = lax.axis_size("gx")
    devices = 2 * n_gx
    rx, ry, rm = factor_x.shape[1], factor_y.shape[1], factor_m.shape[1]
    shares = ry // devices
    params = pltpu.CompilerParams(vmem_limit_bytes=32 * 1024 * 1024)
    vmem = pl.BlockSpec(memory_space=pltpu.VMEM)
    anywhere = pl.BlockSpec(memory_space=pl.ANY)
    tiles = cells_y // LANES
    half = rows // 2
    shape = lambda *dims: jax.ShapeDtypeStruct(dims, jnp.float32)
    held = lambda *arrays: [pltpu.with_memory_space_constraint(a, pltpu.HBM) for a in arrays]
    own = [a.reshape(-1, rows, cells_y) for a in (density, momenta, desired)]
    lines = [a.shape[0] for a in own]
    packed = (sum(lines), half, LANES)
    far = pl.pallas_call(
        far_kernel,
        out_shape=shape(tiles, *packed),
        in_specs=[anywhere] * 3,
        out_specs=vmem,
        scratch_shapes=[pltpu.SemaphoreType.DMA((3 * tiles,))],
        compiler_params=params,
        name="far",
    )(*held(*own))
    *own, fy, fx, near = pl.pallas_call(
        own_kernel,
        out_shape=[shape(tiles, n, rows, LANES) for n in lines]
        + [shape(*factor_y.shape), shape(*factor_x.shape), [shape(*packed)] * tiles],
        in_specs=[anywhere] * 6,
        out_specs=[vmem] * 5 + [[vmem] * tiles],
        scratch_shapes=[
            pltpu.SemaphoreType.DMA((3 * tiles,)),
            pltpu.SemaphoreType.DMA((3 * tiles + 2,)),
        ],
        compiler_params=params,
        name="own",
    )(*held(*own, factor_y, factor_x), far)
    own = [a.reshape(tiles, -1, LANES) for a in own]
    far = far.reshape(tiles, -1, LANES)
    near = [a.reshape(-1, LANES) for a in near]
    far = lax.ppermute(far, "gx", [(i, (i - 1 + i % 2 * 2) % n_gx) for i in range(n_gx)])
    near = [lax.ppermute(a, "gx", [(i, i ^ 1) for i in range(n_gx)]) for a in near]
    own_fm = pl.pallas_call(
        member_kernel,
        out_shape=shape(members, LANES),
        in_specs=[anywhere, vmem],
        out_specs=vmem,
        compiler_params=params,
        name="member",
    )(near[-1], factor_m)
    other_fm = lax.ppermute(own_fm, "mem", [(0, 1), (1, 0)])
    sections = 2 * STEPS
    edges, early, turned_fy = pl.pallas_call(
        inner_kernel,
        out_shape=[
            shape(sections * 9 * members, cells_y),
            shape(2 * half * devices, LANES),
            shape(ry, cells_y),
        ],
        scratch_shapes=[pltpu.VMEM((3 * half * members, cells_y), jnp.float32)],
        compiler_params=params,
        name="inner",
    )(*own, fy, *near)
    height = rows + 2 * half
    sent = pl.pallas_call(
        functools.partial(outer_kernel, n_gx),
        out_shape=shape(devices * height, LANES),
        in_specs=[vmem] * 8 + [anywhere],
        out_specs=vmem,
        scratch_shapes=[pltpu.VMEM((3 * half * members, cells_y), jnp.float32)],
        compiler_params=params,
        name="outer",
    )(*own, far, turned_fy, edges, early, fx, other_fm)
    got = exchange(sent, devices)
    lows = rm // 2
    high = 3 * shares * lows * SUBLANES // LANES
    sent = pl.pallas_call(
        functools.partial(project_kernel, n_gx, rows, rm),
        out_shape=jax.ShapeDtypeStruct((devices * high, LANES), jnp.float32),
        scratch_shapes=[pltpu.VMEM((3, rx, LANES), jnp.float32)],
        compiler_params=params,
        name="project",
    )(got, own_fm, other_fm)
    got = exchange(sent, devices)
    core = pl.pallas_call(
        functools.partial(gather_kernel, shares, lows),
        out_shape=shape(lows, 3, SUBLANES, LANES),
        out_specs=anywhere,
        scratch_shapes=[
            pltpu.VMEM((3, lows * SUBLANES, LANES), jnp.float32),
            pltpu.SemaphoreType.DMA((3,)),
        ],
        compiler_params=params,
        name="gather",
    )(got)
    return core


def solution(mesh):
    return jax.shard_map(
        on_device,
        mesh=mesh,
        in_specs=(
            P("mem", "gx", None),
            P("mem", None, "gx", None),
            P(None, "gx", None),
            P("gx", None),
            P(),
            P("mem", None),
        ),
        out_specs=P("mem", None, "gx", None),
        check_vma=False,
    )
```

```python
import functools

import jax
import jax.numpy as jnp
from jax import lax
from jax.experimental import pallas as pl
from jax.experimental.pallas import tpu as pltpu
from jax.sharding import PartitionSpec as P

STEPS = 2


STIFF = 1.0
RELAX = 1.0
DTIME = 0.2

HIGHEST = lax.Precision.HIGHEST
HIGH = lax.Precision.HIGH
LANES = 128
SUBLANES = 8


def with_halo(cells, sides, width):
    for axis, dim in sides:
        count = lax.axis_size(axis)
        head = lax.slice_in_dim(cells, 0, width, axis=dim)
        tail = lax.slice_in_dim(cells, cells.shape[dim] - width, cells.shape[dim], axis=dim)
        cells = jnp.concatenate(
            [
                lax.ppermute(tail, axis, [(i, (i + 1) % count) for i in range(count)]),
                cells,
                lax.ppermute(head, axis, [((i + 1) % count, i) for i in range(count)]),
            ],
            axis=dim,
        )
    return cells


def tendency(fields, desired):
    density = fields[:, 0]
    moment_x = fields[:, 1]
    moment_y = fields[:, 2]
    speed_x = moment_x / density
    speed_y = moment_y / density
    sound = jnp.sqrt(STIFF * density)
    pressure = 0.5 * STIFF * density * density
    conserved = (density, moment_x, moment_y)
    fluxes_x = (moment_x, moment_x * speed_x + pressure, moment_y * speed_x)
    fluxes_y = (moment_y, moment_x * speed_y, moment_y * speed_y + pressure)
    reach_x = jnp.abs(speed_x) + sound
    bound_x = jnp.maximum(reach_x[:, :-1], reach_x[:, 1:])
    reach_y = (jnp.abs(speed_y) + sound)[:, 1:-1]
    bound_y = jnp.maximum(reach_y, jnp.roll(reach_y, -1, axis=-1))
    changes = []
    for quantity, normal_flux, cross_flux in zip(conserved, fluxes_x, fluxes_y):
        face_x = 0.5 * (normal_flux[:, :-1] + normal_flux[:, 1:]) - 0.5 * bound_x * (
            quantity[:, 1:] - quantity[:, :-1]
        )
        middle = quantity[:, 1:-1]
        cross_mid = cross_flux[:, 1:-1]
        face_y = 0.5 * (cross_mid + jnp.roll(cross_mid, -1, axis=-1)) - 0.5 * bound_y * (
            jnp.roll(middle, -1, axis=-1) - middle
        )
        changes.append(-(face_x[:, 1:] - face_x[:, :-1]) - (face_y - jnp.roll(face_y, 1, axis=-1)))
    centre = density[:, 1:-1]
    changes[1] = changes[1] + (centre * desired[0] - moment_x[:, 1:-1]) / RELAX
    changes[2] = changes[2] + (centre * desired[1] - moment_y[:, 1:-1]) / RELAX
    return jnp.stack(changes, axis=1)


def single_rims(fields):
    return with_halo(fields, (("gx", 2),), 1)


def plain(density, momenta, desired, factor_x, factor_y, factor_m):
    fields = jnp.concatenate([density[:, None], momenta], axis=1)
    for repeat in range(STEPS):
        sectioned = fields + DTIME * tendency(single_rims(fields), desired)
        second = sectioned + DTIME * tendency(single_rims(sectioned), desired)
        fields = 0.5 * fields + 0.5 * second
    along_y = jnp.einsum("mcxy,yb->mcxb", fields, factor_y, precision=HIGHEST)
    spread = lax.all_to_all(along_y, "gx", split_axis=3, concat_axis=2, tiled=True)
    projected = jnp.einsum(
        "mcxb,xa->mcab",
        spread,
        lax.all_gather(factor_x, "gx", axis=0, tiled=True),
        precision=HIGHEST,
    )
    returned = lax.all_to_all(projected, "gx", split_axis=2, concat_axis=3, tiled=True)
    member_terms = jnp.einsum("mcab,mk->kcab", returned, factor_m, precision=HIGHEST)
    return lax.psum_scatter(member_terms, "mem", scatter_dimension=0, tiled=True)


def cell_terms(q):
    rho, mx, my = q
    root = lax.rsqrt(rho)
    inverse = root * root
    sound = rho * root
    u = mx * inverse
    v = my * inverse
    pressure = (0.5 * STIFF) * (rho * rho)
    cross = my * u
    return dict(
        q=q,
        f=(mx, mx * u + pressure, cross),
        g=(my, cross, my * v + pressure),
        ax=jnp.abs(u) + sound,
        ay=jnp.abs(v) + sound,
    )


def x_face(low, high):
    bound = jnp.maximum(low["ax"], high["ax"])
    return tuple(
        fa + fb - bound * (b - a)
        for fa, fb, a, b in zip(low["f"], high["f"], low["q"], high["q"])
    )


def y_difference(row):
    axis = row["ay"].ndim - 1
    size = row["ay"].shape[axis]
    after = lambda a: pltpu.roll(a, size - 1, axis)
    before = lambda a: pltpu.roll(a, 1, axis)
    moved_q = tuple(after(a) for a in row["q"])
    moved_g = (moved_q[2], after(row["g"][1]), after(row["g"][2]))
    bound = jnp.maximum(row["ay"], after(row["ay"]))
    face = tuple(
        ga + gb - bound * (b - a)
        for ga, gb, a, b in zip(row["g"], moved_g, row["q"], moved_q)
    )
    return tuple(a - before(a) for a in face)


def section(row, low_face, high_face, wish):
    cross = y_difference(row)
    rho, mx, my = row["q"]
    half = 0.5 * DTIME
    spread = tuple(h + d for h, d in zip(high_face, cross))
    if low_face is not None:
        spread = tuple(a - l for a, l in zip(spread, low_face))
    keep = 1.0 - DTIME / RELAX
    return (
        rho - half * spread[0],
        keep * mx + rho * wish[0] - half * spread[1],
        keep * my + rho * wish[1] - half * spread[2],
    )


def half_copies(arrays, targets, odd, upper, sems):
    kinds = []
    for low in range(2):
        copies = []
        for t, target in enumerate(targets):
            base = 0
            for whole in arrays:
                lines, rows = whole.shape[:2]
                source = whole.at[:, pl.ds(low * (rows // 2), rows // 2), pl.ds(t * LANES, LANES)]
                copies.append((source, target.at[pl.ds(base, lines)]))
                base += lines
        kinds.append([
            pltpu.make_async_copy(source, target, sems.at[i])
            for i, (source, target) in enumerate(copies)
        ])
    for kind in range(2):

        @pl.when(odd == kind)
        def _():
            for copy in kinds[kind if upper else 1 - kind]:
                copy.start()

    return kinds[0]


def far_kernel(d, m, w, far, sems):
    odd = lax.rem(lax.axis_index("gx"), 2)
    targets = [far.at[t] for t in range(far.shape[0])]
    for copy in half_copies((d, m, w), targets, odd, 1, sems):
        copy.wait()


def own_kernel(d, m, w, fy, fx, far, own_d, own_m, own_w, own_fy, own_fx, near, half_sems, sems):
    tiles = own_d.shape[0]
    odd = lax.rem(lax.axis_index("gx"), 2)
    copies = half_copies((d, m, w), near, odd, 0, half_sems)
    wholes = []
    for whole, cut in ((d, own_d), (m, own_m), (w, own_w)):
        for t in range(tiles):
            wholes.append((whole.at[:, :, pl.ds(t * LANES, LANES)], cut.at[t]))
    wholes += [(fy, own_fy), (fx, own_fx)]
    wholes = [
        pltpu.make_async_copy(source, target, sems.at[i])
        for i, (source, target) in enumerate(wholes)
    ]
    for copy in wholes:
        copy.start()
    for copy in copies + wholes:
        copy.wait()


class Strip:
    def __init__(self, group, own, near, far):
        self.rows = own[2].shape[1] // 2
        self.half = self.rows // 2
        self.members = own[0].shape[1] // self.rows
        self.tiles = own[0].shape[0]
        cut = lambda ref: [ref.at[t] for t in range(self.tiles)]
        self.first, self.own = pl.multiple_of(group * SUBLANES, SUBLANES), tuple(cut(a) for a in own)
        self.near = near
        self.far = None if far is None else cut(far)
        self.odd = lax.rem(lax.axis_index("gx"), 2)
        self.sign = (1 - 2 * self.odd).astype(jnp.float32)

    def every(self, ref, first, count, stride):
        parts = [ref[t][pl.ds(first, count, stride=stride), :] for t in range(self.tiles)]
        return jnp.concatenate(parts, axis=1)

    def place(self, x):
        if x < self.half:
            ref, at, lines = self.far, x, self.half
        elif x < self.half + self.rows:
            ref, at, lines = self.own, x - self.half, self.rows
        else:
            ref, at, lines = self.near, x - self.half - self.rows, self.half
        return ref, self.odd * (lines - 1) + (1 - 2 * self.odd) * at, lines

    def load(self, x):
        ref, at, lines = self.place(x)
        if ref is self.own:
            d, m = ref[0], ref[1]
            base = 0
        else:
            d = m = ref
            base = self.members * lines
        first = self.first
        rho = self.every(d, first * lines + at, SUBLANES, lines)
        mx = self.every(m, base + first * 2 * lines + at, SUBLANES, 2 * lines)
        my = self.every(m, base + (first * 2 + 1) * lines + at, SUBLANES, 2 * lines)
        return rho, self.sign * mx, my

    def wish(self, x):
        ref, at, lines = self.place(x)
        if ref is self.own:
            ref, base = ref[2], 0
        else:
            base = 3 * self.members * lines
        line = [self.every(ref, base + c * lines + at, 1, 1) for c in range(2)]
        rate = DTIME / RELAX
        line = [(rate * self.sign) * line[0], rate * line[1]]
        return tuple(jnp.broadcast_to(a, (SUBLANES, a.shape[1])) for a in line)

    def keep(self, state, x, q):
        for c, a in enumerate((q[0], self.sign * q[1], q[2])):
            at = (3 * x + c) * self.members + self.first
            state[pl.ds(at, SUBLANES), :] = a


def march(computed, fetch, wish, emit, hook=None, bound=None):
    sections = len(computed) - 1
    known, terms, faces = {}, {}, {}

    def value(s, x):
        if (s, x) not in known:
            if x not in computed[s]:
                new = fetch(s, x)
            elif bound is not None and x == computed[s][-1]:
                share = 0.5 * DTIME * (0.5 if s % 2 == 0 else 1.0)
                new = tuple(
                    a + share * b for a, b in zip(bound(s - 1, x)["next"], face(s - 1, x - 1))
                )
            else:
                new = advanced(s, x, face(s - 1, x - 1))
            if x in computed[s]:
                emit(s, x, new)
            known[s, x] = new
        return known[s, x]

    def advanced(s, x, low):
        new = section(cell(s - 1, x), low, face(s - 1, x), wish(x))
        if s % 2 == 0:
            new = tuple(0.5 * (a + b) for a, b in zip(value(s - 2, x), new))
        return new

    def cell(s, x):
        if (s, x) not in terms:
            if bound is not None and x == computed[s + 1][-1]:
                terms[s, x] = bound(s, x)
            else:
                terms[s, x] = cell_terms(value(s, x))
        return terms[s, x]

    def face(s, x):
        if (s, x) not in faces:
            faces[s, x] = x_face(cell(s, x), cell(s, x + 1))
        return faces[s, x]

    for t in range(computed[1][0], computed[-1][-1] + sections + 1):
        for s in range(1, sections + 1):
            if t - s in computed[s]:
                value(s, t - s)
        if hook is not None:
            for s in range(sections):
                hook(s, t - s - 1, cell, advanced)


def edge_line(s, members):
    return s * 9 * members


def deal_columns(state, turned_fy, devices, members, lines):
    turned = lax.dot_general(
        turned_fy,
        state[...],
        (((1,), (1,)), ((), ())),
        precision=HIGH,
        preferred_element_type=jnp.float32,
    )
    shares = turned_fy.shape[0] // devices
    firsts, thirds = [], []
    for x in range(lines):
        at = 3 * x * members
        cut = lambda low, high: jnp.concatenate(
            [
                turned[r * devices : (r + 1) * devices, at + low : at + high]
                for r in range(shares)
            ],
            axis=1,
        )
        firsts.append(cut(0, 2 * members))
        thirds.append(cut(2 * members, 3 * members))
    return firsts, thirds


def member_kernel(near, fm, out):
    out[...] = jnp.concatenate([fm[...]] * (LANES // fm.shape[1]), axis=1)


def inner_kernel(own_d, own_m, own_w, fy, *rest):
    *near, edges, early, fy_out, state = rest
    rows = own_w.shape[1] // 2
    half = rows // 2
    members = own_d.shape[1] // rows
    sections = 2 * STEPS
    count = 2 * rows

    @pl.loop(0, members // SUBLANES)
    def _(group):
        strip = Strip(group, (own_d, own_m, own_w), near, None)

        def emit(s, x, q):
            if s == sections:
                strip.keep(state, x - rows, q)

        def hook(s, x, cell, advanced):
            if x == half + s:
                row = cell(s, x)
                arrays = (*row["q"], *row["f"][1:], row["ax"], *advanced(s + 1, x, None))
                for c, a in enumerate(arrays):
                    at = edge_line(s, members) + c * members + strip.first
                    edges[pl.ds(at, SUBLANES), :] = a

        computed = [range(0)] + [range(half + s, count - s) for s in range(1, sections + 1)]
        march(computed, lambda s, x: strip.load(x), strip.wish, emit, hook)

    devices = early.shape[0] // (2 * half)
    fy_out[...] = fy[...].T
    firsts, thirds = deal_columns(state, fy_out[...], devices, members, half)
    for i in range(half):
        early[pl.ds(i * devices, devices), :] = firsts[i]
        early[pl.ds((half + i) * devices, devices), :] = jnp.concatenate([thirds[i]] * 2, axis=1)


def outer_kernel(
    n_gx, own_d, own_m, own_w, far, fy, edges, early, fx, other_fm, out, state
):
    rows = own_w.shape[1] // 2
    half = rows // 2
    members = own_d.shape[1] // rows
    sections = 2 * STEPS
    for group in range(members // SUBLANES):
        strip = Strip(group, (own_d, own_m, own_w), None, far)

        @functools.cache
        def bound(s, x):
            at = edge_line(s, members) + strip.first
            a = [edges[pl.ds(at + c * members, SUBLANES), :] for c in range(9)]
            return dict(q=tuple(a[:3]), f=(a[1], a[3], a[4]), ax=a[5], next=tuple(a[6:]))

        def fetch(s, x):
            return strip.load(x) if x < half else bound(s, x)["q"]

        def emit(s, x, q):
            if s == sections:
                strip.keep(state, x - half, q)

        computed = [range(0)] + [range(s, half + s) for s in range(1, sections + 1)]
        march(computed, fetch, strip.wish, emit, bound=bound)

    devices = 2 * n_gx
    height = out.shape[0] // devices
    firsts, thirds = deal_columns(state, fy[...], devices, members, half)
    middle = LANES // 2
    for i in range(half):
        out[pl.ds(i, devices, stride=height), :] = firsts[i]
        out[pl.ds(half + i, devices, stride=height), :] = early[pl.ds(i * devices, devices), :]
        other = early[pl.ds((half + i) * devices, devices), :]
        out[pl.ds(rows + i, devices, stride=height), :] = jnp.concatenate(
            [thirds[i], other[:, middle:]], axis=1
        )
    mem = lax.axis_index("mem")
    for r in range(half):
        line = fx[pl.ds(mem * half + r, 1), :]
        out[pl.ds(rows + half + r, devices, stride=height), :] = jnp.broadcast_to(
            line, (devices, line.shape[1])
        )


def project_kernel(n_gx, rows, rm, inp, own_fm, other_fm, out, tall):
    devices = 2 * n_gx
    members = n_gx
    height = inp.shape[0] // devices
    half = rows // 2
    middle = LANES // 2
    low_rank = rm // 2
    line = lambda j: inp[pl.ds(j, devices, stride=height), :]
    swap = lambda a: pltpu.roll(a, middle, 1)
    lane = lax.broadcasted_iota(jnp.int32, (members, LANES), 1)
    firsts = [line(x) for x in range(rows)]
    firsts = jnp.concatenate(
        [
            jnp.concatenate([a[mem * n_gx : (mem + 1) * n_gx] for a in firsts], axis=0)
            for mem in range(2)
        ],
        axis=1,
    )
    thirds = [line(rows + i) for i in range(half)]
    pairs = [(a[:n_gx], a[n_gx:]) for a in thirds]
    thirds = jnp.concatenate(
        [jnp.where(lane < middle, a, swap(b)) for a, b in pairs]
        + [jnp.where(lane < middle, swap(a), b) for a, b in pairs],
        axis=0,
    )
    first = lax.axis_index("mem") == 0
    a, b = own_fm[...], other_fm[...]
    fm = jnp.concatenate([jnp.where(first, a, b), jnp.where(first, b, a)], axis=0)
    wide = lax.broadcasted_iota(jnp.int32, fm.shape, 1)
    first_half = wide % rm < low_rank
    repeated = (
        jnp.where(first_half, fm, pltpu.roll(fm, low_rank, 1)),
        jnp.where(first_half, pltpu.roll(fm, LANES - low_rank, 1), fm),
    )
    block = lane // low_rank
    part = lambda k, mem: repeated[k][mem * members : (mem + 1) * members]
    count = LANES // members
    diagonal = jnp.concatenate(
        [
            jnp.concatenate(
                [jnp.where(block == p, part(k, mem), 0.0) for mem in range(2) for p in range(count)],
                axis=0,
            )
            for k in range(2)
        ],
        axis=1,
    )
    small = jnp.concatenate(
        [
            jnp.where(
                block == p,
                part(0, mem),
                jnp.where(block == count // 2 + p, part(1, mem), 0.0),
            )
            for mem in range(2)
            for p in range(count // 2)
        ],
        axis=0,
    )
    product = functools.partial(jnp.dot, precision=HIGH, preferred_element_type=jnp.float32)
    halves = [line(rows + half + r) for r in range(half)]
    lines = [a[:n_gx] for a in halves] + [a[n_gx:] for a in halves]
    odd = lax.broadcasted_iota(jnp.int32, (n_gx, LANES), 0) % 2 == 1
    lines = [jnp.where(odd, lines[rows - 1 - r], lines[r]) for r in range(rows)]
    fx = jnp.concatenate(lines, axis=0)
    turned_fx = fx.T
    firsts = product(product(turned_fx, firsts), diagonal)
    thirds = product(product(turned_fx, thirds), small)
    core = jnp.concatenate([firsts[:, :LANES], thirds, firsts[:, LANES:]], axis=1)
    high = out.shape[0] // devices
    for t in range(3):
        tall[t] = core[:, t * LANES : (t + 1) * LANES]
    lane = lax.broadcasted_iota(jnp.int32, (n_gx, LANES), 1)
    for a in range(SUBLANES):
        for k in range(2):
            out[pl.ds(k * n_gx * high + a, n_gx, stride=high), :] = tall[
                2 * k, pl.ds(a, n_gx, stride=SUBLANES), :
            ]
    for i in range(SUBLANES // 2):
        upper = tall[1, pl.ds(i, n_gx, stride=SUBLANES), :]
        lower = tall[1, pl.ds(i + SUBLANES // 2, n_gx, stride=SUBLANES), :]
        first = jnp.where(lane < LANES // 2, upper, pltpu.roll(lower, LANES // 2, 1))
        second = jnp.where(lane < LANES // 2, pltpu.roll(upper, LANES // 2, 1), lower)
        out[pl.ds(SUBLANES + i, n_gx, stride=high), :] = first
        out[pl.ds(n_gx * high + SUBLANES + i, n_gx, stride=high), :] = second


def gather_kernel(shares, lows, inp, core, out, sems):
    devices = LANES // shares
    high = inp.shape[0] // devices
    quarter = SUBLANES // 2

    def turn(first):
        return jnp.concatenate(
            [inp[pl.ds(first + i, devices, stride=high), :] for i in range(quarter)], axis=0
        ).T

    def place(turned, base, apart, c, a0):
        for i in range(quarter):
            line = jnp.concatenate(
                [
                    turned[base + r * apart : base + r * apart + lows, i * devices : (i + 1) * devices]
                    for r in range(shares)
                ],
                axis=1,
            )
            out[c, :, a0 + i, :] = line

    def send(c):
        return pltpu.make_async_copy(out.at[c], core.at[:, c], sems.at[c])

    turned = [turn(h * quarter) for h in range(2)]
    for c in range(2):
        for h in range(2):
            place(turned[h], c * lows, 2 * lows, c, h * quarter)
        send(c).start()
    turned = turn(SUBLANES)
    for h in range(2):
        place(turned, h * shares * lows, lows, 2, h * quarter)
    send(2).start()
    for c in range(3):
        send(c).wait()


def exchange(chunks, devices):
    block = chunks.reshape(devices, chunks.shape[0] // devices, 1, chunks.shape[1])
    moved = lax.all_to_all(block, ("mem", "gx"), split_axis=0, concat_axis=0, tiled=True)
    return moved.reshape(chunks.shape)


def laid_out(density, factor_x, factor_y, factor_m):
    members, rows, cells_y = density.shape
    n_mem, n_gx = lax.axis_size("mem"), lax.axis_size("gx")
    rx, ry, rm = factor_x.shape[1], factor_y.shape[1], factor_m.shape[1]
    shares = ry // (n_mem * n_gx)
    return (
        n_mem == 2
        and rows == 4 * STEPS == SUBLANES
        and members == n_gx
        and n_gx % 2 == 0
        and members * rows == LANES
        and members % SUBLANES == 0
        and cells_y % LANES == 0
        and rx == LANES == n_gx * SUBLANES
        and ry == LANES == shares * n_mem * n_gx
        and shares * rm == LANES
        and shares * rm // 2 * 2 == LANES
        and 2 * shares * members == LANES
        and 2 * members == rm
    )


def on_device(density, momenta, desired, factor_x, factor_y, factor_m):
    if not laid_out(density, factor_x, factor_y, factor_m):
        return plain(density, momenta, desired, factor_x, factor_y, factor_m)
    members, rows, cells_y = density.shape
    n_gx = lax.axis_size("gx")
    devices = 2 * n_gx
    rx, ry, rm = factor_x.shape[1], factor_y.shape[1], factor_m.shape[1]
    shares = ry // devices
    params = pltpu.CompilerParams(vmem_limit_bytes=32 * 1024 * 1024)
    vmem = pl.BlockSpec(memory_space=pltpu.VMEM)
    anywhere = pl.BlockSpec(memory_space=pl.ANY)
    tiles = cells_y // LANES
    half = rows // 2
    shape = lambda *dims: jax.ShapeDtypeStruct(dims, jnp.float32)
    held = lambda *arrays: [pltpu.with_memory_space_constraint(a, pltpu.HBM) for a in arrays]
    own = [a.reshape(-1, rows, cells_y) for a in (density, momenta, desired)]
    lines = [a.shape[0] for a in own]
    packed = (sum(lines), half, LANES)
    far = pl.pallas_call(
        far_kernel,
        out_shape=shape(tiles, *packed),
        in_specs=[anywhere] * 3,
        out_specs=vmem,
        scratch_shapes=[pltpu.SemaphoreType.DMA((3 * tiles,))],
        compiler_params=params,
        name="far",
    )(*held(*own))
    *own, fy, fx, near = pl.pallas_call(
        own_kernel,
        out_shape=[shape(tiles, n, rows, LANES) for n in lines]
        + [shape(*factor_y.shape), shape(*factor_x.shape), [shape(*packed)] * tiles],
        in_specs=[anywhere] * 6,
        out_specs=[vmem] * 5 + [[vmem] * tiles],
        scratch_shapes=[
            pltpu.SemaphoreType.DMA((3 * tiles,)),
            pltpu.SemaphoreType.DMA((3 * tiles + 2,)),
        ],
        compiler_params=params,
        name="own",
    )(*held(*own, factor_y, factor_x), far)
    own = [a.reshape(tiles, -1, LANES) for a in own]
    far = far.reshape(tiles, -1, LANES)
    near = [a.reshape(-1, LANES) for a in near]
    far = lax.ppermute(far, "gx", [(i, (i - 1 + i % 2 * 2) % n_gx) for i in range(n_gx)])
    near = [lax.ppermute(a, "gx", [(i, i ^ 1) for i in range(n_gx)]) for a in near]
    own_fm = pl.pallas_call(
        member_kernel,
        out_shape=shape(members, LANES),
        in_specs=[anywhere, vmem],
        out_specs=vmem,
        compiler_params=params,
        name="member",
    )(near[-1], factor_m)
    other_fm = lax.ppermute(own_fm, "mem", [(0, 1), (1, 0)])
    sections = 2 * STEPS
    edges, early, turned_fy = pl.pallas_call(
        inner_kernel,
        out_shape=[
            shape(sections * 9 * members, cells_y),
            shape(2 * half * devices, LANES),
            shape(ry, cells_y),
        ],
        scratch_shapes=[pltpu.VMEM((3 * half * members, cells_y), jnp.float32)],
        compiler_params=params,
        name="inner",
    )(*own, fy, *near)
    height = rows + 2 * half
    sent = pl.pallas_call(
        functools.partial(outer_kernel, n_gx),
        out_shape=shape(devices * height, LANES),
        in_specs=[vmem] * 8 + [anywhere],
        out_specs=vmem,
        scratch_shapes=[pltpu.VMEM((3 * half * members, cells_y), jnp.float32)],
        compiler_params=params,
        name="outer",
    )(*own, far, turned_fy, edges, early, fx, other_fm)
    got = exchange(sent, devices)
    lows = rm // 2
    high = 3 * shares * lows * SUBLANES // LANES
    sent = pl.pallas_call(
        functools.partial(project_kernel, n_gx, rows, rm),
        out_shape=jax.ShapeDtypeStruct((devices * high, LANES), jnp.float32),
        scratch_shapes=[pltpu.VMEM((3, rx, LANES), jnp.float32)],
        compiler_params=params,
        name="project",
    )(got, own_fm, other_fm)
    got = exchange(sent, devices)
    core = pl.pallas_call(
        functools.partial(gather_kernel, shares, lows),
        out_shape=shape(lows, 3, SUBLANES, LANES),
        out_specs=anywhere,
        scratch_shapes=[
            pltpu.VMEM((3, lows, SUBLANES, LANES), jnp.float32),
            pltpu.SemaphoreType.DMA((3,)),
        ],
        compiler_params=params,
        name="gather",
    )(got)
    return core


def solution(mesh):
    return jax.shard_map(
        on_device,
        mesh=mesh,
        in_specs=(
            P("mem", "gx", None),
            P("mem", None, "gx", None),
            P(None, "gx", None),
            P("gx", None),
            P(),
            P("mem", None),
        ),
        out_specs=P("mem", None, "gx", None),
        check_vma=False,
    )
```

```python
import functools

import jax
import jax.numpy as jnp
from jax import lax
from jax.experimental import pallas as pl
from jax.experimental.pallas import tpu as pltpu
from jax.sharding import PartitionSpec as P

STEPS = 2


STIFF = 1.0
RELAX = 1.0
DTIME = 0.2

HIGHEST = lax.Precision.HIGHEST
HIGH = lax.Precision.HIGH
LANES = 128
SUBLANES = 8


def with_halo(cells, sides, width):
    for axis, dim in sides:
        count = lax.axis_size(axis)
        head = lax.slice_in_dim(cells, 0, width, axis=dim)
        tail = lax.slice_in_dim(cells, cells.shape[dim] - width, cells.shape[dim], axis=dim)
        cells = jnp.concatenate(
            [
                lax.ppermute(tail, axis, [(i, (i + 1) % count) for i in range(count)]),
                cells,
                lax.ppermute(head, axis, [((i + 1) % count, i) for i in range(count)]),
            ],
            axis=dim,
        )
    return cells


def tendency(fields, desired):
    density = fields[:, 0]
    moment_x = fields[:, 1]
    moment_y = fields[:, 2]
    speed_x = moment_x / density
    speed_y = moment_y / density
    sound = jnp.sqrt(STIFF * density)
    pressure = 0.5 * STIFF * density * density
    conserved = (density, moment_x, moment_y)
    fluxes_x = (moment_x, moment_x * speed_x + pressure, moment_y * speed_x)
    fluxes_y = (moment_y, moment_x * speed_y, moment_y * speed_y + pressure)
    reach_x = jnp.abs(speed_x) + sound
    bound_x = jnp.maximum(reach_x[:, :-1], reach_x[:, 1:])
    reach_y = (jnp.abs(speed_y) + sound)[:, 1:-1]
    bound_y = jnp.maximum(reach_y, jnp.roll(reach_y, -1, axis=-1))
    changes = []
    for quantity, normal_flux, cross_flux in zip(conserved, fluxes_x, fluxes_y):
        face_x = 0.5 * (normal_flux[:, :-1] + normal_flux[:, 1:]) - 0.5 * bound_x * (
            quantity[:, 1:] - quantity[:, :-1]
        )
        middle = quantity[:, 1:-1]
        cross_mid = cross_flux[:, 1:-1]
        face_y = 0.5 * (cross_mid + jnp.roll(cross_mid, -1, axis=-1)) - 0.5 * bound_y * (
            jnp.roll(middle, -1, axis=-1) - middle
        )
        changes.append(-(face_x[:, 1:] - face_x[:, :-1]) - (face_y - jnp.roll(face_y, 1, axis=-1)))
    centre = density[:, 1:-1]
    changes[1] = changes[1] + (centre * desired[0] - moment_x[:, 1:-1]) / RELAX
    changes[2] = changes[2] + (centre * desired[1] - moment_y[:, 1:-1]) / RELAX
    return jnp.stack(changes, axis=1)


def single_rims(fields):
    return with_halo(fields, (("gx", 2),), 1)


def plain(density, momenta, desired, factor_x, factor_y, factor_m):
    fields = jnp.concatenate([density[:, None], momenta], axis=1)
    for repeat in range(STEPS):
        sectioned = fields + DTIME * tendency(single_rims(fields), desired)
        second = sectioned + DTIME * tendency(single_rims(sectioned), desired)
        fields = 0.5 * fields + 0.5 * second
    along_y = jnp.einsum("mcxy,yb->mcxb", fields, factor_y, precision=HIGHEST)
    spread = lax.all_to_all(along_y, "gx", split_axis=3, concat_axis=2, tiled=True)
    projected = jnp.einsum(
        "mcxb,xa->mcab",
        spread,
        lax.all_gather(factor_x, "gx", axis=0, tiled=True),
        precision=HIGHEST,
    )
    returned = lax.all_to_all(projected, "gx", split_axis=2, concat_axis=3, tiled=True)
    member_terms = jnp.einsum("mcab,mk->kcab", returned, factor_m, precision=HIGHEST)
    return lax.psum_scatter(member_terms, "mem", scatter_dimension=0, tiled=True)


def cell_terms(q):
    rho, mx, my = q
    root = lax.rsqrt(rho)
    inverse = root * root
    sound = rho * root
    u = mx * inverse
    v = my * inverse
    pressure = (0.5 * STIFF) * (rho * rho)
    cross = my * u
    return dict(
        q=q,
        f=(mx, mx * u + pressure, cross),
        g=(my, cross, my * v + pressure),
        ax=jnp.abs(u) + sound,
        ay=jnp.abs(v) + sound,
    )


def x_face(low, high):
    bound = jnp.maximum(low["ax"], high["ax"])
    return tuple(
        fa + fb - bound * (b - a)
        for fa, fb, a, b in zip(low["f"], high["f"], low["q"], high["q"])
    )


def y_difference(row):
    axis = row["ay"].ndim - 1
    size = row["ay"].shape[axis]
    q = tuple(pltpu.roll(a, size - 1, axis) for a in row["q"])
    ahead = cell_terms(q)
    bound = jnp.maximum(row["ay"], ahead["ay"])
    face = tuple(
        ga + gb - bound * (b - a) for ga, gb, a, b in zip(row["g"], ahead["g"], row["q"], q)
    )
    return tuple(a - pltpu.roll(a, 1, axis) for a in face)


def section(row, low_face, high_face, wish):
    cross = y_difference(row)
    rho, mx, my = row["q"]
    half = 0.5 * DTIME
    spread = tuple(h + d for h, d in zip(high_face, cross))
    if low_face is not None:
        spread = tuple(a - l for a, l in zip(spread, low_face))
    keep = 1.0 - DTIME / RELAX
    return (
        rho - half * spread[0],
        keep * mx + rho * wish[0] - half * spread[1],
        keep * my + rho * wish[1] - half * spread[2],
    )


def half_copies(arrays, targets, odd, upper, sems):
    kinds = []
    for low in range(2):
        copies = []
        for t, target in enumerate(targets):
            base = 0
            for whole in arrays:
                lines, rows = whole.shape[:2]
                source = whole.at[:, pl.ds(low * (rows // 2), rows // 2), pl.ds(t * LANES, LANES)]
                copies.append((source, target.at[pl.ds(base, lines)]))
                base += lines
        kinds.append([
            pltpu.make_async_copy(source, target, sems.at[i])
            for i, (source, target) in enumerate(copies)
        ])
    for kind in range(2):

        @pl.when(odd == kind)
        def _():
            for copy in kinds[kind if upper else 1 - kind]:
                copy.start()

    return kinds[0]


def far_kernel(d, m, w, far, sems):
    odd = lax.rem(lax.axis_index("gx"), 2)
    targets = [far.at[t] for t in range(far.shape[0])]
    for copy in half_copies((d, m, w), targets, odd, 1, sems):
        copy.wait()


def own_kernel(d, m, w, fy, fx, far, own_d, own_m, own_w, own_fy, own_fx, near, half_sems, sems):
    tiles = own_d.shape[0]
    odd = lax.rem(lax.axis_index("gx"), 2)
    copies = half_copies((d, m, w), near, odd, 0, half_sems)
    wholes = []
    for whole, cut in ((d, own_d), (m, own_m), (w, own_w)):
        for t in range(tiles):
            wholes.append((whole.at[:, :, pl.ds(t * LANES, LANES)], cut.at[t]))
    wholes += [(fy, own_fy), (fx, own_fx)]
    wholes = [
        pltpu.make_async_copy(source, target, sems.at[i])
        for i, (source, target) in enumerate(wholes)
    ]
    for copy in wholes:
        copy.start()
    for copy in copies + wholes:
        copy.wait()


class Strip:
    def __init__(self, group, own, near, far):
        self.rows = own[2].shape[1] // 2
        self.half = self.rows // 2
        self.members = own[0].shape[1] // self.rows
        self.tiles = own[0].shape[0]
        cut = lambda ref: [ref.at[t] for t in range(self.tiles)]
        self.first, self.own = pl.multiple_of(group * SUBLANES, SUBLANES), tuple(cut(a) for a in own)
        self.near = near
        self.far = None if far is None else cut(far)
        self.odd = lax.rem(lax.axis_index("gx"), 2)
        self.sign = (1 - 2 * self.odd).astype(jnp.float32)

    def every(self, ref, first, count, stride):
        parts = [ref[t][pl.ds(first, count, stride=stride), :] for t in range(self.tiles)]
        return jnp.concatenate(parts, axis=1)

    def place(self, x):
        if x < self.half:
            ref, at, lines = self.far, x, self.half
        elif x < self.half + self.rows:
            ref, at, lines = self.own, x - self.half, self.rows
        else:
            ref, at, lines = self.near, x - self.half - self.rows, self.half
        return ref, self.odd * (lines - 1) + (1 - 2 * self.odd) * at, lines

    def load(self, x):
        ref, at, lines = self.place(x)
        if ref is self.own:
            d, m = ref[0], ref[1]
            base = 0
        else:
            d = m = ref
            base = self.members * lines
        first = self.first
        rho = self.every(d, first * lines + at, SUBLANES, lines)
        mx = self.every(m, base + first * 2 * lines + at, SUBLANES, 2 * lines)
        my = self.every(m, base + (first * 2 + 1) * lines + at, SUBLANES, 2 * lines)
        return rho, self.sign * mx, my

    def wish(self, x):
        ref, at, lines = self.place(x)
        if ref is self.own:
            ref, base = ref[2], 0
        else:
            base = 3 * self.members * lines
        line = [self.every(ref, base + c * lines + at, 1, 1) for c in range(2)]
        rate = DTIME / RELAX
        line = [(rate * self.sign) * line[0], rate * line[1]]
        return tuple(jnp.broadcast_to(a, (SUBLANES, a.shape[1])) for a in line)

    def keep(self, state, x, q):
        for c, a in enumerate((q[0], self.sign * q[1], q[2])):
            at = (3 * x + c) * self.members + self.first
            state[pl.ds(at, SUBLANES), :] = a


def march(computed, fetch, wish, emit, hook=None, bound=None):
    sections = len(computed) - 1
    known, terms, faces = {}, {}, {}

    def value(s, x):
        if (s, x) not in known:
            if x not in computed[s]:
                new = fetch(s, x)
            elif bound is not None and x == computed[s][-1]:
                share = 0.5 * DTIME * (0.5 if s % 2 == 0 else 1.0)
                new = tuple(
                    a + share * b for a, b in zip(bound(s - 1, x)["next"], face(s - 1, x - 1))
                )
            else:
                new = advanced(s, x, face(s - 1, x - 1))
            if x in computed[s]:
                emit(s, x, new)
            known[s, x] = new
        return known[s, x]

    def advanced(s, x, low):
        new = section(cell(s - 1, x), low, face(s - 1, x), wish(x))
        if s % 2 == 0:
            new = tuple(0.5 * (a + b) for a, b in zip(value(s - 2, x), new))
        return new

    def cell(s, x):
        if (s, x) not in terms:
            if bound is not None and x == computed[s + 1][-1]:
                terms[s, x] = bound(s, x)
            else:
                terms[s, x] = cell_terms(value(s, x))
        return terms[s, x]

    def face(s, x):
        if (s, x) not in faces:
            faces[s, x] = x_face(cell(s, x), cell(s, x + 1))
        return faces[s, x]

    for t in range(computed[1][0], computed[-1][-1] + sections + 1):
        for s in range(1, sections + 1):
            if t - s in computed[s]:
                value(s, t - s)
        if hook is not None:
            for s in range(sections):
                hook(s, t - s - 1, cell, advanced)


def edge_line(s, members):
    return s * 9 * members


def deal_columns(state, turned_fy, devices, members, lines):
    turned = lax.dot_general(
        turned_fy,
        state[...],
        (((1,), (1,)), ((), ())),
        precision=HIGH,
        preferred_element_type=jnp.float32,
    )
    shares = turned_fy.shape[0] // devices
    firsts, thirds = [], []
    for x in range(lines):
        at = 3 * x * members
        cut = lambda low, high: jnp.concatenate(
            [
                turned[r * devices : (r + 1) * devices, at + low : at + high]
                for r in range(shares)
            ],
            axis=1,
        )
        firsts.append(cut(0, 2 * members))
        thirds.append(cut(2 * members, 3 * members))
    return firsts, thirds


def member_kernel(near, fm, out):
    out[...] = jnp.concatenate([fm[...]] * (LANES // fm.shape[1]), axis=1)


def inner_kernel(own_d, own_m, own_w, fy, *rest):
    *near, edges, early, fy_out, state = rest
    rows = own_w.shape[1] // 2
    half = rows // 2
    members = own_d.shape[1] // rows
    sections = 2 * STEPS
    count = 2 * rows

    @pl.loop(0, members // SUBLANES)
    def _(group):
        strip = Strip(group, (own_d, own_m, own_w), near, None)

        def emit(s, x, q):
            if s == sections:
                strip.keep(state, x - rows, q)

        def hook(s, x, cell, advanced):
            if x == half + s:
                row = cell(s, x)
                arrays = (*row["q"], *row["f"][1:], row["ax"], *advanced(s + 1, x, None))
                for c, a in enumerate(arrays):
                    at = edge_line(s, members) + c * members + strip.first
                    edges[pl.ds(at, SUBLANES), :] = a

        computed = [range(0)] + [range(half + s, count - s) for s in range(1, sections + 1)]
        march(computed, lambda s, x: strip.load(x), strip.wish, emit, hook)

    devices = early.shape[0] // (2 * half)
    fy_out[...] = fy[...].T
    firsts, thirds = deal_columns(state, fy_out[...], devices, members, half)
    for i in range(half):
        early[pl.ds(i * devices, devices), :] = firsts[i]
        early[pl.ds((half + i) * devices, devices), :] = jnp.concatenate([thirds[i]] * 2, axis=1)


def outer_kernel(
    n_gx, own_d, own_m, own_w, far, fy, edges, early, fx, other_fm, out, state
):
    rows = own_w.shape[1] // 2
    half = rows // 2
    members = own_d.shape[1] // rows
    sections = 2 * STEPS
    for group in range(members // SUBLANES):
        strip = Strip(group, (own_d, own_m, own_w), None, far)

        @functools.cache
        def bound(s, x):
            at = edge_line(s, members) + strip.first
            a = [edges[pl.ds(at + c * members, SUBLANES), :] for c in range(9)]
            return dict(q=tuple(a[:3]), f=(a[1], a[3], a[4]), ax=a[5], next=tuple(a[6:]))

        def fetch(s, x):
            return strip.load(x) if x < half else bound(s, x)["q"]

        def emit(s, x, q):
            if s == sections:
                strip.keep(state, x - half, q)

        computed = [range(0)] + [range(s, half + s) for s in range(1, sections + 1)]
        march(computed, fetch, strip.wish, emit, bound=bound)

    devices = 2 * n_gx
    height = out.shape[0] // devices
    firsts, thirds = deal_columns(state, fy[...], devices, members, half)
    middle = LANES // 2
    for i in range(half):
        out[pl.ds(i, devices, stride=height), :] = firsts[i]
        out[pl.ds(half + i, devices, stride=height), :] = early[pl.ds(i * devices, devices), :]
        other = early[pl.ds((half + i) * devices, devices), :]
        out[pl.ds(rows + i, devices, stride=height), :] = jnp.concatenate(
            [thirds[i], other[:, middle:]], axis=1
        )
    mem = lax.axis_index("mem")
    for r in range(half):
        line = fx[pl.ds(mem * half + r, 1), :]
        out[pl.ds(rows + half + r, devices, stride=height), :] = jnp.broadcast_to(
            line, (devices, line.shape[1])
        )


def project_kernel(n_gx, rows, rm, inp, own_fm, other_fm, out, tall):
    devices = 2 * n_gx
    members = n_gx
    height = inp.shape[0] // devices
    half = rows // 2
    middle = LANES // 2
    low_rank = rm // 2
    line = lambda j: inp[pl.ds(j, devices, stride=height), :]
    swap = lambda a: pltpu.roll(a, middle, 1)
    lane = lax.broadcasted_iota(jnp.int32, (members, LANES), 1)
    firsts = [line(x) for x in range(rows)]
    firsts = jnp.concatenate(
        [
            jnp.concatenate([a[mem * n_gx : (mem + 1) * n_gx] for a in firsts], axis=0)
            for mem in range(2)
        ],
        axis=1,
    )
    thirds = [line(rows + i) for i in range(half)]
    pairs = [(a[:n_gx], a[n_gx:]) for a in thirds]
    thirds = jnp.concatenate(
        [jnp.where(lane < middle, a, swap(b)) for a, b in pairs]
        + [jnp.where(lane < middle, swap(a), b) for a, b in pairs],
        axis=0,
    )
    first = lax.axis_index("mem") == 0
    a, b = own_fm[...], other_fm[...]
    fm = jnp.concatenate([jnp.where(first, a, b), jnp.where(first, b, a)], axis=0)
    wide = lax.broadcasted_iota(jnp.int32, fm.shape, 1)
    first_half = wide % rm < low_rank
    repeated = (
        jnp.where(first_half, fm, pltpu.roll(fm, low_rank, 1)),
        jnp.where(first_half, pltpu.roll(fm, LANES - low_rank, 1), fm),
    )
    block = lane // low_rank
    part = lambda k, mem: repeated[k][mem * members : (mem + 1) * members]
    count = LANES // members
    diagonal = jnp.concatenate(
        [
            jnp.concatenate(
                [jnp.where(block == p, part(k, mem), 0.0) for mem in range(2) for p in range(count)],
                axis=0,
            )
            for k in range(2)
        ],
        axis=1,
    )
    small = jnp.concatenate(
        [
            jnp.where(
                block == p,
                part(0, mem),
                jnp.where(block == count // 2 + p, part(1, mem), 0.0),
            )
            for mem in range(2)
            for p in range(count // 2)
        ],
        axis=0,
    )
    product = functools.partial(jnp.dot, precision=HIGH, preferred_element_type=jnp.float32)
    halves = [line(rows + half + r) for r in range(half)]
    lines = [a[:n_gx] for a in halves] + [a[n_gx:] for a in halves]
    odd = lax.broadcasted_iota(jnp.int32, (n_gx, LANES), 0) % 2 == 1
    lines = [jnp.where(odd, lines[rows - 1 - r], lines[r]) for r in range(rows)]
    fx = jnp.concatenate(lines, axis=0)
    turned_fx = fx.T
    firsts = product(product(turned_fx, firsts), diagonal)
    thirds = product(product(turned_fx, thirds), small)
    core = jnp.concatenate([firsts[:, :LANES], thirds, firsts[:, LANES:]], axis=1)
    high = out.shape[0] // devices
    for t in range(3):
        tall[t] = core[:, t * LANES : (t + 1) * LANES]
    lane = lax.broadcasted_iota(jnp.int32, (n_gx, LANES), 1)
    for a in range(SUBLANES):
        for k in range(2):
            out[pl.ds(k * n_gx * high + a, n_gx, stride=high), :] = tall[
                2 * k, pl.ds(a, n_gx, stride=SUBLANES), :
            ]
    for i in range(SUBLANES // 2):
        upper = tall[1, pl.ds(i, n_gx, stride=SUBLANES), :]
        lower = tall[1, pl.ds(i + SUBLANES // 2, n_gx, stride=SUBLANES), :]
        first = jnp.where(lane < LANES // 2, upper, pltpu.roll(lower, LANES // 2, 1))
        second = jnp.where(lane < LANES // 2, pltpu.roll(upper, LANES // 2, 1), lower)
        out[pl.ds(SUBLANES + i, n_gx, stride=high), :] = first
        out[pl.ds(n_gx * high + SUBLANES + i, n_gx, stride=high), :] = second


def gather_kernel(shares, lows, inp, core, out, sems):
    devices = LANES // shares
    high = inp.shape[0] // devices
    quarter = SUBLANES // 2

    def turn(first):
        return jnp.concatenate(
            [inp[pl.ds(first + i, devices, stride=high), :] for i in range(quarter)], axis=0
        ).T

    def place(turned, base, apart, c, a0):
        for i in range(quarter):
            line = jnp.concatenate(
                [
                    turned[base + r * apart : base + r * apart + lows, i * devices : (i + 1) * devices]
                    for r in range(shares)
                ],
                axis=1,
            )
            out[c, :, a0 + i, :] = line

    def send(c):
        return pltpu.make_async_copy(out.at[c], core.at[:, c], sems.at[c])

    turned = [turn(h * quarter) for h in range(2)]
    for c in range(2):
        for h in range(2):
            place(turned[h], c * lows, 2 * lows, c, h * quarter)
        send(c).start()
    turned = turn(SUBLANES)
    for h in range(2):
        place(turned, h * shares * lows, lows, 2, h * quarter)
    send(2).start()
    for c in range(3):
        send(c).wait()


def exchange(chunks, devices):
    block = chunks.reshape(devices, chunks.shape[0] // devices, 1, chunks.shape[1])
    moved = lax.all_to_all(block, ("mem", "gx"), split_axis=0, concat_axis=0, tiled=True)
    return moved.reshape(chunks.shape)


def laid_out(density, factor_x, factor_y, factor_m):
    members, rows, cells_y = density.shape
    n_mem, n_gx = lax.axis_size("mem"), lax.axis_size("gx")
    rx, ry, rm = factor_x.shape[1], factor_y.shape[1], factor_m.shape[1]
    shares = ry // (n_mem * n_gx)
    return (
        n_mem == 2
        and rows == 4 * STEPS == SUBLANES
        and members == n_gx
        and n_gx % 2 == 0
        and members * rows == LANES
        and members % SUBLANES == 0
        and cells_y % LANES == 0
        and rx == LANES == n_gx * SUBLANES
        and ry == LANES == shares * n_mem * n_gx
        and shares * rm == LANES
        and shares * rm // 2 * 2 == LANES
        and 2 * shares * members == LANES
        and 2 * members == rm
    )


def on_device(density, momenta, desired, factor_x, factor_y, factor_m):
    if not laid_out(density, factor_x, factor_y, factor_m):
        return plain(density, momenta, desired, factor_x, factor_y, factor_m)
    members, rows, cells_y = density.shape
    n_gx = lax.axis_size("gx")
    devices = 2 * n_gx
    rx, ry, rm = factor_x.shape[1], factor_y.shape[1], factor_m.shape[1]
    shares = ry // devices
    params = pltpu.CompilerParams(vmem_limit_bytes=32 * 1024 * 1024)
    vmem = pl.BlockSpec(memory_space=pltpu.VMEM)
    anywhere = pl.BlockSpec(memory_space=pl.ANY)
    tiles = cells_y // LANES
    half = rows // 2
    shape = lambda *dims: jax.ShapeDtypeStruct(dims, jnp.float32)
    held = lambda *arrays: [pltpu.with_memory_space_constraint(a, pltpu.HBM) for a in arrays]
    own = [a.reshape(-1, rows, cells_y) for a in (density, momenta, desired)]
    lines = [a.shape[0] for a in own]
    packed = (sum(lines), half, LANES)
    far = pl.pallas_call(
        far_kernel,
        out_shape=shape(tiles, *packed),
        in_specs=[anywhere] * 3,
        out_specs=vmem,
        scratch_shapes=[pltpu.SemaphoreType.DMA((3 * tiles,))],
        compiler_params=params,
        name="far",
    )(*held(*own))
    *own, fy, fx, near = pl.pallas_call(
        own_kernel,
        out_shape=[shape(tiles, n, rows, LANES) for n in lines]
        + [shape(*factor_y.shape), shape(*factor_x.shape), [shape(*packed)] * tiles],
        in_specs=[anywhere] * 6,
        out_specs=[vmem] * 5 + [[vmem] * tiles],
        scratch_shapes=[
            pltpu.SemaphoreType.DMA((3 * tiles,)),
            pltpu.SemaphoreType.DMA((3 * tiles + 2,)),
        ],
        compiler_params=params,
        name="own",
    )(*held(*own, factor_y, factor_x), far)
    own = [a.reshape(tiles, -1, LANES) for a in own]
    far = far.reshape(tiles, -1, LANES)
    near = [a.reshape(-1, LANES) for a in near]
    far = lax.ppermute(far, "gx", [(i, (i - 1 + i % 2 * 2) % n_gx) for i in range(n_gx)])
    near = [lax.ppermute(a, "gx", [(i, i ^ 1) for i in range(n_gx)]) for a in near]
    own_fm = pl.pallas_call(
        member_kernel,
        out_shape=shape(members, LANES),
        in_specs=[anywhere, vmem],
        out_specs=vmem,
        compiler_params=params,
        name="member",
    )(near[-1], factor_m)
    other_fm = lax.ppermute(own_fm, "mem", [(0, 1), (1, 0)])
    sections = 2 * STEPS
    edges, early, turned_fy = pl.pallas_call(
        inner_kernel,
        out_shape=[
            shape(sections * 9 * members, cells_y),
            shape(2 * half * devices, LANES),
            shape(ry, cells_y),
        ],
        scratch_shapes=[pltpu.VMEM((3 * half * members, cells_y), jnp.float32)],
        compiler_params=params,
        name="inner",
    )(*own, fy, *near)
    height = rows + 2 * half
    sent = pl.pallas_call(
        functools.partial(outer_kernel, n_gx),
        out_shape=shape(devices * height, LANES),
        in_specs=[vmem] * 8 + [anywhere],
        out_specs=vmem,
        scratch_shapes=[pltpu.VMEM((3 * half * members, cells_y), jnp.float32)],
        compiler_params=params,
        name="outer",
    )(*own, far, turned_fy, edges, early, fx, other_fm)
    got = exchange(sent, devices)
    lows = rm // 2
    high = 3 * shares * lows * SUBLANES // LANES
    sent = pl.pallas_call(
        functools.partial(project_kernel, n_gx, rows, rm),
        out_shape=jax.ShapeDtypeStruct((devices * high, LANES), jnp.float32),
        scratch_shapes=[pltpu.VMEM((3, rx, LANES), jnp.float32)],
        compiler_params=params,
        name="project",
    )(got, own_fm, other_fm)
    got = exchange(sent, devices)
    core = pl.pallas_call(
        functools.partial(gather_kernel, shares, lows),
        out_shape=shape(lows, 3, SUBLANES, LANES),
        out_specs=anywhere,
        scratch_shapes=[
            pltpu.VMEM((3, lows, SUBLANES, LANES), jnp.float32),
            pltpu.SemaphoreType.DMA((3,)),
        ],
        compiler_params=params,
        name="gather",
    )(got)
    return core


def solution(mesh):
    return jax.shard_map(
        on_device,
        mesh=mesh,
        in_specs=(
            P("mem", "gx", None),
            P("mem", None, "gx", None),
            P(None, "gx", None),
            P("gx", None),
            P(),
            P("mem", None),
        ),
        out_specs=P("mem", None, "gx", None),
        check_vma=False,
    )
```

```python
import functools

import jax
import jax.numpy as jnp
from jax import lax
from jax.experimental import pallas as pl
from jax.experimental.pallas import tpu as pltpu
from jax.sharding import PartitionSpec as P

STEPS = 2


STIFF = 1.0
RELAX = 1.0
DTIME = 0.2

HIGHEST = lax.Precision.HIGHEST
HIGH = lax.Precision.HIGH
LANES = 128
SUBLANES = 8


def with_halo(cells, sides, width):
    for axis, dim in sides:
        count = lax.axis_size(axis)
        head = lax.slice_in_dim(cells, 0, width, axis=dim)
        tail = lax.slice_in_dim(cells, cells.shape[dim] - width, cells.shape[dim], axis=dim)
        cells = jnp.concatenate(
            [
                lax.ppermute(tail, axis, [(i, (i + 1) % count) for i in range(count)]),
                cells,
                lax.ppermute(head, axis, [((i + 1) % count, i) for i in range(count)]),
            ],
            axis=dim,
        )
    return cells


def tendency(fields, desired):
    density = fields[:, 0]
    moment_x = fields[:, 1]
    moment_y = fields[:, 2]
    speed_x = moment_x / density
    speed_y = moment_y / density
    sound = jnp.sqrt(STIFF * density)
    pressure = 0.5 * STIFF * density * density
    conserved = (density, moment_x, moment_y)
    fluxes_x = (moment_x, moment_x * speed_x + pressure, moment_y * speed_x)
    fluxes_y = (moment_y, moment_x * speed_y, moment_y * speed_y + pressure)
    reach_x = jnp.abs(speed_x) + sound
    bound_x = jnp.maximum(reach_x[:, :-1], reach_x[:, 1:])
    reach_y = (jnp.abs(speed_y) + sound)[:, 1:-1]
    bound_y = jnp.maximum(reach_y, jnp.roll(reach_y, -1, axis=-1))
    changes = []
    for quantity, normal_flux, cross_flux in zip(conserved, fluxes_x, fluxes_y):
        face_x = 0.5 * (normal_flux[:, :-1] + normal_flux[:, 1:]) - 0.5 * bound_x * (
            quantity[:, 1:] - quantity[:, :-1]
        )
        middle = quantity[:, 1:-1]
        cross_mid = cross_flux[:, 1:-1]
        face_y = 0.5 * (cross_mid + jnp.roll(cross_mid, -1, axis=-1)) - 0.5 * bound_y * (
            jnp.roll(middle, -1, axis=-1) - middle
        )
        changes.append(-(face_x[:, 1:] - face_x[:, :-1]) - (face_y - jnp.roll(face_y, 1, axis=-1)))
    centre = density[:, 1:-1]
    changes[1] = changes[1] + (centre * desired[0] - moment_x[:, 1:-1]) / RELAX
    changes[2] = changes[2] + (centre * desired[1] - moment_y[:, 1:-1]) / RELAX
    return jnp.stack(changes, axis=1)


def single_rims(fields):
    return with_halo(fields, (("gx", 2),), 1)


def plain(density, momenta, desired, factor_x, factor_y, factor_m):
    fields = jnp.concatenate([density[:, None], momenta], axis=1)
    for repeat in range(STEPS):
        sectioned = fields + DTIME * tendency(single_rims(fields), desired)
        second = sectioned + DTIME * tendency(single_rims(sectioned), desired)
        fields = 0.5 * fields + 0.5 * second
    along_y = jnp.einsum("mcxy,yb->mcxb", fields, factor_y, precision=HIGHEST)
    spread = lax.all_to_all(along_y, "gx", split_axis=3, concat_axis=2, tiled=True)
    projected = jnp.einsum(
        "mcxb,xa->mcab",
        spread,
        lax.all_gather(factor_x, "gx", axis=0, tiled=True),
        precision=HIGHEST,
    )
    returned = lax.all_to_all(projected, "gx", split_axis=2, concat_axis=3, tiled=True)
    member_terms = jnp.einsum("mcab,mk->kcab", returned, factor_m, precision=HIGHEST)
    return lax.psum_scatter(member_terms, "mem", scatter_dimension=0, tiled=True)


def cell_terms(q):
    rho, mx, my = q
    root = lax.rsqrt(rho)
    inverse = root * root
    sound = rho * root
    u = mx * inverse
    v = my * inverse
    pressure = (0.5 * STIFF) * (rho * rho)
    cross = my * u
    return dict(
        q=q,
        f=(mx, mx * u + pressure, cross),
        g=(my, cross, my * v + pressure),
        ax=jnp.abs(u) + sound,
        ay=jnp.abs(v) + sound,
    )


def x_face(low, high):
    bound = jnp.maximum(low["ax"], high["ax"])
    return tuple(
        fa + fb - bound * (b - a)
        for fa, fb, a, b in zip(low["f"], high["f"], low["q"], high["q"])
    )


def y_difference(row):
    axis = row["ay"].ndim - 1
    size = row["ay"].shape[axis]
    q = tuple(pltpu.roll(a, size - 1, axis) for a in row["q"])
    ahead = cell_terms(q)
    bound = jnp.maximum(row["ay"], ahead["ay"])
    face = tuple(
        ga + gb - bound * (b - a) for ga, gb, a, b in zip(row["g"], ahead["g"], row["q"], q)
    )
    return tuple(a - pltpu.roll(a, 1, axis) for a in face)


def section(row, low_face, high_face, wish):
    cross = y_difference(row)
    rho, mx, my = row["q"]
    half = 0.5 * DTIME
    spread = tuple(h + d for h, d in zip(high_face, cross))
    if low_face is not None:
        spread = tuple(a - l for a, l in zip(spread, low_face))
    keep = 1.0 - DTIME / RELAX
    return (
        rho - half * spread[0],
        keep * mx + rho * wish[0] - half * spread[1],
        keep * my + rho * wish[1] - half * spread[2],
    )


def half_copies(arrays, targets, odd, upper, sems):
    kinds = []
    for low in range(2):
        copies = []
        for t, target in enumerate(targets):
            base = 0
            for whole in arrays:
                lines, rows = whole.shape[:2]
                source = whole.at[:, pl.ds(low * (rows // 2), rows // 2), pl.ds(t * LANES, LANES)]
                copies.append((source, target.at[pl.ds(base, lines)]))
                base += lines
        kinds.append([
            pltpu.make_async_copy(source, target, sems.at[i])
            for i, (source, target) in enumerate(copies)
        ])
    for kind in range(2):

        @pl.when(odd == kind)
        def _():
            for copy in kinds[kind if upper else 1 - kind]:
                copy.start()

    return kinds[0]


def far_kernel(d, m, w, far, sems):
    odd = lax.rem(lax.axis_index("gx"), 2)
    targets = [far.at[t] for t in range(far.shape[0])]
    for copy in half_copies((d, m, w), targets, odd, 1, sems):
        copy.wait()


def own_kernel(d, m, w, fy, fx, far, own_d, own_m, own_w, own_fy, own_fx, near, half_sems, sems):
    tiles = own_d.shape[0]
    odd = lax.rem(lax.axis_index("gx"), 2)
    copies = half_copies((d, m, w), near, odd, 0, half_sems)
    wholes = []
    for whole, cut in ((d, own_d), (m, own_m), (w, own_w)):
        for t in range(tiles):
            wholes.append((whole.at[:, :, pl.ds(t * LANES, LANES)], cut.at[t]))
    wholes += [(fy, own_fy), (fx, own_fx)]
    wholes = [
        pltpu.make_async_copy(source, target, sems.at[i])
        for i, (source, target) in enumerate(wholes)
    ]
    for copy in wholes:
        copy.start()
    for copy in copies + wholes:
        copy.wait()


class Strip:
    def __init__(self, group, own, near, far):
        self.rows = own[2].shape[1] // 2
        self.half = self.rows // 2
        self.members = own[0].shape[1] // self.rows
        self.tiles = own[0].shape[0]
        cut = lambda ref: [ref.at[t] for t in range(self.tiles)]
        self.first, self.own = pl.multiple_of(group * SUBLANES, SUBLANES), tuple(cut(a) for a in own)
        self.near = near
        self.far = None if far is None else cut(far)
        self.odd = lax.rem(lax.axis_index("gx"), 2)
        self.sign = (1 - 2 * self.odd).astype(jnp.float32)

    def every(self, ref, first, count, stride):
        parts = [ref[t][pl.ds(first, count, stride=stride), :] for t in range(self.tiles)]
        return jnp.concatenate(parts, axis=1)

    def place(self, x):
        if x < self.half:
            ref, at, lines = self.far, x, self.half
        elif x < self.half + self.rows:
            ref, at, lines = self.own, x - self.half, self.rows
        else:
            ref, at, lines = self.near, x - self.half - self.rows, self.half
        return ref, self.odd * (lines - 1) + (1 - 2 * self.odd) * at, lines

    def load(self, x):
        ref, at, lines = self.place(x)
        if ref is self.own:
            d, m = ref[0], ref[1]
            base = 0
        else:
            d = m = ref
            base = self.members * lines
        first = self.first
        rho = self.every(d, first * lines + at, SUBLANES, lines)
        mx = self.every(m, base + first * 2 * lines + at, SUBLANES, 2 * lines)
        my = self.every(m, base + (first * 2 + 1) * lines + at, SUBLANES, 2 * lines)
        return rho, self.sign * mx, my

    def wish(self, x):
        ref, at, lines = self.place(x)
        if ref is self.own:
            ref, base = ref[2], 0
        else:
            base = 3 * self.members * lines
        line = [self.every(ref, base + c * lines + at, 1, 1) for c in range(2)]
        rate = DTIME / RELAX
        line = [(rate * self.sign) * line[0], rate * line[1]]
        return tuple(jnp.broadcast_to(a, (SUBLANES, a.shape[1])) for a in line)

    def keep(self, state, x, q):
        for c, a in enumerate((q[0], self.sign * q[1], q[2])):
            at = (3 * x + c) * self.members + self.first
            state[pl.ds(at, SUBLANES), :] = a


def march(computed, fetch, wish, emit, hook=None, bound=None):
    sections = len(computed) - 1
    known, terms, faces = {}, {}, {}

    def value(s, x):
        if (s, x) not in known:
            if x not in computed[s]:
                new = fetch(s, x)
            elif bound is not None and x == computed[s][-1]:
                share = 0.5 * DTIME * (0.5 if s % 2 == 0 else 1.0)
                new = tuple(
                    a + share * b for a, b in zip(bound(s - 1, x)["next"], face(s - 1, x - 1))
                )
            else:
                new = advanced(s, x, face(s - 1, x - 1))
            if x in computed[s]:
                emit(s, x, new)
            known[s, x] = new
        return known[s, x]

    def advanced(s, x, low):
        new = section(cell(s - 1, x), low, face(s - 1, x), wish(x))
        if s % 2 == 0:
            new = tuple(0.5 * (a + b) for a, b in zip(value(s - 2, x), new))
        return new

    def cell(s, x):
        if (s, x) not in terms:
            if bound is not None and x == computed[s + 1][-1]:
                terms[s, x] = bound(s, x)
            else:
                terms[s, x] = cell_terms(value(s, x))
        return terms[s, x]

    def face(s, x):
        if (s, x) not in faces:
            faces[s, x] = x_face(cell(s, x), cell(s, x + 1))
        return faces[s, x]

    for t in range(computed[1][0], computed[-1][-1] + sections + 1):
        for s in range(1, sections + 1):
            if t - s in computed[s]:
                value(s, t - s)
        if hook is not None:
            for s in range(sections):
                hook(s, t - s - 1, cell, advanced)


def edge_line(s, members):
    return s * 9 * members


def deal_columns(state, turned_fy, devices, members, lines):
    turned = lax.dot_general(
        turned_fy,
        state[...],
        (((1,), (1,)), ((), ())),
        precision=HIGH,
        preferred_element_type=jnp.float32,
    )
    shares = turned_fy.shape[0] // devices
    firsts, thirds = [], []
    for x in range(lines):
        at = 3 * x * members
        cut = lambda low, high: jnp.concatenate(
            [
                turned[r * devices : (r + 1) * devices, at + low : at + high]
                for r in range(shares)
            ],
            axis=1,
        )
        firsts.append(cut(0, 2 * members))
        thirds.append(cut(2 * members, 3 * members))
    return firsts, thirds


def member_kernel(near, fm, out):
    out[...] = jnp.concatenate([fm[...]] * (LANES // fm.shape[1]), axis=1)


def inner_kernel(own_d, own_m, own_w, fy, *rest):
    *near, edges, early, fy_out, state = rest
    rows = own_w.shape[1] // 2
    half = rows // 2
    members = own_d.shape[1] // rows
    sections = 2 * STEPS
    count = 2 * rows

    @pl.loop(0, members // SUBLANES)
    def _(group):
        strip = Strip(group, (own_d, own_m, own_w), near, None)

        def emit(s, x, q):
            if s == sections:
                strip.keep(state, x - rows, q)

        def hook(s, x, cell, advanced):
            if x == half + s:
                row = cell(s, x)
                arrays = (*row["q"], *row["f"][1:], row["ax"], *advanced(s + 1, x, None))
                for c, a in enumerate(arrays):
                    at = edge_line(s, members) + c * members + strip.first
                    edges[pl.ds(at, SUBLANES), :] = a

        computed = [range(0)] + [range(half + s, count - s) for s in range(1, sections + 1)]
        march(computed, lambda s, x: strip.load(x), strip.wish, emit, hook)

    devices = early.shape[0] // (2 * half)
    fy_out[...] = fy[...].T
    firsts, thirds = deal_columns(state, fy_out[...], devices, members, half)
    for i in range(half):
        early[pl.ds(i * devices, devices), :] = firsts[i]
        early[pl.ds((half + i) * devices, devices), :] = jnp.concatenate([thirds[i]] * 2, axis=1)


def outer_kernel(
    n_gx, own_d, own_m, own_w, far, fy, edges, early, fx, other_fm, out, state
):
    rows = own_w.shape[1] // 2
    half = rows // 2
    members = own_d.shape[1] // rows
    sections = 2 * STEPS
    for group in range(members // SUBLANES):
        strip = Strip(group, (own_d, own_m, own_w), None, far)

        @functools.cache
        def bound(s, x):
            at = edge_line(s, members) + strip.first
            a = [edges[pl.ds(at + c * members, SUBLANES), :] for c in range(9)]
            return dict(q=tuple(a[:3]), f=(a[1], a[3], a[4]), ax=a[5], next=tuple(a[6:]))

        def fetch(s, x):
            return strip.load(x) if x < half else bound(s, x)["q"]

        def emit(s, x, q):
            if s == sections:
                strip.keep(state, x - half, q)

        computed = [range(0)] + [range(s, half + s) for s in range(1, sections + 1)]
        march(computed, fetch, strip.wish, emit, bound=bound)

    devices = 2 * n_gx
    height = out.shape[0] // devices
    firsts, thirds = deal_columns(state, fy[...], devices, members, half)
    middle = LANES // 2
    for i in range(half):
        out[pl.ds(i, devices, stride=height), :] = firsts[i]
        out[pl.ds(half + i, devices, stride=height), :] = early[pl.ds(i * devices, devices), :]
        other = early[pl.ds((half + i) * devices, devices), :]
        out[pl.ds(rows + i, devices, stride=height), :] = jnp.concatenate(
            [thirds[i], other[:, middle:]], axis=1
        )
    mem = lax.axis_index("mem")
    for r in range(half):
        line = fx[pl.ds(mem * half + r, 1), :]
        out[pl.ds(rows + half + r, devices, stride=height), :] = jnp.broadcast_to(
            line, (devices, line.shape[1])
        )


def project_kernel(n_gx, rows, rm, inp, own_fm, other_fm, out, tall):
    devices = 2 * n_gx
    members = n_gx
    height = inp.shape[0] // devices
    half = rows // 2
    middle = LANES // 2
    low_rank = rm // 2
    line = lambda j: inp[pl.ds(j, devices, stride=height), :]
    swap = lambda a: pltpu.roll(a, middle, 1)
    lane = lax.broadcasted_iota(jnp.int32, (members, LANES), 1)
    firsts = [line(x) for x in range(rows)]
    firsts = jnp.concatenate(
        [
            jnp.concatenate([a[mem * n_gx : (mem + 1) * n_gx] for a in firsts], axis=0)
            for mem in range(2)
        ],
        axis=1,
    )
    thirds = [line(rows + i) for i in range(half)]
    pairs = [(a[:n_gx], a[n_gx:]) for a in thirds]
    thirds = jnp.concatenate(
        [jnp.where(lane < middle, a, swap(b)) for a, b in pairs]
        + [jnp.where(lane < middle, swap(a), b) for a, b in pairs],
        axis=0,
    )
    first = lax.axis_index("mem") == 0
    a, b = own_fm[...], other_fm[...]
    fm = jnp.concatenate([jnp.where(first, a, b), jnp.where(first, b, a)], axis=0)
    wide = lax.broadcasted_iota(jnp.int32, fm.shape, 1)
    first_half = wide % rm < low_rank
    repeated = (
        jnp.where(first_half, fm, pltpu.roll(fm, low_rank, 1)),
        jnp.where(first_half, pltpu.roll(fm, LANES - low_rank, 1), fm),
    )
    block = lane // low_rank
    part = lambda k, mem: repeated[k][mem * members : (mem + 1) * members]
    count = LANES // members
    diagonal = jnp.concatenate(
        [
            jnp.concatenate(
                [jnp.where(block == p, part(k, mem), 0.0) for mem in range(2) for p in range(count)],
                axis=0,
            )
            for k in range(2)
        ],
        axis=1,
    )
    small = jnp.concatenate(
        [
            jnp.where(
                block == p,
                part(0, mem),
                jnp.where(block == count // 2 + p, part(1, mem), 0.0),
            )
            for mem in range(2)
            for p in range(count // 2)
        ],
        axis=0,
    )
    product = functools.partial(jnp.dot, precision=HIGH, preferred_element_type=jnp.float32)
    halves = [line(rows + half + r) for r in range(half)]
    lines = [a[:n_gx] for a in halves] + [a[n_gx:] for a in halves]
    odd = lax.broadcasted_iota(jnp.int32, (n_gx, LANES), 0) >= n_gx // 2
    lines = [jnp.where(odd, lines[rows - 1 - r], lines[r]) for r in range(rows)]
    fx = jnp.concatenate(lines, axis=0)
    turned_fx = fx.T
    firsts = product(product(turned_fx, firsts), diagonal)
    thirds = product(product(turned_fx, thirds), small)
    core = jnp.concatenate([firsts[:, :LANES], thirds, firsts[:, LANES:]], axis=1)
    high = out.shape[0] // devices
    for t in range(3):
        tall[t] = core[:, t * LANES : (t + 1) * LANES]
    pairs = n_gx // 2
    lane = lax.broadcasted_iota(jnp.int32, (pairs, LANES), 1)
    for odd in range(2):
        share = lambda t, a: tall[t, pl.ds(odd * SUBLANES + a, pairs, stride=2 * SUBLANES), :]
        spot = lambda k, i: pl.ds((k * n_gx + odd * pairs) * high + i, pairs, stride=high)
        for a in range(SUBLANES):
            for k in range(2):
                out[spot(k, a), :] = share(2 * k, a)
        for i in range(SUBLANES // 2):
            upper = share(1, i)
            lower = share(1, i + SUBLANES // 2)
            first = jnp.where(lane < middle, upper, swap(lower))
            second = jnp.where(lane < middle, swap(upper), lower)
            out[spot(0, SUBLANES + i), :] = first
            out[spot(1, SUBLANES + i), :] = second


def gather_kernel(shares, lows, inp, core, out, sems):
    devices = LANES // shares
    high = inp.shape[0] // devices
    quarter = SUBLANES // 2

    def turn(first):
        return jnp.concatenate(
            [inp[pl.ds(first + i, devices, stride=high), :] for i in range(quarter)], axis=0
        ).T

    def place(turned, base, apart, c, a0):
        for i in range(quarter):
            line = jnp.concatenate(
                [
                    turned[base + r * apart : base + r * apart + lows, i * devices : (i + 1) * devices]
                    for r in range(shares)
                ],
                axis=1,
            )
            out[c, :, a0 + i, :] = line

    def send(c):
        return pltpu.make_async_copy(out.at[c], core.at[:, c], sems.at[c])

    turned = [turn(h * quarter) for h in range(2)]
    for c in range(2):
        for h in range(2):
            place(turned[h], c * lows, 2 * lows, c, h * quarter)
        send(c).start()
    turned = turn(SUBLANES)
    for h in range(2):
        place(turned, h * shares * lows, lows, 2, h * quarter)
    send(2).start()
    for c in range(3):
        send(c).wait()


def exchange(chunks, devices):
    block = chunks.reshape(devices, chunks.shape[0] // devices, 1, chunks.shape[1])
    n_gx = lax.axis_size("gx")
    order = [mem * n_gx + i for mem in range(devices // n_gx) for odd in range(2) for i in range(odd, n_gx, 2)]
    moved = lax.all_to_all(
        block, ("mem", "gx"), split_axis=0, concat_axis=0, axis_index_groups=[order], tiled=True
    )
    return moved.reshape(chunks.shape)


def laid_out(density, factor_x, factor_y, factor_m):
    members, rows, cells_y = density.shape
    n_mem, n_gx = lax.axis_size("mem"), lax.axis_size("gx")
    rx, ry, rm = factor_x.shape[1], factor_y.shape[1], factor_m.shape[1]
    shares = ry // (n_mem * n_gx)
    return (
        n_mem == 2
        and rows == 4 * STEPS == SUBLANES
        and members == n_gx
        and n_gx % 2 == 0
        and members * rows == LANES
        and members % SUBLANES == 0
        and cells_y % LANES == 0
        and rx == LANES == n_gx * SUBLANES
        and ry == LANES == shares * n_mem * n_gx
        and shares * rm == LANES
        and shares * rm // 2 * 2 == LANES
        and 2 * shares * members == LANES
        and 2 * members == rm
    )


def on_device(density, momenta, desired, factor_x, factor_y, factor_m):
    if not laid_out(density, factor_x, factor_y, factor_m):
        return plain(density, momenta, desired, factor_x, factor_y, factor_m)
    members, rows, cells_y = density.shape
    n_gx = lax.axis_size("gx")
    devices = 2 * n_gx
    rx, ry, rm = factor_x.shape[1], factor_y.shape[1], factor_m.shape[1]
    shares = ry // devices
    params = pltpu.CompilerParams(vmem_limit_bytes=32 * 1024 * 1024)
    vmem = pl.BlockSpec(memory_space=pltpu.VMEM)
    anywhere = pl.BlockSpec(memory_space=pl.ANY)
    tiles = cells_y // LANES
    half = rows // 2
    shape = lambda *dims: jax.ShapeDtypeStruct(dims, jnp.float32)
    held = lambda *arrays: [pltpu.with_memory_space_constraint(a, pltpu.HBM) for a in arrays]
    own = [a.reshape(-1, rows, cells_y) for a in (density, momenta, desired)]
    lines = [a.shape[0] for a in own]
    packed = (sum(lines), half, LANES)
    far = pl.pallas_call(
        far_kernel,
        out_shape=shape(tiles, *packed),
        in_specs=[anywhere] * 3,
        out_specs=vmem,
        scratch_shapes=[pltpu.SemaphoreType.DMA((3 * tiles,))],
        compiler_params=params,
        name="far",
    )(*held(*own))
    *own, fy, fx, near = pl.pallas_call(
        own_kernel,
        out_shape=[shape(tiles, n, rows, LANES) for n in lines]
        + [shape(*factor_y.shape), shape(*factor_x.shape), [shape(*packed)] * tiles],
        in_specs=[anywhere] * 6,
        out_specs=[vmem] * 5 + [[vmem] * tiles],
        scratch_shapes=[
            pltpu.SemaphoreType.DMA((3 * tiles,)),
            pltpu.SemaphoreType.DMA((3 * tiles + 2,)),
        ],
        compiler_params=params,
        name="own",
    )(*held(*own, factor_y, factor_x), far)
    own = [a.reshape(tiles, -1, LANES) for a in own]
    far = far.reshape(tiles, -1, LANES)
    near = [a.reshape(-1, LANES) for a in near]
    far = lax.ppermute(far, "gx", [(i, (i - 1 + i % 2 * 2) % n_gx) for i in range(n_gx)])
    near = [lax.ppermute(a, "gx", [(i, i ^ 1) for i in range(n_gx)]) for a in near]
    own_fm = pl.pallas_call(
        member_kernel,
        out_shape=shape(members, LANES),
        in_specs=[anywhere, vmem],
        out_specs=vmem,
        compiler_params=params,
        name="member",
    )(near[-1], factor_m)
    other_fm = lax.ppermute(own_fm, "mem", [(0, 1), (1, 0)])
    sections = 2 * STEPS
    edges, early, turned_fy = pl.pallas_call(
        inner_kernel,
        out_shape=[
            shape(sections * 9 * members, cells_y),
            shape(2 * half * devices, LANES),
            shape(ry, cells_y),
        ],
        scratch_shapes=[pltpu.VMEM((3 * half * members, cells_y), jnp.float32)],
        compiler_params=params,
        name="inner",
    )(*own, fy, *near)
    height = rows + 2 * half
    sent = pl.pallas_call(
        functools.partial(outer_kernel, n_gx),
        out_shape=shape(devices * height, LANES),
        in_specs=[vmem] * 8 + [anywhere],
        out_specs=vmem,
        scratch_shapes=[pltpu.VMEM((3 * half * members, cells_y), jnp.float32)],
        compiler_params=params,
        name="outer",
    )(*own, far, turned_fy, edges, early, fx, other_fm)
    got = exchange(sent, devices)
    lows = rm // 2
    high = 3 * shares * lows * SUBLANES // LANES
    sent = pl.pallas_call(
        functools.partial(project_kernel, n_gx, rows, rm),
        out_shape=jax.ShapeDtypeStruct((devices * high, LANES), jnp.float32),
        scratch_shapes=[pltpu.VMEM((3, rx, LANES), jnp.float32)],
        compiler_params=params,
        name="project",
    )(got, own_fm, other_fm)
    got = exchange(sent, devices)
    core = pl.pallas_call(
        functools.partial(gather_kernel, shares, lows),
        out_shape=shape(lows, 3, SUBLANES, LANES),
        out_specs=anywhere,
        scratch_shapes=[
            pltpu.VMEM((3, lows, SUBLANES, LANES), jnp.float32),
            pltpu.SemaphoreType.DMA((3,)),
        ],
        compiler_params=params,
        name="gather",
    )(got)
    return core


def solution(mesh):
    return jax.shard_map(
        on_device,
        mesh=mesh,
        in_specs=(
            P("mem", "gx", None),
            P("mem", None, "gx", None),
            P(None, "gx", None),
            P("gx", None),
            P(),
            P("mem", None),
        ),
        out_specs=P("mem", None, "gx", None),
        check_vma=False,
    )
```

```python
import functools

import jax
import jax.numpy as jnp
from jax import lax
from jax.experimental import pallas as pl
from jax.experimental.pallas import tpu as pltpu
from jax.sharding import PartitionSpec as P

STEPS = 2


STIFF = 1.0
RELAX = 1.0
DTIME = 0.2

HIGHEST = lax.Precision.HIGHEST
HIGH = lax.Precision.HIGH
LANES = 128
SUBLANES = 8


def with_halo(cells, sides, width):
    for axis, dim in sides:
        count = lax.axis_size(axis)
        head = lax.slice_in_dim(cells, 0, width, axis=dim)
        tail = lax.slice_in_dim(cells, cells.shape[dim] - width, cells.shape[dim], axis=dim)
        cells = jnp.concatenate(
            [
                lax.ppermute(tail, axis, [(i, (i + 1) % count) for i in range(count)]),
                cells,
                lax.ppermute(head, axis, [((i + 1) % count, i) for i in range(count)]),
            ],
            axis=dim,
        )
    return cells


def tendency(fields, desired):
    density = fields[:, 0]
    moment_x = fields[:, 1]
    moment_y = fields[:, 2]
    speed_x = moment_x / density
    speed_y = moment_y / density
    sound = jnp.sqrt(STIFF * density)
    pressure = 0.5 * STIFF * density * density
    conserved = (density, moment_x, moment_y)
    fluxes_x = (moment_x, moment_x * speed_x + pressure, moment_y * speed_x)
    fluxes_y = (moment_y, moment_x * speed_y, moment_y * speed_y + pressure)
    reach_x = jnp.abs(speed_x) + sound
    bound_x = jnp.maximum(reach_x[:, :-1], reach_x[:, 1:])
    reach_y = (jnp.abs(speed_y) + sound)[:, 1:-1]
    bound_y = jnp.maximum(reach_y, jnp.roll(reach_y, -1, axis=-1))
    changes = []
    for quantity, normal_flux, cross_flux in zip(conserved, fluxes_x, fluxes_y):
        face_x = 0.5 * (normal_flux[:, :-1] + normal_flux[:, 1:]) - 0.5 * bound_x * (
            quantity[:, 1:] - quantity[:, :-1]
        )
        middle = quantity[:, 1:-1]
        cross_mid = cross_flux[:, 1:-1]
        face_y = 0.5 * (cross_mid + jnp.roll(cross_mid, -1, axis=-1)) - 0.5 * bound_y * (
            jnp.roll(middle, -1, axis=-1) - middle
        )
        changes.append(-(face_x[:, 1:] - face_x[:, :-1]) - (face_y - jnp.roll(face_y, 1, axis=-1)))
    centre = density[:, 1:-1]
    changes[1] = changes[1] + (centre * desired[0] - moment_x[:, 1:-1]) / RELAX
    changes[2] = changes[2] + (centre * desired[1] - moment_y[:, 1:-1]) / RELAX
    return jnp.stack(changes, axis=1)


def single_rims(fields):
    return with_halo(fields, (("gx", 2),), 1)


def plain(density, momenta, desired, factor_x, factor_y, factor_m):
    fields = jnp.concatenate([density[:, None], momenta], axis=1)
    for repeat in range(STEPS):
        sectioned = fields + DTIME * tendency(single_rims(fields), desired)
        second = sectioned + DTIME * tendency(single_rims(sectioned), desired)
        fields = 0.5 * fields + 0.5 * second
    along_y = jnp.einsum("mcxy,yb->mcxb", fields, factor_y, precision=HIGHEST)
    spread = lax.all_to_all(along_y, "gx", split_axis=3, concat_axis=2, tiled=True)
    projected = jnp.einsum(
        "mcxb,xa->mcab",
        spread,
        lax.all_gather(factor_x, "gx", axis=0, tiled=True),
        precision=HIGHEST,
    )
    returned = lax.all_to_all(projected, "gx", split_axis=2, concat_axis=3, tiled=True)
    member_terms = jnp.einsum("mcab,mk->kcab", returned, factor_m, precision=HIGHEST)
    return lax.psum_scatter(member_terms, "mem", scatter_dimension=0, tiled=True)


def cell_terms(q):
    rho, mx, my = q
    root = lax.rsqrt(rho)
    inverse = root * root
    sound = rho * root
    u = mx * inverse
    v = my * inverse
    pressure = (0.5 * STIFF) * (rho * rho)
    cross = my * u
    return dict(
        q=q,
        f=(mx, mx * u + pressure, cross),
        g=(my, cross, my * v + pressure),
        ax=jnp.abs(u) + sound,
        ay=jnp.abs(v) + sound,
    )


def x_face(low, high):
    bound = jnp.maximum(low["ax"], high["ax"])
    return tuple(
        fa + fb - bound * (b - a)
        for fa, fb, a, b in zip(low["f"], high["f"], low["q"], high["q"])
    )


def y_difference(row):
    axis = row["ay"].ndim - 1
    size = row["ay"].shape[axis]
    q = tuple(pltpu.roll(a, size - 1, axis) for a in row["q"])
    ahead = cell_terms(q)
    bound = jnp.maximum(row["ay"], ahead["ay"])
    face = tuple(
        ga + gb - bound * (b - a) for ga, gb, a, b in zip(row["g"], ahead["g"], row["q"], q)
    )
    return tuple(a - pltpu.roll(a, 1, axis) for a in face)


def section(row, low_face, high_face, wish):
    cross = y_difference(row)
    rho, mx, my = row["q"]
    half = 0.5 * DTIME
    spread = tuple(h + d for h, d in zip(high_face, cross))
    if low_face is not None:
        spread = tuple(a - l for a, l in zip(spread, low_face))
    keep = 1.0 - DTIME / RELAX
    return (
        rho - half * spread[0],
        keep * mx + rho * wish[0] - half * spread[1],
        keep * my + rho * wish[1] - half * spread[2],
    )


def half_copies(arrays, targets, odd, upper, sems):
    kinds = []
    for low in range(2):
        copies = []
        for t, target in enumerate(targets):
            base = 0
            for whole in arrays:
                lines, rows = whole.shape[:2]
                source = whole.at[:, pl.ds(low * (rows // 2), rows // 2), pl.ds(t * LANES, LANES)]
                copies.append((source, target.at[pl.ds(base, lines)]))
                base += lines
        kinds.append([
            pltpu.make_async_copy(source, target, sems.at[i])
            for i, (source, target) in enumerate(copies)
        ])
    for kind in range(2):

        @pl.when(odd == kind)
        def _():
            for copy in kinds[kind if upper else 1 - kind]:
                copy.start()

    return kinds[0]


def far_kernel(d, m, w, far, sems):
    odd = lax.rem(lax.axis_index("gx"), 2)
    targets = [far.at[t] for t in range(far.shape[0])]
    for copy in half_copies((d, m, w), targets, odd, 1, sems):
        copy.wait()


def own_kernel(d, m, w, fy, fx, far, own_d, own_m, own_w, own_fy, own_fx, near, half_sems, sems):
    tiles = own_d.shape[0]
    odd = lax.rem(lax.axis_index("gx"), 2)
    copies = half_copies((d, m, w), near, odd, 0, half_sems)
    wholes = []
    for whole, cut in ((d, own_d), (m, own_m), (w, own_w)):
        for t in range(tiles):
            wholes.append((whole.at[:, :, pl.ds(t * LANES, LANES)], cut.at[t]))
    wholes += [(fy, own_fy), (fx, own_fx)]
    wholes = [
        pltpu.make_async_copy(source, target, sems.at[i])
        for i, (source, target) in enumerate(wholes)
    ]
    for copy in wholes:
        copy.start()
    for copy in copies + wholes:
        copy.wait()


class Strip:
    def __init__(self, group, own, near, far):
        self.rows = own[2].shape[1] // 2
        self.half = self.rows // 2
        self.members = own[0].shape[1] // self.rows
        self.tiles = own[0].shape[0]
        cut = lambda ref: [ref.at[t] for t in range(self.tiles)]
        self.first, self.own = pl.multiple_of(group * SUBLANES, SUBLANES), tuple(cut(a) for a in own)
        self.near = near
        self.far = None if far is None else cut(far)
        self.odd = lax.rem(lax.axis_index("gx"), 2)
        self.sign = (1 - 2 * self.odd).astype(jnp.float32)

    def every(self, ref, first, count, stride):
        parts = [ref[t][pl.ds(first, count, stride=stride), :] for t in range(self.tiles)]
        return jnp.concatenate(parts, axis=1)

    def place(self, x):
        if x < self.half:
            ref, at, lines = self.far, x, self.half
        elif x < self.half + self.rows:
            ref, at, lines = self.own, x - self.half, self.rows
        else:
            ref, at, lines = self.near, x - self.half - self.rows, self.half
        return ref, self.odd * (lines - 1) + (1 - 2 * self.odd) * at, lines

    def load(self, x):
        ref, at, lines = self.place(x)
        if ref is self.own:
            d, m = ref[0], ref[1]
            base = 0
        else:
            d = m = ref
            base = self.members * lines
        first = self.first
        rho = self.every(d, first * lines + at, SUBLANES, lines)
        mx = self.every(m, base + first * 2 * lines + at, SUBLANES, 2 * lines)
        my = self.every(m, base + (first * 2 + 1) * lines + at, SUBLANES, 2 * lines)
        return rho, self.sign * mx, my

    def wish(self, x):
        ref, at, lines = self.place(x)
        if ref is self.own:
            ref, base = ref[2], 0
        else:
            base = 3 * self.members * lines
        line = [self.every(ref, base + c * lines + at, 1, 1) for c in range(2)]
        rate = DTIME / RELAX
        line = [(rate * self.sign) * line[0], rate * line[1]]
        return tuple(jnp.broadcast_to(a, (SUBLANES, a.shape[1])) for a in line)

    def keep(self, state, x, q):
        for c, a in enumerate((q[0], self.sign * q[1], q[2])):
            at = (3 * x + c) * self.members + self.first
            state[pl.ds(at, SUBLANES), :] = a


def march(computed, fetch, wish, emit, hook=None, bound=None):
    sections = len(computed) - 1
    known, terms, faces = {}, {}, {}

    def value(s, x):
        if (s, x) not in known:
            if x not in computed[s]:
                new = fetch(s, x)
            elif bound is not None and x == computed[s][-1]:
                share = 0.5 * DTIME * (0.5 if s % 2 == 0 else 1.0)
                new = tuple(
                    a + share * b for a, b in zip(bound(s - 1, x)["next"], face(s - 1, x - 1))
                )
            else:
                new = advanced(s, x, face(s - 1, x - 1))
            if x in computed[s]:
                emit(s, x, new)
            known[s, x] = new
        return known[s, x]

    def advanced(s, x, low):
        new = section(cell(s - 1, x), low, face(s - 1, x), wish(x))
        if s % 2 == 0:
            new = tuple(0.5 * (a + b) for a, b in zip(value(s - 2, x), new))
        return new

    def cell(s, x):
        if (s, x) not in terms:
            if bound is not None and x == computed[s + 1][-1]:
                terms[s, x] = bound(s, x)
            else:
                terms[s, x] = cell_terms(value(s, x))
        return terms[s, x]

    def face(s, x):
        if (s, x) not in faces:
            faces[s, x] = x_face(cell(s, x), cell(s, x + 1))
        return faces[s, x]

    for t in range(computed[1][0], computed[-1][-1] + sections + 1):
        for s in range(1, sections + 1):
            if t - s in computed[s]:
                value(s, t - s)
        if hook is not None:
            for s in range(sections):
                hook(s, t - s - 1, cell, advanced)


def edge_line(s, members):
    return s * 9 * members


def deal_columns(state, turned_fy, devices, members, lines):
    turned = lax.dot_general(
        turned_fy,
        state[...],
        (((1,), (1,)), ((), ())),
        precision=HIGH,
        preferred_element_type=jnp.float32,
    )
    shares = turned_fy.shape[0] // devices
    firsts, thirds = [], []
    for x in range(lines):
        at = 3 * x * members
        cut = lambda low, high: jnp.concatenate(
            [
                turned[r * devices : (r + 1) * devices, at + low : at + high]
                for r in range(shares)
            ],
            axis=1,
        )
        firsts.append(cut(0, 2 * members))
        thirds.append(cut(2 * members, 3 * members))
    return firsts, thirds


def member_kernel(near, fm, out):
    out[...] = jnp.concatenate([fm[...]] * (LANES // fm.shape[1]), axis=1)


def inner_kernel(own_d, own_m, own_w, fy, *rest):
    *near, edges, early, fy_out, state = rest
    rows = own_w.shape[1] // 2
    half = rows // 2
    members = own_d.shape[1] // rows
    sections = 2 * STEPS
    count = 2 * rows

    @pl.loop(0, members // SUBLANES)
    def _(group):
        strip = Strip(group, (own_d, own_m, own_w), near, None)

        def emit(s, x, q):
            if s == sections:
                strip.keep(state, x - rows, q)

        def hook(s, x, cell, advanced):
            if x == half + s:
                row = cell(s, x)
                arrays = (*row["q"], *row["f"][1:], row["ax"], *advanced(s + 1, x, None))
                for c, a in enumerate(arrays):
                    at = edge_line(s, members) + c * members + strip.first
                    edges[pl.ds(at, SUBLANES), :] = a

        computed = [range(0)] + [range(half + s, count - s) for s in range(1, sections + 1)]
        march(computed, lambda s, x: strip.load(x), strip.wish, emit, hook)

    devices = early.shape[0] // (2 * half)
    fy_out[...] = fy[...].T
    firsts, thirds = deal_columns(state, fy_out[...], devices, members, half)
    for i in range(half):
        early[pl.ds(i * devices, devices), :] = firsts[i]
        early[pl.ds((half + i) * devices, devices), :] = jnp.concatenate([thirds[i]] * 2, axis=1)


def outer_kernel(
    n_gx, own_d, own_m, own_w, far, fy, edges, early, fx, other_fm, out, state
):
    rows = own_w.shape[1] // 2
    half = rows // 2
    members = own_d.shape[1] // rows
    sections = 2 * STEPS
    for group in range(members // SUBLANES):
        strip = Strip(group, (own_d, own_m, own_w), None, far)

        @functools.cache
        def bound(s, x):
            at = edge_line(s, members) + strip.first
            a = [edges[pl.ds(at + c * members, SUBLANES), :] for c in range(9)]
            return dict(q=tuple(a[:3]), f=(a[1], a[3], a[4]), ax=a[5], next=tuple(a[6:]))

        def fetch(s, x):
            return strip.load(x) if x < half else bound(s, x)["q"]

        def emit(s, x, q):
            if s == sections:
                strip.keep(state, x - half, q)

        computed = [range(0)] + [range(s, half + s) for s in range(1, sections + 1)]
        march(computed, fetch, strip.wish, emit, bound=bound)

    devices = 2 * n_gx
    height = out.shape[0] // devices
    firsts, thirds = deal_columns(state, fy[...], devices, members, half)
    middle = LANES // 2
    for i in range(half):
        out[pl.ds(i, devices, stride=height), :] = firsts[i]
        out[pl.ds(half + i, devices, stride=height), :] = early[pl.ds(i * devices, devices), :]
        other = early[pl.ds((half + i) * devices, devices), :]
        out[pl.ds(rows + i, devices, stride=height), :] = jnp.concatenate(
            [thirds[i], other[:, middle:]], axis=1
        )
    mem = lax.axis_index("mem")
    for r in range(half):
        line = fx[pl.ds(mem * half + r, 1), :]
        out[pl.ds(rows + half + r, devices, stride=height), :] = jnp.broadcast_to(
            line, (devices, line.shape[1])
        )


def project_kernel(n_gx, rows, rm, inp, own_fm, other_fm, out, tall):
    devices = 2 * n_gx
    members = n_gx
    height = inp.shape[0] // devices
    half = rows // 2
    middle = LANES // 2
    low_rank = rm // 2
    line = lambda j: inp[pl.ds(j, devices, stride=height), :]
    swap = lambda a: pltpu.roll(a, middle, 1)
    lane = lax.broadcasted_iota(jnp.int32, (members, LANES), 1)
    firsts = [line(x) for x in range(rows)]
    firsts = jnp.concatenate(
        [
            jnp.concatenate([a[mem * n_gx : (mem + 1) * n_gx] for a in firsts], axis=0)
            for mem in range(2)
        ],
        axis=1,
    )
    thirds = [line(rows + i) for i in range(half)]
    pairs = [(a[:n_gx], a[n_gx:]) for a in thirds]
    thirds = jnp.concatenate(
        [jnp.where(lane < middle, a, swap(b)) for a, b in pairs]
        + [jnp.where(lane < middle, swap(a), b) for a, b in pairs],
        axis=0,
    )
    first = lax.axis_index("mem") == 0
    a, b = own_fm[...], other_fm[...]
    fm = jnp.concatenate([jnp.where(first, a, b), jnp.where(first, b, a)], axis=0)
    wide = lax.broadcasted_iota(jnp.int32, fm.shape, 1)
    first_half = wide % rm < low_rank
    repeated = (
        jnp.where(first_half, fm, pltpu.roll(fm, low_rank, 1)),
        jnp.where(first_half, pltpu.roll(fm, LANES - low_rank, 1), fm),
    )
    block = lane // low_rank
    part = lambda k, mem: repeated[k][mem * members : (mem + 1) * members]
    count = LANES // members
    diagonal = jnp.concatenate(
        [
            jnp.concatenate(
                [jnp.where(block == p, part(k, mem), 0.0) for mem in range(2) for p in range(count)],
                axis=0,
            )
            for k in range(2)
        ],
        axis=1,
    )
    small = jnp.concatenate(
        [
            jnp.where(
                block == p,
                part(0, mem),
                jnp.where(block == count // 2 + p, part(1, mem), 0.0),
            )
            for mem in range(2)
            for p in range(count // 2)
        ],
        axis=0,
    )
    product = functools.partial(jnp.dot, precision=HIGH, preferred_element_type=jnp.float32)
    halves = [line(rows + half + r) for r in range(half)]
    lines = [a[:n_gx] for a in halves] + [a[n_gx:] for a in halves]
    odd = lax.broadcasted_iota(jnp.int32, (n_gx, LANES), 0) >= n_gx // 2
    lines = [jnp.where(odd, lines[rows - 1 - r], lines[r]) for r in range(rows)]
    fx = jnp.concatenate(lines, axis=0)
    turned_fx = fx.T
    both = product(turned_fx, jnp.concatenate([firsts, thirds], axis=1))
    firsts = product(both[:, : 2 * LANES], diagonal)
    thirds = product(both[:, 2 * LANES :], small)
    core = jnp.concatenate([firsts[:, :LANES], thirds, firsts[:, LANES:]], axis=1)
    high = out.shape[0] // devices
    for t in range(3):
        tall[t] = core[:, t * LANES : (t + 1) * LANES]
    pairs = n_gx // 2
    lane = lax.broadcasted_iota(jnp.int32, (pairs, LANES), 1)
    for odd in range(2):
        share = lambda t, a: tall[t, pl.ds(odd * SUBLANES + a, pairs, stride=2 * SUBLANES), :]
        spot = lambda k, i: pl.ds((k * n_gx + odd * pairs) * high + i, pairs, stride=high)
        for a in range(SUBLANES):
            for k in range(2):
                out[spot(k, a), :] = share(2 * k, a)
        for i in range(SUBLANES // 2):
            upper = share(1, i)
            lower = share(1, i + SUBLANES // 2)
            first = jnp.where(lane < middle, upper, swap(lower))
            second = jnp.where(lane < middle, swap(upper), lower)
            out[spot(0, SUBLANES + i), :] = first
            out[spot(1, SUBLANES + i), :] = second


def gather_kernel(shares, lows, inp, core, out, sems):
    devices = LANES // shares
    high = inp.shape[0] // devices
    quarter = SUBLANES // 2

    def turn(first):
        return jnp.concatenate(
            [inp[pl.ds(first + i, devices, stride=high), :] for i in range(quarter)], axis=0
        ).T

    def place(turned, base, apart, c, a0):
        for i in range(quarter):
            line = jnp.concatenate(
                [
                    turned[base + r * apart : base + r * apart + lows, i * devices : (i + 1) * devices]
                    for r in range(shares)
                ],
                axis=1,
            )
            out[c, :, a0 + i, :] = line

    def send(c):
        return pltpu.make_async_copy(out.at[c], core.at[:, c], sems.at[c])

    turned = [turn(h * quarter) for h in range(2)]
    for c in range(2):
        for h in range(2):
            place(turned[h], c * lows, 2 * lows, c, h * quarter)
        send(c).start()
    turned = turn(SUBLANES)
    for h in range(2):
        place(turned, h * shares * lows, lows, 2, h * quarter)
    send(2).start()
    for c in range(3):
        send(c).wait()


def exchange(chunks, devices):
    block = chunks.reshape(devices, chunks.shape[0] // devices, 1, chunks.shape[1])
    n_gx = lax.axis_size("gx")
    order = [mem * n_gx + i for mem in range(devices // n_gx) for odd in range(2) for i in range(odd, n_gx, 2)]
    moved = lax.all_to_all(
        block, ("mem", "gx"), split_axis=0, concat_axis=0, axis_index_groups=[order], tiled=True
    )
    return moved.reshape(chunks.shape)


def laid_out(density, factor_x, factor_y, factor_m):
    members, rows, cells_y = density.shape
    n_mem, n_gx = lax.axis_size("mem"), lax.axis_size("gx")
    rx, ry, rm = factor_x.shape[1], factor_y.shape[1], factor_m.shape[1]
    shares = ry // (n_mem * n_gx)
    return (
        n_mem == 2
        and rows == 4 * STEPS == SUBLANES
        and members == n_gx
        and n_gx % 2 == 0
        and members * rows == LANES
        and members % SUBLANES == 0
        and cells_y % LANES == 0
        and rx == LANES == n_gx * SUBLANES
        and ry == LANES == shares * n_mem * n_gx
        and shares * rm == LANES
        and shares * rm // 2 * 2 == LANES
        and 2 * shares * members == LANES
        and 2 * members == rm
    )


def on_device(density, momenta, desired, factor_x, factor_y, factor_m):
    if not laid_out(density, factor_x, factor_y, factor_m):
        return plain(density, momenta, desired, factor_x, factor_y, factor_m)
    members, rows, cells_y = density.shape
    n_gx = lax.axis_size("gx")
    devices = 2 * n_gx
    rx, ry, rm = factor_x.shape[1], factor_y.shape[1], factor_m.shape[1]
    shares = ry // devices
    params = pltpu.CompilerParams(vmem_limit_bytes=32 * 1024 * 1024)
    vmem = pl.BlockSpec(memory_space=pltpu.VMEM)
    anywhere = pl.BlockSpec(memory_space=pl.ANY)
    tiles = cells_y // LANES
    half = rows // 2
    shape = lambda *dims: jax.ShapeDtypeStruct(dims, jnp.float32)
    held = lambda *arrays: [pltpu.with_memory_space_constraint(a, pltpu.HBM) for a in arrays]
    own = [a.reshape(-1, rows, cells_y) for a in (density, momenta, desired)]
    lines = [a.shape[0] for a in own]
    packed = (sum(lines), half, LANES)
    far = pl.pallas_call(
        far_kernel,
        out_shape=shape(tiles, *packed),
        in_specs=[anywhere] * 3,
        out_specs=vmem,
        scratch_shapes=[pltpu.SemaphoreType.DMA((3 * tiles,))],
        compiler_params=params,
        name="far",
    )(*held(*own))
    *own, fy, fx, near = pl.pallas_call(
        own_kernel,
        out_shape=[shape(tiles, n, rows, LANES) for n in lines]
        + [shape(*factor_y.shape), shape(*factor_x.shape), [shape(*packed)] * tiles],
        in_specs=[anywhere] * 6,
        out_specs=[vmem] * 5 + [[vmem] * tiles],
        scratch_shapes=[
            pltpu.SemaphoreType.DMA((3 * tiles,)),
            pltpu.SemaphoreType.DMA((3 * tiles + 2,)),
        ],
        compiler_params=params,
        name="own",
    )(*held(*own, factor_y, factor_x), far)
    own = [a.reshape(tiles, -1, LANES) for a in own]
    far = far.reshape(tiles, -1, LANES)
    near = [a.reshape(-1, LANES) for a in near]
    far = lax.ppermute(far, "gx", [(i, (i - 1 + i % 2 * 2) % n_gx) for i in range(n_gx)])
    near = [lax.ppermute(a, "gx", [(i, i ^ 1) for i in range(n_gx)]) for a in near]
    own_fm = pl.pallas_call(
        member_kernel,
        out_shape=shape(members, LANES),
        in_specs=[anywhere, vmem],
        out_specs=vmem,
        compiler_params=params,
        name="member",
    )(near[-1], factor_m)
    other_fm = lax.ppermute(own_fm, "mem", [(0, 1), (1, 0)])
    sections = 2 * STEPS
    edges, early, turned_fy = pl.pallas_call(
        inner_kernel,
        out_shape=[
            shape(sections * 9 * members, cells_y),
            shape(2 * half * devices, LANES),
            shape(ry, cells_y),
        ],
        scratch_shapes=[pltpu.VMEM((3 * half * members, cells_y), jnp.float32)],
        compiler_params=params,
        name="inner",
    )(*own, fy, *near)
    height = rows + 2 * half
    sent = pl.pallas_call(
        functools.partial(outer_kernel, n_gx),
        out_shape=shape(devices * height, LANES),
        in_specs=[vmem] * 8 + [anywhere],
        out_specs=vmem,
        scratch_shapes=[pltpu.VMEM((3 * half * members, cells_y), jnp.float32)],
        compiler_params=params,
        name="outer",
    )(*own, far, turned_fy, edges, early, fx, other_fm)
    got = exchange(sent, devices)
    lows = rm // 2
    high = 3 * shares * lows * SUBLANES // LANES
    sent = pl.pallas_call(
        functools.partial(project_kernel, n_gx, rows, rm),
        out_shape=jax.ShapeDtypeStruct((devices * high, LANES), jnp.float32),
        scratch_shapes=[pltpu.VMEM((3, rx, LANES), jnp.float32)],
        compiler_params=params,
        name="project",
    )(got, own_fm, other_fm)
    got = exchange(sent, devices)
    core = pl.pallas_call(
        functools.partial(gather_kernel, shares, lows),
        out_shape=shape(lows, 3, SUBLANES, LANES),
        out_specs=anywhere,
        scratch_shapes=[
            pltpu.VMEM((3, lows, SUBLANES, LANES), jnp.float32),
            pltpu.SemaphoreType.DMA((3,)),
        ],
        compiler_params=params,
        name="gather",
    )(got)
    return core


def solution(mesh):
    return jax.shard_map(
        on_device,
        mesh=mesh,
        in_specs=(
            P("mem", "gx", None),
            P("mem", None, "gx", None),
            P(None, "gx", None),
            P("gx", None),
            P(),
            P("mem", None),
        ),
        out_specs=P("mem", None, "gx", None),
        check_vma=False,
    )
```

```python
import functools

import jax
import jax.numpy as jnp
from jax import lax
from jax.experimental import pallas as pl
from jax.experimental.pallas import tpu as pltpu
from jax.sharding import PartitionSpec as P

STEPS = 2


STIFF = 1.0
RELAX = 1.0
DTIME = 0.2

HIGHEST = lax.Precision.HIGHEST
HIGH = lax.Precision.HIGH
LANES = 128
SUBLANES = 8


def with_halo(cells, sides, width):
    for axis, dim in sides:
        count = lax.axis_size(axis)
        head = lax.slice_in_dim(cells, 0, width, axis=dim)
        tail = lax.slice_in_dim(cells, cells.shape[dim] - width, cells.shape[dim], axis=dim)
        cells = jnp.concatenate(
            [
                lax.ppermute(tail, axis, [(i, (i + 1) % count) for i in range(count)]),
                cells,
                lax.ppermute(head, axis, [((i + 1) % count, i) for i in range(count)]),
            ],
            axis=dim,
        )
    return cells


def tendency(fields, desired):
    density = fields[:, 0]
    moment_x = fields[:, 1]
    moment_y = fields[:, 2]
    speed_x = moment_x / density
    speed_y = moment_y / density
    sound = jnp.sqrt(STIFF * density)
    pressure = 0.5 * STIFF * density * density
    conserved = (density, moment_x, moment_y)
    fluxes_x = (moment_x, moment_x * speed_x + pressure, moment_y * speed_x)
    fluxes_y = (moment_y, moment_x * speed_y, moment_y * speed_y + pressure)
    reach_x = jnp.abs(speed_x) + sound
    bound_x = jnp.maximum(reach_x[:, :-1], reach_x[:, 1:])
    reach_y = (jnp.abs(speed_y) + sound)[:, 1:-1]
    bound_y = jnp.maximum(reach_y, jnp.roll(reach_y, -1, axis=-1))
    changes = []
    for quantity, normal_flux, cross_flux in zip(conserved, fluxes_x, fluxes_y):
        face_x = 0.5 * (normal_flux[:, :-1] + normal_flux[:, 1:]) - 0.5 * bound_x * (
            quantity[:, 1:] - quantity[:, :-1]
        )
        middle = quantity[:, 1:-1]
        cross_mid = cross_flux[:, 1:-1]
        face_y = 0.5 * (cross_mid + jnp.roll(cross_mid, -1, axis=-1)) - 0.5 * bound_y * (
            jnp.roll(middle, -1, axis=-1) - middle
        )
        changes.append(-(face_x[:, 1:] - face_x[:, :-1]) - (face_y - jnp.roll(face_y, 1, axis=-1)))
    centre = density[:, 1:-1]
    changes[1] = changes[1] + (centre * desired[0] - moment_x[:, 1:-1]) / RELAX
    changes[2] = changes[2] + (centre * desired[1] - moment_y[:, 1:-1]) / RELAX
    return jnp.stack(changes, axis=1)


def single_rims(fields):
    return with_halo(fields, (("gx", 2),), 1)


def plain(density, momenta, desired, factor_x, factor_y, factor_m):
    fields = jnp.concatenate([density[:, None], momenta], axis=1)
    for repeat in range(STEPS):
        sectioned = fields + DTIME * tendency(single_rims(fields), desired)
        second = sectioned + DTIME * tendency(single_rims(sectioned), desired)
        fields = 0.5 * fields + 0.5 * second
    along_y = jnp.einsum("mcxy,yb->mcxb", fields, factor_y, precision=HIGHEST)
    spread = lax.all_to_all(along_y, "gx", split_axis=3, concat_axis=2, tiled=True)
    projected = jnp.einsum(
        "mcxb,xa->mcab",
        spread,
        lax.all_gather(factor_x, "gx", axis=0, tiled=True),
        precision=HIGHEST,
    )
    returned = lax.all_to_all(projected, "gx", split_axis=2, concat_axis=3, tiled=True)
    member_terms = jnp.einsum("mcab,mk->kcab", returned, factor_m, precision=HIGHEST)
    return lax.psum_scatter(member_terms, "mem", scatter_dimension=0, tiled=True)


def cell_terms(q):
    rho, mx, my = q
    root = lax.rsqrt(rho)
    inverse = root * root
    sound = rho * root
    u = mx * inverse
    v = my * inverse
    pressure = (0.5 * STIFF) * (rho * rho)
    cross = my * u
    return dict(
        q=q,
        f=(mx, mx * u + pressure, cross),
        g=(my, cross, my * v + pressure),
        ax=jnp.abs(u) + sound,
        ay=jnp.abs(v) + sound,
    )


def x_face(low, high):
    bound = jnp.maximum(low["ax"], high["ax"])
    return tuple(
        fa + fb - bound * (b - a)
        for fa, fb, a, b in zip(low["f"], high["f"], low["q"], high["q"])
    )


def y_difference(row):
    axis = row["ay"].ndim - 1
    size = row["ay"].shape[axis]
    q = tuple(pltpu.roll(a, size - 1, axis) for a in row["q"])
    ahead = cell_terms(q)
    bound = jnp.maximum(row["ay"], ahead["ay"])
    face = tuple(
        ga + gb - bound * (b - a) for ga, gb, a, b in zip(row["g"], ahead["g"], row["q"], q)
    )
    return tuple(a - pltpu.roll(a, 1, axis) for a in face)


def section(row, low_face, high_face, wish):
    cross = y_difference(row)
    rho, mx, my = row["q"]
    half = 0.5 * DTIME
    spread = tuple(h + d for h, d in zip(high_face, cross))
    if low_face is not None:
        spread = tuple(a - l for a, l in zip(spread, low_face))
    keep = 1.0 - DTIME / RELAX
    return (
        rho - half * spread[0],
        keep * mx + rho * wish[0] - half * spread[1],
        keep * my + rho * wish[1] - half * spread[2],
    )


def half_copies(arrays, targets, odd, upper, sems):
    kinds = []
    for low in range(2):
        copies = []
        for t, target in enumerate(targets):
            base = 0
            for whole in arrays:
                lines, rows = whole.shape[:2]
                source = whole.at[:, pl.ds(low * (rows // 2), rows // 2), pl.ds(t * LANES, LANES)]
                copies.append((source, target.at[pl.ds(base, lines)]))
                base += lines
        kinds.append([
            pltpu.make_async_copy(source, target, sems.at[i])
            for i, (source, target) in enumerate(copies)
        ])
    for kind in range(2):

        @pl.when(odd == kind)
        def _():
            for copy in kinds[kind if upper else 1 - kind]:
                copy.start()

    return kinds[0]


def far_kernel(d, m, w, far, sems):
    odd = lax.rem(lax.axis_index("gx"), 2)
    targets = [far.at[t] for t in range(far.shape[0])]
    for copy in half_copies((d, m, w), targets, odd, 1, sems):
        copy.wait()


def own_kernel(d, m, w, fy, fx, far, own_d, own_m, own_w, own_fy, own_fx, near, half_sems, sems):
    tiles = own_d.shape[0]
    odd = lax.rem(lax.axis_index("gx"), 2)
    copies = half_copies((d, m, w), near, odd, 0, half_sems)
    wholes = []
    for whole, cut in ((d, own_d), (m, own_m), (w, own_w)):
        for t in range(tiles):
            wholes.append((whole.at[:, :, pl.ds(t * LANES, LANES)], cut.at[t]))
    wholes += [(fy, own_fy), (fx, own_fx)]
    wholes = [
        pltpu.make_async_copy(source, target, sems.at[i])
        for i, (source, target) in enumerate(wholes)
    ]
    for copy in wholes:
        copy.start()
    for copy in copies + wholes:
        copy.wait()


class Strip:
    def __init__(self, group, own, near, far, width=SUBLANES):
        self.width = width
        self.rows = own[2].shape[1] // 2
        self.half = self.rows // 2
        self.members = own[0].shape[1] // self.rows
        self.tiles = own[0].shape[0]
        cut = lambda ref: [ref.at[t] for t in range(self.tiles)]
        self.first, self.own = pl.multiple_of(group * width, SUBLANES), tuple(cut(a) for a in own)
        self.near = near
        self.far = None if far is None else cut(far)
        self.odd = lax.rem(lax.axis_index("gx"), 2)
        self.sign = (1 - 2 * self.odd).astype(jnp.float32)

    def every(self, ref, first, count, stride):
        parts = [ref[t][pl.ds(first, count, stride=stride), :] for t in range(self.tiles)]
        return jnp.concatenate(parts, axis=1)

    def place(self, x):
        if x < self.half:
            ref, at, lines = self.far, x, self.half
        elif x < self.half + self.rows:
            ref, at, lines = self.own, x - self.half, self.rows
        else:
            ref, at, lines = self.near, x - self.half - self.rows, self.half
        return ref, self.odd * (lines - 1) + (1 - 2 * self.odd) * at, lines

    def load(self, x):
        ref, at, lines = self.place(x)
        if ref is self.own:
            d, m = ref[0], ref[1]
            base = 0
        else:
            d = m = ref
            base = self.members * lines
        first = self.first
        rho = self.every(d, first * lines + at, self.width, lines)
        mx = self.every(m, base + first * 2 * lines + at, self.width, 2 * lines)
        my = self.every(m, base + (first * 2 + 1) * lines + at, self.width, 2 * lines)
        return rho, self.sign * mx, my

    def wish(self, x):
        ref, at, lines = self.place(x)
        if ref is self.own:
            ref, base = ref[2], 0
        else:
            base = 3 * self.members * lines
        line = [self.every(ref, base + c * lines + at, 1, 1) for c in range(2)]
        rate = DTIME / RELAX
        line = [(rate * self.sign) * line[0], rate * line[1]]
        return tuple(jnp.broadcast_to(a, (self.width, a.shape[1])) for a in line)

    def keep(self, state, x, q):
        for c, a in enumerate((q[0], self.sign * q[1], q[2])):
            at = (3 * x + c) * self.members + self.first
            state[pl.ds(at, self.width), :] = a


def march(computed, fetch, wish, emit, hook=None, bound=None):
    sections = len(computed) - 1
    known, terms, faces = {}, {}, {}

    def value(s, x):
        if (s, x) not in known:
            if x not in computed[s]:
                new = fetch(s, x)
            elif bound is not None and x == computed[s][-1]:
                share = 0.5 * DTIME * (0.5 if s % 2 == 0 else 1.0)
                new = tuple(
                    a + share * b for a, b in zip(bound(s - 1, x)["next"], face(s - 1, x - 1))
                )
            else:
                new = advanced(s, x, face(s - 1, x - 1))
            if x in computed[s]:
                emit(s, x, new)
            known[s, x] = new
        return known[s, x]

    def advanced(s, x, low):
        new = section(cell(s - 1, x), low, face(s - 1, x), wish(x))
        if s % 2 == 0:
            new = tuple(0.5 * (a + b) for a, b in zip(value(s - 2, x), new))
        return new

    def cell(s, x):
        if (s, x) not in terms:
            if bound is not None and x == computed[s + 1][-1]:
                terms[s, x] = bound(s, x)
            else:
                terms[s, x] = cell_terms(value(s, x))
        return terms[s, x]

    def face(s, x):
        if (s, x) not in faces:
            faces[s, x] = x_face(cell(s, x), cell(s, x + 1))
        return faces[s, x]

    for t in range(computed[1][0], computed[-1][-1] + sections + 1):
        for s in range(1, sections + 1):
            if t - s in computed[s]:
                value(s, t - s)
        if hook is not None:
            for s in range(sections):
                hook(s, t - s - 1, cell, advanced)


def edge_line(s, members):
    return s * 9 * members


def deal_columns(state, turned_fy, devices, members, lines):
    turned = lax.dot_general(
        turned_fy,
        state[...],
        (((1,), (1,)), ((), ())),
        precision=HIGH,
        preferred_element_type=jnp.float32,
    )
    shares = turned_fy.shape[0] // devices
    firsts, thirds = [], []
    for x in range(lines):
        at = 3 * x * members
        cut = lambda low, high: jnp.concatenate(
            [
                turned[r * devices : (r + 1) * devices, at + low : at + high]
                for r in range(shares)
            ],
            axis=1,
        )
        firsts.append(cut(0, 2 * members))
        thirds.append(cut(2 * members, 3 * members))
    return firsts, thirds


def member_kernel(near, fm, out):
    out[...] = jnp.concatenate([fm[...]] * (LANES // fm.shape[1]), axis=1)


def inner_kernel(own_d, own_m, own_w, fy, *rest):
    *near, edges, early, fy_out, state = rest
    rows = own_w.shape[1] // 2
    half = rows // 2
    members = own_d.shape[1] // rows
    sections = 2 * STEPS
    count = 2 * rows

    @pl.loop(0, members // SUBLANES)
    def _(group):
        strip = Strip(group, (own_d, own_m, own_w), near, None)

        def emit(s, x, q):
            if s == sections:
                strip.keep(state, x - rows, q)

        def hook(s, x, cell, advanced):
            if x == half + s:
                row = cell(s, x)
                arrays = (*row["q"], *row["f"][1:], row["ax"], *advanced(s + 1, x, None))
                for c, a in enumerate(arrays):
                    at = edge_line(s, members) + c * members + strip.first
                    edges[pl.ds(at, SUBLANES), :] = a

        computed = [range(0)] + [range(half + s, count - s) for s in range(1, sections + 1)]
        march(computed, lambda s, x: strip.load(x), strip.wish, emit, hook)

    devices = early.shape[0] // (2 * half)
    fy_out[...] = fy[...].T
    firsts, thirds = deal_columns(state, fy_out[...], devices, members, half)
    for i in range(half):
        early[pl.ds(i * devices, devices), :] = firsts[i]
        early[pl.ds((half + i) * devices, devices), :] = jnp.concatenate([thirds[i]] * 2, axis=1)


def outer_kernel(
    n_gx, own_d, own_m, own_w, far, fy, edges, early, fx, other_fm, out, state
):
    rows = own_w.shape[1] // 2
    half = rows // 2
    members = own_d.shape[1] // rows
    sections = 2 * STEPS
    strip = Strip(0, (own_d, own_m, own_w), None, far, members)

    @functools.cache
    def bound(s, x):
        at = edge_line(s, members) + strip.first
        a = [edges[pl.ds(at + c * members, members), :] for c in range(9)]
        return dict(q=tuple(a[:3]), f=(a[1], a[3], a[4]), ax=a[5], next=tuple(a[6:]))

    def fetch(s, x):
        return strip.load(x) if x < half else bound(s, x)["q"]

    def emit(s, x, q):
        if s == sections:
            strip.keep(state, x - half, q)

    computed = [range(0)] + [range(s, half + s) for s in range(1, sections + 1)]
    march(computed, fetch, strip.wish, emit, bound=bound)

    devices = 2 * n_gx
    height = out.shape[0] // devices
    firsts, thirds = deal_columns(state, fy[...], devices, members, half)
    middle = LANES // 2
    for i in range(half):
        out[pl.ds(i, devices, stride=height), :] = firsts[i]
        out[pl.ds(half + i, devices, stride=height), :] = early[pl.ds(i * devices, devices), :]
        other = early[pl.ds((half + i) * devices, devices), :]
        out[pl.ds(rows + i, devices, stride=height), :] = jnp.concatenate(
            [thirds[i], other[:, middle:]], axis=1
        )
    mem = lax.axis_index("mem")
    for r in range(half):
        line = fx[pl.ds(mem * half + r, 1), :]
        out[pl.ds(rows + half + r, devices, stride=height), :] = jnp.broadcast_to(
            line, (devices, line.shape[1])
        )


def project_kernel(n_gx, rows, rm, inp, own_fm, other_fm, out, tall):
    devices = 2 * n_gx
    members = n_gx
    height = inp.shape[0] // devices
    half = rows // 2
    middle = LANES // 2
    low_rank = rm // 2
    line = lambda j: inp[pl.ds(j, devices, stride=height), :]
    swap = lambda a: pltpu.roll(a, middle, 1)
    lane = lax.broadcasted_iota(jnp.int32, (members, LANES), 1)
    firsts = [line(x) for x in range(rows)]
    firsts = jnp.concatenate(
        [
            jnp.concatenate([a[mem * n_gx : (mem + 1) * n_gx] for a in firsts], axis=0)
            for mem in range(2)
        ],
        axis=1,
    )
    thirds = [line(rows + i) for i in range(half)]
    pairs = [(a[:n_gx], a[n_gx:]) for a in thirds]
    thirds = jnp.concatenate(
        [jnp.where(lane < middle, a, swap(b)) for a, b in pairs]
        + [jnp.where(lane < middle, swap(a), b) for a, b in pairs],
        axis=0,
    )
    first = lax.axis_index("mem") == 0
    a, b = own_fm[...], other_fm[...]
    fm = jnp.concatenate([jnp.where(first, a, b), jnp.where(first, b, a)], axis=0)
    wide = lax.broadcasted_iota(jnp.int32, fm.shape, 1)
    first_half = wide % rm < low_rank
    repeated = (
        jnp.where(first_half, fm, pltpu.roll(fm, low_rank, 1)),
        jnp.where(first_half, pltpu.roll(fm, LANES - low_rank, 1), fm),
    )
    block = lane // low_rank
    part = lambda k, mem: repeated[k][mem * members : (mem + 1) * members]
    count = LANES // members
    diagonal = jnp.concatenate(
        [
            jnp.concatenate(
                [jnp.where(block == p, part(k, mem), 0.0) for mem in range(2) for p in range(count)],
                axis=0,
            )
            for k in range(2)
        ],
        axis=1,
    )
    small = jnp.concatenate(
        [
            jnp.where(
                block == p,
                part(0, mem),
                jnp.where(block == count // 2 + p, part(1, mem), 0.0),
            )
            for mem in range(2)
            for p in range(count // 2)
        ],
        axis=0,
    )
    product = functools.partial(jnp.dot, precision=HIGH, preferred_element_type=jnp.float32)
    halves = [line(rows + half + r) for r in range(half)]
    lines = [a[:n_gx] for a in halves] + [a[n_gx:] for a in halves]
    odd = lax.broadcasted_iota(jnp.int32, (n_gx, LANES), 0) >= n_gx // 2
    lines = [jnp.where(odd, lines[rows - 1 - r], lines[r]) for r in range(rows)]
    fx = jnp.concatenate(lines, axis=0)
    turned_fx = fx.T
    both = product(turned_fx, jnp.concatenate([firsts, thirds], axis=1))
    firsts = product(both[:, : 2 * LANES], diagonal)
    thirds = product(both[:, 2 * LANES :], small)
    core = jnp.concatenate([firsts[:, :LANES], thirds, firsts[:, LANES:]], axis=1)
    high = out.shape[0] // devices
    for t in range(3):
        tall[t] = core[:, t * LANES : (t + 1) * LANES]
    pairs = n_gx // 2
    lane = lax.broadcasted_iota(jnp.int32, (pairs, LANES), 1)
    for odd in range(2):
        share = lambda t, a: tall[t, pl.ds(odd * SUBLANES + a, pairs, stride=2 * SUBLANES), :]
        spot = lambda k, i: pl.ds((k * n_gx + odd * pairs) * high + i, pairs, stride=high)
        for a in range(SUBLANES):
            for k in range(2):
                out[spot(k, a), :] = share(2 * k, a)
        for i in range(SUBLANES // 2):
            upper = share(1, i)
            lower = share(1, i + SUBLANES // 2)
            first = jnp.where(lane < middle, upper, swap(lower))
            second = jnp.where(lane < middle, swap(upper), lower)
            out[spot(0, SUBLANES + i), :] = first
            out[spot(1, SUBLANES + i), :] = second


def gather_kernel(shares, lows, inp, core, out, sems):
    devices = LANES // shares
    high = inp.shape[0] // devices
    quarter = SUBLANES // 2

    def turn(first):
        return jnp.concatenate(
            [inp[pl.ds(first + i, devices, stride=high), :] for i in range(quarter)], axis=0
        ).T

    def place(turned, base, apart, c, a0):
        for i in range(quarter):
            line = jnp.concatenate(
                [
                    turned[base + r * apart : base + r * apart + lows, i * devices : (i + 1) * devices]
                    for r in range(shares)
                ],
                axis=1,
            )
            out[c, :, a0 + i, :] = line

    def send(c):
        return pltpu.make_async_copy(out.at[c], core.at[:, c], sems.at[c])

    turned = [turn(h * quarter) for h in range(2)]
    for c in range(2):
        for h in range(2):
            place(turned[h], c * lows, 2 * lows, c, h * quarter)
        send(c).start()
    turned = turn(SUBLANES)
    for h in range(2):
        place(turned, h * shares * lows, lows, 2, h * quarter)
    send(2).start()
    for c in range(3):
        send(c).wait()


def exchange(chunks, devices):
    block = chunks.reshape(devices, chunks.shape[0] // devices, 1, chunks.shape[1])
    n_gx = lax.axis_size("gx")
    order = [mem * n_gx + i for mem in range(devices // n_gx) for odd in range(2) for i in range(odd, n_gx, 2)]
    moved = lax.all_to_all(
        block, ("mem", "gx"), split_axis=0, concat_axis=0, axis_index_groups=[order], tiled=True
    )
    return moved.reshape(chunks.shape)


def laid_out(density, factor_x, factor_y, factor_m):
    members, rows, cells_y = density.shape
    n_mem, n_gx = lax.axis_size("mem"), lax.axis_size("gx")
    rx, ry, rm = factor_x.shape[1], factor_y.shape[1], factor_m.shape[1]
    shares = ry // (n_mem * n_gx)
    return (
        n_mem == 2
        and rows == 4 * STEPS == SUBLANES
        and members == n_gx
        and n_gx % 2 == 0
        and members * rows == LANES
        and members % SUBLANES == 0
        and cells_y % LANES == 0
        and rx == LANES == n_gx * SUBLANES
        and ry == LANES == shares * n_mem * n_gx
        and shares * rm == LANES
        and shares * rm // 2 * 2 == LANES
        and 2 * shares * members == LANES
        and 2 * members == rm
    )


def on_device(density, momenta, desired, factor_x, factor_y, factor_m):
    if not laid_out(density, factor_x, factor_y, factor_m):
        return plain(density, momenta, desired, factor_x, factor_y, factor_m)
    members, rows, cells_y = density.shape
    n_gx = lax.axis_size("gx")
    devices = 2 * n_gx
    rx, ry, rm = factor_x.shape[1], factor_y.shape[1], factor_m.shape[1]
    shares = ry // devices
    params = pltpu.CompilerParams(vmem_limit_bytes=32 * 1024 * 1024)
    vmem = pl.BlockSpec(memory_space=pltpu.VMEM)
    anywhere = pl.BlockSpec(memory_space=pl.ANY)
    tiles = cells_y // LANES
    half = rows // 2
    shape = lambda *dims: jax.ShapeDtypeStruct(dims, jnp.float32)
    held = lambda *arrays: [pltpu.with_memory_space_constraint(a, pltpu.HBM) for a in arrays]
    own = [a.reshape(-1, rows, cells_y) for a in (density, momenta, desired)]
    lines = [a.shape[0] for a in own]
    packed = (sum(lines), half, LANES)
    far = pl.pallas_call(
        far_kernel,
        out_shape=shape(tiles, *packed),
        in_specs=[anywhere] * 3,
        out_specs=vmem,
        scratch_shapes=[pltpu.SemaphoreType.DMA((3 * tiles,))],
        compiler_params=params,
        name="far",
    )(*held(*own))
    *own, fy, fx, near = pl.pallas_call(
        own_kernel,
        out_shape=[shape(tiles, n, rows, LANES) for n in lines]
        + [shape(*factor_y.shape), shape(*factor_x.shape), [shape(*packed)] * tiles],
        in_specs=[anywhere] * 6,
        out_specs=[vmem] * 5 + [[vmem] * tiles],
        scratch_shapes=[
            pltpu.SemaphoreType.DMA((3 * tiles,)),
            pltpu.SemaphoreType.DMA((3 * tiles + 2,)),
        ],
        compiler_params=params,
        name="own",
    )(*held(*own, factor_y, factor_x), far)
    own = [a.reshape(tiles, -1, LANES) for a in own]
    far = far.reshape(tiles, -1, LANES)
    near = [a.reshape(-1, LANES) for a in near]
    far = lax.ppermute(far, "gx", [(i, (i - 1 + i % 2 * 2) % n_gx) for i in range(n_gx)])
    near = [lax.ppermute(a, "gx", [(i, i ^ 1) for i in range(n_gx)]) for a in near]
    own_fm = pl.pallas_call(
        member_kernel,
        out_shape=shape(members, LANES),
        in_specs=[anywhere, vmem],
        out_specs=vmem,
        compiler_params=params,
        name="member",
    )(near[-1], factor_m)
    other_fm = lax.ppermute(own_fm, "mem", [(0, 1), (1, 0)])
    sections = 2 * STEPS
    edges, early, turned_fy = pl.pallas_call(
        inner_kernel,
        out_shape=[
            shape(sections * 9 * members, cells_y),
            shape(2 * half * devices, LANES),
            shape(ry, cells_y),
        ],
        scratch_shapes=[pltpu.VMEM((3 * half * members, cells_y), jnp.float32)],
        compiler_params=params,
        name="inner",
    )(*own, fy, *near)
    height = rows + 2 * half
    sent = pl.pallas_call(
        functools.partial(outer_kernel, n_gx),
        out_shape=shape(devices * height, LANES),
        in_specs=[vmem] * 8 + [anywhere],
        out_specs=vmem,
        scratch_shapes=[pltpu.VMEM((3 * half * members, cells_y), jnp.float32)],
        compiler_params=params,
        name="outer",
    )(*own, far, turned_fy, edges, early, fx, other_fm)
    got = exchange(sent, devices)
    lows = rm // 2
    high = 3 * shares * lows * SUBLANES // LANES
    sent = pl.pallas_call(
        functools.partial(project_kernel, n_gx, rows, rm),
        out_shape=jax.ShapeDtypeStruct((devices * high, LANES), jnp.float32),
        scratch_shapes=[pltpu.VMEM((3, rx, LANES), jnp.float32)],
        compiler_params=params,
        name="project",
    )(got, own_fm, other_fm)
    got = exchange(sent, devices)
    core = pl.pallas_call(
        functools.partial(gather_kernel, shares, lows),
        out_shape=shape(lows, 3, SUBLANES, LANES),
        out_specs=anywhere,
        scratch_shapes=[
            pltpu.VMEM((3, lows, SUBLANES, LANES), jnp.float32),
            pltpu.SemaphoreType.DMA((3,)),
        ],
        compiler_params=params,
        name="gather",
    )(got)
    return core


def solution(mesh):
    return jax.shard_map(
        on_device,
        mesh=mesh,
        in_specs=(
            P("mem", "gx", None),
            P("mem", None, "gx", None),
            P(None, "gx", None),
            P("gx", None),
            P(),
            P("mem", None),
        ),
        out_specs=P("mem", None, "gx", None),
        check_vma=False,
    )
```

```python
import functools

import jax
import jax.numpy as jnp
from jax import lax
from jax.experimental import pallas as pl
from jax.experimental.pallas import tpu as pltpu
from jax.sharding import PartitionSpec as P

STEPS = 2


STIFF = 1.0
RELAX = 1.0
DTIME = 0.2

HIGHEST = lax.Precision.HIGHEST
HIGH = lax.Precision.HIGH
LANES = 128
SUBLANES = 8


def with_halo(cells, sides, width):
    for axis, dim in sides:
        count = lax.axis_size(axis)
        head = lax.slice_in_dim(cells, 0, width, axis=dim)
        tail = lax.slice_in_dim(cells, cells.shape[dim] - width, cells.shape[dim], axis=dim)
        cells = jnp.concatenate(
            [
                lax.ppermute(tail, axis, [(i, (i + 1) % count) for i in range(count)]),
                cells,
                lax.ppermute(head, axis, [((i + 1) % count, i) for i in range(count)]),
            ],
            axis=dim,
        )
    return cells


def tendency(fields, desired):
    density = fields[:, 0]
    moment_x = fields[:, 1]
    moment_y = fields[:, 2]
    speed_x = moment_x / density
    speed_y = moment_y / density
    sound = jnp.sqrt(STIFF * density)
    pressure = 0.5 * STIFF * density * density
    conserved = (density, moment_x, moment_y)
    fluxes_x = (moment_x, moment_x * speed_x + pressure, moment_y * speed_x)
    fluxes_y = (moment_y, moment_x * speed_y, moment_y * speed_y + pressure)
    reach_x = jnp.abs(speed_x) + sound
    bound_x = jnp.maximum(reach_x[:, :-1], reach_x[:, 1:])
    reach_y = (jnp.abs(speed_y) + sound)[:, 1:-1]
    bound_y = jnp.maximum(reach_y, jnp.roll(reach_y, -1, axis=-1))
    changes = []
    for quantity, normal_flux, cross_flux in zip(conserved, fluxes_x, fluxes_y):
        face_x = 0.5 * (normal_flux[:, :-1] + normal_flux[:, 1:]) - 0.5 * bound_x * (
            quantity[:, 1:] - quantity[:, :-1]
        )
        middle = quantity[:, 1:-1]
        cross_mid = cross_flux[:, 1:-1]
        face_y = 0.5 * (cross_mid + jnp.roll(cross_mid, -1, axis=-1)) - 0.5 * bound_y * (
            jnp.roll(middle, -1, axis=-1) - middle
        )
        changes.append(-(face_x[:, 1:] - face_x[:, :-1]) - (face_y - jnp.roll(face_y, 1, axis=-1)))
    centre = density[:, 1:-1]
    changes[1] = changes[1] + (centre * desired[0] - moment_x[:, 1:-1]) / RELAX
    changes[2] = changes[2] + (centre * desired[1] - moment_y[:, 1:-1]) / RELAX
    return jnp.stack(changes, axis=1)


def single_rims(fields):
    return with_halo(fields, (("gx", 2),), 1)


def plain(density, momenta, desired, factor_x, factor_y, factor_m):
    fields = jnp.concatenate([density[:, None], momenta], axis=1)
    for repeat in range(STEPS):
        sectioned = fields + DTIME * tendency(single_rims(fields), desired)
        second = sectioned + DTIME * tendency(single_rims(sectioned), desired)
        fields = 0.5 * fields + 0.5 * second
    along_y = jnp.einsum("mcxy,yb->mcxb", fields, factor_y, precision=HIGHEST)
    spread = lax.all_to_all(along_y, "gx", split_axis=3, concat_axis=2, tiled=True)
    projected = jnp.einsum(
        "mcxb,xa->mcab",
        spread,
        lax.all_gather(factor_x, "gx", axis=0, tiled=True),
        precision=HIGHEST,
    )
    returned = lax.all_to_all(projected, "gx", split_axis=2, concat_axis=3, tiled=True)
    member_terms = jnp.einsum("mcab,mk->kcab", returned, factor_m, precision=HIGHEST)
    return lax.psum_scatter(member_terms, "mem", scatter_dimension=0, tiled=True)


def cell_terms(q):
    rho, mx, my = q
    root = lax.rsqrt(rho)
    inverse = root * root
    sound = rho * root
    u = mx * inverse
    v = my * inverse
    pressure = (0.5 * STIFF) * (rho * rho)
    cross = my * u
    return dict(
        q=q,
        f=(mx, mx * u + pressure, cross),
        g=(my, cross, my * v + pressure),
        ax=jnp.abs(u) + sound,
        ay=jnp.abs(v) + sound,
    )


def x_face(low, high):
    bound = jnp.maximum(low["ax"], high["ax"])
    return tuple(
        fa + fb - bound * (b - a)
        for fa, fb, a, b in zip(low["f"], high["f"], low["q"], high["q"])
    )


def y_difference(row):
    axis = row["ay"].ndim - 1
    size = row["ay"].shape[axis]
    q = tuple(pltpu.roll(a, size - 1, axis) for a in row["q"])
    ahead = cell_terms(q)
    bound = jnp.maximum(row["ay"], ahead["ay"])
    face = tuple(
        ga + gb - bound * (b - a) for ga, gb, a, b in zip(row["g"], ahead["g"], row["q"], q)
    )
    return tuple(a - pltpu.roll(a, 1, axis) for a in face)


def section(row, low_face, high_face, wish):
    cross = y_difference(row)
    rho, mx, my = row["q"]
    half = 0.5 * DTIME
    spread = tuple(h + d for h, d in zip(high_face, cross))
    if low_face is not None:
        spread = tuple(a - l for a, l in zip(spread, low_face))
    keep = 1.0 - DTIME / RELAX
    return (
        rho - half * spread[0],
        keep * mx + rho * wish[0] - half * spread[1],
        keep * my + rho * wish[1] - half * spread[2],
    )


def half_copies(arrays, targets, odd, upper, sems):
    kinds = []
    for low in range(2):
        copies = []
        for t, target in enumerate(targets):
            base = 0
            for whole in arrays:
                lines, rows = whole.shape[:2]
                source = whole.at[:, pl.ds(low * (rows // 2), rows // 2), pl.ds(t * LANES, LANES)]
                copies.append((source, target.at[pl.ds(base, lines)]))
                base += lines
        kinds.append([
            pltpu.make_async_copy(source, target, sems.at[i])
            for i, (source, target) in enumerate(copies)
        ])
    for kind in range(2):

        @pl.when(odd == kind)
        def _():
            for copy in kinds[kind if upper else 1 - kind]:
                copy.start()

    return kinds[0]


def far_kernel(d, m, w, far, sems):
    odd = lax.rem(lax.axis_index("gx"), 2)
    targets = [far.at[t] for t in range(far.shape[0])]
    for copy in half_copies((d, m, w), targets, odd, 1, sems):
        copy.wait()


def near_kernel(d, m, w, far, *rest):
    *near, sems = rest
    odd = lax.rem(lax.axis_index("gx"), 2)
    for copy in half_copies((d, m, w), near, odd, 0, sems):
        copy.wait()


def own_kernel(d, m, w, fy, fx, near, own_d, own_m, own_w, own_fy, own_fx, sems):
    tiles = own_d.shape[0]
    pairs = []
    for whole, cut in ((d, own_d), (m, own_m), (w, own_w)):
        for t in range(tiles):
            pairs.append((whole.at[:, :, pl.ds(t * LANES, LANES)], cut.at[t]))
    pairs += [(fy, own_fy), (fx, own_fx)]
    copies = [
        pltpu.make_async_copy(source, target, sems.at[i])
        for i, (source, target) in enumerate(pairs)
    ]
    for copy in copies:
        copy.start()
    for copy in copies:
        copy.wait()


class Strip:
    def __init__(self, group, own, near, far, width=SUBLANES):
        self.width = width
        self.rows = own[2].shape[1] // 2
        self.half = self.rows // 2
        self.members = own[0].shape[1] // self.rows
        self.tiles = own[0].shape[0]
        cut = lambda ref: [ref.at[t] for t in range(self.tiles)]
        self.first, self.own = pl.multiple_of(group * width, SUBLANES), tuple(cut(a) for a in own)
        self.near = near
        self.far = None if far is None else cut(far)
        self.odd = lax.rem(lax.axis_index("gx"), 2)
        self.sign = (1 - 2 * self.odd).astype(jnp.float32)

    def every(self, ref, first, count, stride):
        parts = [ref[t][pl.ds(first, count, stride=stride), :] for t in range(self.tiles)]
        return jnp.concatenate(parts, axis=1)

    def place(self, x):
        if x < self.half:
            ref, at, lines = self.far, x, self.half
        elif x < self.half + self.rows:
            ref, at, lines = self.own, x - self.half, self.rows
        else:
            ref, at, lines = self.near, x - self.half - self.rows, self.half
        return ref, self.odd * (lines - 1) + (1 - 2 * self.odd) * at, lines

    def load(self, x):
        ref, at, lines = self.place(x)
        if ref is self.own:
            d, m = ref[0], ref[1]
            base = 0
        else:
            d = m = ref
            base = self.members * lines
        first = self.first
        rho = self.every(d, first * lines + at, self.width, lines)
        mx = self.every(m, base + first * 2 * lines + at, self.width, 2 * lines)
        my = self.every(m, base + (first * 2 + 1) * lines + at, self.width, 2 * lines)
        return rho, self.sign * mx, my

    def wish(self, x):
        ref, at, lines = self.place(x)
        if ref is self.own:
            ref, base = ref[2], 0
        else:
            base = 3 * self.members * lines
        line = [self.every(ref, base + c * lines + at, 1, 1) for c in range(2)]
        rate = DTIME / RELAX
        line = [(rate * self.sign) * line[0], rate * line[1]]
        return tuple(jnp.broadcast_to(a, (self.width, a.shape[1])) for a in line)

    def keep(self, state, x, q):
        for c, a in enumerate((q[0], self.sign * q[1], q[2])):
            at = (3 * x + c) * self.members + self.first
            state[pl.ds(at, self.width), :] = a


def march(computed, fetch, wish, emit, hook=None, bound=None):
    sections = len(computed) - 1
    known, terms, faces = {}, {}, {}

    def value(s, x):
        if (s, x) not in known:
            if x not in computed[s]:
                new = fetch(s, x)
            elif bound is not None and x == computed[s][-1]:
                share = 0.5 * DTIME * (0.5 if s % 2 == 0 else 1.0)
                new = tuple(
                    a + share * b for a, b in zip(bound(s - 1, x)["next"], face(s - 1, x - 1))
                )
            else:
                new = advanced(s, x, face(s - 1, x - 1))
            if x in computed[s]:
                emit(s, x, new)
            known[s, x] = new
        return known[s, x]

    def advanced(s, x, low):
        new = section(cell(s - 1, x), low, face(s - 1, x), wish(x))
        if s % 2 == 0:
            new = tuple(0.5 * (a + b) for a, b in zip(value(s - 2, x), new))
        return new

    def cell(s, x):
        if (s, x) not in terms:
            if bound is not None and x == computed[s + 1][-1]:
                terms[s, x] = bound(s, x)
            else:
                terms[s, x] = cell_terms(value(s, x))
        return terms[s, x]

    def face(s, x):
        if (s, x) not in faces:
            faces[s, x] = x_face(cell(s, x), cell(s, x + 1))
        return faces[s, x]

    for t in range(computed[1][0], computed[-1][-1] + sections + 1):
        for s in range(1, sections + 1):
            if t - s in computed[s]:
                value(s, t - s)
        if hook is not None:
            for s in range(sections):
                hook(s, t - s - 1, cell, advanced)


def edge_line(s, members):
    return s * 9 * members


def deal_columns(state, turned_fy, devices, members, lines):
    turned = lax.dot_general(
        turned_fy,
        state[...],
        (((1,), (1,)), ((), ())),
        precision=HIGH,
        preferred_element_type=jnp.float32,
    )
    shares = turned_fy.shape[0] // devices
    firsts, thirds = [], []
    for x in range(lines):
        at = 3 * x * members
        cut = lambda low, high: jnp.concatenate(
            [
                turned[r * devices : (r + 1) * devices, at + low : at + high]
                for r in range(shares)
            ],
            axis=1,
        )
        firsts.append(cut(0, 2 * members))
        thirds.append(cut(2 * members, 3 * members))
    return firsts, thirds


def member_kernel(near, own_w, fm, out):
    out[...] = jnp.concatenate([fm[...]] * (LANES // fm.shape[1]), axis=1)


def inner_kernel(own_d, own_m, own_w, fy, *rest):
    *near, edges, early, fy_out, state = rest
    rows = own_w.shape[1] // 2
    half = rows // 2
    members = own_d.shape[1] // rows
    sections = 2 * STEPS
    count = 2 * rows

    @pl.loop(0, members // SUBLANES)
    def _(group):
        strip = Strip(group, (own_d, own_m, own_w), near, None)

        def emit(s, x, q):
            if s == sections:
                strip.keep(state, x - rows, q)

        def hook(s, x, cell, advanced):
            if x == half + s:
                row = cell(s, x)
                arrays = (*row["q"], *row["f"][1:], row["ax"], *advanced(s + 1, x, None))
                for c, a in enumerate(arrays):
                    at = edge_line(s, members) + c * members + strip.first
                    edges[pl.ds(at, SUBLANES), :] = a

        computed = [range(0)] + [range(half + s, count - s) for s in range(1, sections + 1)]
        march(computed, lambda s, x: strip.load(x), strip.wish, emit, hook)

    devices = early.shape[0] // (2 * half)
    fy_out[...] = fy[...].T
    firsts, thirds = deal_columns(state, fy_out[...], devices, members, half)
    for i in range(half):
        early[pl.ds(i * devices, devices), :] = firsts[i]
        early[pl.ds((half + i) * devices, devices), :] = jnp.concatenate([thirds[i]] * 2, axis=1)


def outer_kernel(
    n_gx, own_d, own_m, own_w, far, fy, edges, early, fx, other_fm, out, state
):
    rows = own_w.shape[1] // 2
    half = rows // 2
    members = own_d.shape[1] // rows
    sections = 2 * STEPS
    strip = Strip(0, (own_d, own_m, own_w), None, far, members)

    @functools.cache
    def bound(s, x):
        at = edge_line(s, members) + strip.first
        a = [edges[pl.ds(at + c * members, members), :] for c in range(9)]
        return dict(q=tuple(a[:3]), f=(a[1], a[3], a[4]), ax=a[5], next=tuple(a[6:]))

    def fetch(s, x):
        return strip.load(x) if x < half else bound(s, x)["q"]

    def emit(s, x, q):
        if s == sections:
            strip.keep(state, x - half, q)

    computed = [range(0)] + [range(s, half + s) for s in range(1, sections + 1)]
    march(computed, fetch, strip.wish, emit, bound=bound)

    devices = 2 * n_gx
    height = out.shape[0] // devices
    firsts, thirds = deal_columns(state, fy[...], devices, members, half)
    middle = LANES // 2
    for i in range(half):
        out[pl.ds(i, devices, stride=height), :] = firsts[i]
        out[pl.ds(half + i, devices, stride=height), :] = early[pl.ds(i * devices, devices), :]
        other = early[pl.ds((half + i) * devices, devices), :]
        out[pl.ds(rows + i, devices, stride=height), :] = jnp.concatenate(
            [thirds[i], other[:, middle:]], axis=1
        )
    mem = lax.axis_index("mem")
    for r in range(half):
        line = fx[pl.ds(mem * half + r, 1), :]
        out[pl.ds(rows + half + r, devices, stride=height), :] = jnp.broadcast_to(
            line, (devices, line.shape[1])
        )


def project_kernel(n_gx, rows, rm, inp, own_fm, other_fm, out, tall):
    devices = 2 * n_gx
    members = n_gx
    height = inp.shape[0] // devices
    half = rows // 2
    middle = LANES // 2
    low_rank = rm // 2
    line = lambda j: inp[pl.ds(j, devices, stride=height), :]
    swap = lambda a: pltpu.roll(a, middle, 1)
    lane = lax.broadcasted_iota(jnp.int32, (members, LANES), 1)
    firsts = [line(x) for x in range(rows)]
    firsts = jnp.concatenate(
        [
            jnp.concatenate([a[mem * n_gx : (mem + 1) * n_gx] for a in firsts], axis=0)
            for mem in range(2)
        ],
        axis=1,
    )
    thirds = [line(rows + i) for i in range(half)]
    pairs = [(a[:n_gx], a[n_gx:]) for a in thirds]
    thirds = jnp.concatenate(
        [jnp.where(lane < middle, a, swap(b)) for a, b in pairs]
        + [jnp.where(lane < middle, swap(a), b) for a, b in pairs],
        axis=0,
    )
    first = lax.axis_index("mem") == 0
    a, b = own_fm[...], other_fm[...]
    fm = jnp.concatenate([jnp.where(first, a, b), jnp.where(first, b, a)], axis=0)
    wide = lax.broadcasted_iota(jnp.int32, fm.shape, 1)
    first_half = wide % rm < low_rank
    repeated = (
        jnp.where(first_half, fm, pltpu.roll(fm, low_rank, 1)),
        jnp.where(first_half, pltpu.roll(fm, LANES - low_rank, 1), fm),
    )
    block = lane // low_rank
    part = lambda k, mem: repeated[k][mem * members : (mem + 1) * members]
    count = LANES // members
    diagonal = jnp.concatenate(
        [
            jnp.concatenate(
                [jnp.where(block == p, part(k, mem), 0.0) for mem in range(2) for p in range(count)],
                axis=0,
            )
            for k in range(2)
        ],
        axis=1,
    )
    small = jnp.concatenate(
        [
            jnp.where(
                block == p,
                part(0, mem),
                jnp.where(block == count // 2 + p, part(1, mem), 0.0),
            )
            for mem in range(2)
            for p in range(count // 2)
        ],
        axis=0,
    )
    product = functools.partial(jnp.dot, precision=HIGH, preferred_element_type=jnp.float32)
    halves = [line(rows + half + r) for r in range(half)]
    lines = [a[:n_gx] for a in halves] + [a[n_gx:] for a in halves]
    odd = lax.broadcasted_iota(jnp.int32, (n_gx, LANES), 0) >= n_gx // 2
    lines = [jnp.where(odd, lines[rows - 1 - r], lines[r]) for r in range(rows)]
    fx = jnp.concatenate(lines, axis=0)
    turned_fx = fx.T
    both = product(turned_fx, jnp.concatenate([firsts, thirds], axis=1))
    firsts = product(both[:, : 2 * LANES], diagonal)
    thirds = product(both[:, 2 * LANES :], small)
    core = jnp.concatenate([firsts[:, :LANES], thirds, firsts[:, LANES:]], axis=1)
    high = out.shape[0] // devices
    for t in range(3):
        tall[t] = core[:, t * LANES : (t + 1) * LANES]
    pairs = n_gx // 2
    lane = lax.broadcasted_iota(jnp.int32, (pairs, LANES), 1)
    for odd in range(2):
        share = lambda t, a: tall[t, pl.ds(odd * SUBLANES + a, pairs, stride=2 * SUBLANES), :]
        spot = lambda k, i: pl.ds((k * n_gx + odd * pairs) * high + i, pairs, stride=high)
        for a in range(SUBLANES):
            for k in range(2):
                out[spot(k, a), :] = share(2 * k, a)
        for i in range(SUBLANES // 2):
            upper = share(1, i)
            lower = share(1, i + SUBLANES // 2)
            first = jnp.where(lane < middle, upper, swap(lower))
            second = jnp.where(lane < middle, swap(upper), lower)
            out[spot(0, SUBLANES + i), :] = first
            out[spot(1, SUBLANES + i), :] = second


def gather_kernel(shares, lows, inp, core, out, sems):
    devices = LANES // shares
    high = inp.shape[0] // devices
    quarter = SUBLANES // 2

    def turn(first):
        return jnp.concatenate(
            [inp[pl.ds(first + i, devices, stride=high), :] for i in range(quarter)], axis=0
        ).T

    def place(turned, base, apart, c, a0):
        for i in range(quarter):
            line = jnp.concatenate(
                [
                    turned[base + r * apart : base + r * apart + lows, i * devices : (i + 1) * devices]
                    for r in range(shares)
                ],
                axis=1,
            )
            out[c, :, a0 + i, :] = line

    def send(c):
        return pltpu.make_async_copy(out.at[c], core.at[:, c], sems.at[c])

    turned = [turn(h * quarter) for h in range(2)]
    for c in range(2):
        for h in range(2):
            place(turned[h], c * lows, 2 * lows, c, h * quarter)
        send(c).start()
    turned = turn(SUBLANES)
    for h in range(2):
        place(turned, h * shares * lows, lows, 2, h * quarter)
    send(2).start()
    for c in range(3):
        send(c).wait()


def exchange(chunks, devices):
    block = chunks.reshape(devices, chunks.shape[0] // devices, 1, chunks.shape[1])
    n_gx = lax.axis_size("gx")
    order = [mem * n_gx + i for mem in range(devices // n_gx) for odd in range(2) for i in range(odd, n_gx, 2)]
    moved = lax.all_to_all(
        block, ("mem", "gx"), split_axis=0, concat_axis=0, axis_index_groups=[order], tiled=True
    )
    return moved.reshape(chunks.shape)


def laid_out(density, factor_x, factor_y, factor_m):
    members, rows, cells_y = density.shape
    n_mem, n_gx = lax.axis_size("mem"), lax.axis_size("gx")
    rx, ry, rm = factor_x.shape[1], factor_y.shape[1], factor_m.shape[1]
    shares = ry // (n_mem * n_gx)
    return (
        n_mem == 2
        and rows == 4 * STEPS == SUBLANES
        and members == n_gx
        and n_gx % 2 == 0
        and members * rows == LANES
        and members % SUBLANES == 0
        and cells_y % LANES == 0
        and rx == LANES == n_gx * SUBLANES
        and ry == LANES == shares * n_mem * n_gx
        and shares * rm == LANES
        and shares * rm // 2 * 2 == LANES
        and 2 * shares * members == LANES
        and 2 * members == rm
    )


def on_device(density, momenta, desired, factor_x, factor_y, factor_m):
    if not laid_out(density, factor_x, factor_y, factor_m):
        return plain(density, momenta, desired, factor_x, factor_y, factor_m)
    members, rows, cells_y = density.shape
    n_gx = lax.axis_size("gx")
    devices = 2 * n_gx
    rx, ry, rm = factor_x.shape[1], factor_y.shape[1], factor_m.shape[1]
    shares = ry // devices
    params = pltpu.CompilerParams(vmem_limit_bytes=32 * 1024 * 1024)
    vmem = pl.BlockSpec(memory_space=pltpu.VMEM)
    anywhere = pl.BlockSpec(memory_space=pl.ANY)
    tiles = cells_y // LANES
    half = rows // 2
    shape = lambda *dims: jax.ShapeDtypeStruct(dims, jnp.float32)
    held = lambda *arrays: [pltpu.with_memory_space_constraint(a, pltpu.HBM) for a in arrays]
    own = [a.reshape(-1, rows, cells_y) for a in (density, momenta, desired)]
    lines = [a.shape[0] for a in own]
    packed = (sum(lines), half, LANES)
    far = pl.pallas_call(
        far_kernel,
        out_shape=shape(tiles, *packed),
        in_specs=[anywhere] * 3,
        out_specs=vmem,
        scratch_shapes=[pltpu.SemaphoreType.DMA((3 * tiles,))],
        compiler_params=params,
        name="far",
    )(*held(*own))
    near = pl.pallas_call(
        near_kernel,
        out_shape=[shape(*packed)] * tiles,
        in_specs=[anywhere] * 4,
        out_specs=[vmem] * tiles,
        scratch_shapes=[pltpu.SemaphoreType.DMA((3 * tiles,))],
        compiler_params=params,
        name="near",
    )(*held(*own), far)
    *own, fy, fx = pl.pallas_call(
        own_kernel,
        out_shape=[shape(tiles, n, rows, LANES) for n in lines]
        + [shape(*factor_y.shape), shape(*factor_x.shape)],
        in_specs=[anywhere] * 6,
        out_specs=[vmem] * 5,
        scratch_shapes=[pltpu.SemaphoreType.DMA((3 * tiles + 2,))],
        compiler_params=params,
        name="own",
    )(*held(*own, factor_y, factor_x), near[-1])
    own = [a.reshape(tiles, -1, LANES) for a in own]
    far = far.reshape(tiles, -1, LANES)
    near = [a.reshape(-1, LANES) for a in near]
    far = lax.ppermute(far, "gx", [(i, (i - 1 + i % 2 * 2) % n_gx) for i in range(n_gx)])
    near = [lax.ppermute(a, "gx", [(i, i ^ 1) for i in range(n_gx)]) for a in near]
    own_fm = pl.pallas_call(
        member_kernel,
        out_shape=shape(members, LANES),
        in_specs=[anywhere, anywhere, vmem],
        out_specs=vmem,
        compiler_params=params,
        name="member",
    )(near[-1], own[-1], factor_m)
    other_fm = lax.ppermute(own_fm, "mem", [(0, 1), (1, 0)])
    sections = 2 * STEPS
    edges, early, turned_fy = pl.pallas_call(
        inner_kernel,
        out_shape=[
            shape(sections * 9 * members, cells_y),
            shape(2 * half * devices, LANES),
            shape(ry, cells_y),
        ],
        scratch_shapes=[pltpu.VMEM((3 * half * members, cells_y), jnp.float32)],
        compiler_params=params,
        name="inner",
    )(*own, fy, *near)
    height = rows + 2 * half
    sent = pl.pallas_call(
        functools.partial(outer_kernel, n_gx),
        out_shape=shape(devices * height, LANES),
        in_specs=[vmem] * 8 + [anywhere],
        out_specs=vmem,
        scratch_shapes=[pltpu.VMEM((3 * half * members, cells_y), jnp.float32)],
        compiler_params=params,
        name="outer",
    )(*own, far, turned_fy, edges, early, fx, other_fm)
    got = exchange(sent, devices)
    lows = rm // 2
    high = 3 * shares * lows * SUBLANES // LANES
    sent = pl.pallas_call(
        functools.partial(project_kernel, n_gx, rows, rm),
        out_shape=jax.ShapeDtypeStruct((devices * high, LANES), jnp.float32),
        scratch_shapes=[pltpu.VMEM((3, rx, LANES), jnp.float32)],
        compiler_params=params,
        name="project",
    )(got, own_fm, other_fm)
    got = exchange(sent, devices)
    core = pl.pallas_call(
        functools.partial(gather_kernel, shares, lows),
        out_shape=shape(lows, 3, SUBLANES, LANES),
        out_specs=anywhere,
        scratch_shapes=[
            pltpu.VMEM((3, lows, SUBLANES, LANES), jnp.float32),
            pltpu.SemaphoreType.DMA((3,)),
        ],
        compiler_params=params,
        name="gather",
    )(got)
    return core


def solution(mesh):
    return jax.shard_map(
        on_device,
        mesh=mesh,
        in_specs=(
            P("mem", "gx", None),
            P("mem", None, "gx", None),
            P(None, "gx", None),
            P("gx", None),
            P(),
            P("mem", None),
        ),
        out_specs=P("mem", None, "gx", None),
        check_vma=False,
    )
```

```python
import functools

import jax
import jax.numpy as jnp
from jax import lax
from jax.experimental import pallas as pl
from jax.experimental.pallas import tpu as pltpu
from jax.sharding import PartitionSpec as P

STEPS = 2


STIFF = 1.0
RELAX = 1.0
DTIME = 0.2

HIGHEST = lax.Precision.HIGHEST
HIGH = lax.Precision.HIGH
LANES = 128
SUBLANES = 8


def with_halo(cells, sides, width):
    for axis, dim in sides:
        count = lax.axis_size(axis)
        head = lax.slice_in_dim(cells, 0, width, axis=dim)
        tail = lax.slice_in_dim(cells, cells.shape[dim] - width, cells.shape[dim], axis=dim)
        cells = jnp.concatenate(
            [
                lax.ppermute(tail, axis, [(i, (i + 1) % count) for i in range(count)]),
                cells,
                lax.ppermute(head, axis, [((i + 1) % count, i) for i in range(count)]),
            ],
            axis=dim,
        )
    return cells


def tendency(fields, desired):
    density = fields[:, 0]
    moment_x = fields[:, 1]
    moment_y = fields[:, 2]
    speed_x = moment_x / density
    speed_y = moment_y / density
    sound = jnp.sqrt(STIFF * density)
    pressure = 0.5 * STIFF * density * density
    conserved = (density, moment_x, moment_y)
    fluxes_x = (moment_x, moment_x * speed_x + pressure, moment_y * speed_x)
    fluxes_y = (moment_y, moment_x * speed_y, moment_y * speed_y + pressure)
    reach_x = jnp.abs(speed_x) + sound
    bound_x = jnp.maximum(reach_x[:, :-1], reach_x[:, 1:])
    reach_y = (jnp.abs(speed_y) + sound)[:, 1:-1]
    bound_y = jnp.maximum(reach_y, jnp.roll(reach_y, -1, axis=-1))
    changes = []
    for quantity, normal_flux, cross_flux in zip(conserved, fluxes_x, fluxes_y):
        face_x = 0.5 * (normal_flux[:, :-1] + normal_flux[:, 1:]) - 0.5 * bound_x * (
            quantity[:, 1:] - quantity[:, :-1]
        )
        middle = quantity[:, 1:-1]
        cross_mid = cross_flux[:, 1:-1]
        face_y = 0.5 * (cross_mid + jnp.roll(cross_mid, -1, axis=-1)) - 0.5 * bound_y * (
            jnp.roll(middle, -1, axis=-1) - middle
        )
        changes.append(-(face_x[:, 1:] - face_x[:, :-1]) - (face_y - jnp.roll(face_y, 1, axis=-1)))
    centre = density[:, 1:-1]
    changes[1] = changes[1] + (centre * desired[0] - moment_x[:, 1:-1]) / RELAX
    changes[2] = changes[2] + (centre * desired[1] - moment_y[:, 1:-1]) / RELAX
    return jnp.stack(changes, axis=1)


def single_rims(fields):
    return with_halo(fields, (("gx", 2),), 1)


def plain(density, momenta, desired, factor_x, factor_y, factor_m):
    fields = jnp.concatenate([density[:, None], momenta], axis=1)
    for repeat in range(STEPS):
        sectioned = fields + DTIME * tendency(single_rims(fields), desired)
        second = sectioned + DTIME * tendency(single_rims(sectioned), desired)
        fields = 0.5 * fields + 0.5 * second
    along_y = jnp.einsum("mcxy,yb->mcxb", fields, factor_y, precision=HIGHEST)
    spread = lax.all_to_all(along_y, "gx", split_axis=3, concat_axis=2, tiled=True)
    projected = jnp.einsum(
        "mcxb,xa->mcab",
        spread,
        lax.all_gather(factor_x, "gx", axis=0, tiled=True),
        precision=HIGHEST,
    )
    returned = lax.all_to_all(projected, "gx", split_axis=2, concat_axis=3, tiled=True)
    member_terms = jnp.einsum("mcab,mk->kcab", returned, factor_m, precision=HIGHEST)
    return lax.psum_scatter(member_terms, "mem", scatter_dimension=0, tiled=True)


def cell_terms(q):
    rho, mx, my = q
    root = lax.rsqrt(rho)
    inverse = root * root
    sound = rho * root
    u = mx * inverse
    v = my * inverse
    pressure = (0.5 * STIFF) * (rho * rho)
    cross = my * u
    return dict(
        q=q,
        f=(mx, mx * u + pressure, cross),
        g=(my, cross, my * v + pressure),
        ax=jnp.abs(u) + sound,
        ay=jnp.abs(v) + sound,
    )


def x_face(low, high):
    bound = jnp.maximum(low["ax"], high["ax"])
    return tuple(
        fa + fb - bound * (b - a)
        for fa, fb, a, b in zip(low["f"], high["f"], low["q"], high["q"])
    )


def y_difference(row):
    axis = row["ay"].ndim - 1
    size = row["ay"].shape[axis]
    q = tuple(pltpu.roll(a, size - 1, axis) for a in row["q"])
    ahead = cell_terms(q)
    bound = jnp.maximum(row["ay"], ahead["ay"])
    face = tuple(
        ga + gb - bound * (b - a) for ga, gb, a, b in zip(row["g"], ahead["g"], row["q"], q)
    )
    return tuple(a - pltpu.roll(a, 1, axis) for a in face)


def section(row, low_face, high_face, wish):
    cross = y_difference(row)
    rho, mx, my = row["q"]
    half = 0.5 * DTIME
    spread = tuple(h + d for h, d in zip(high_face, cross))
    if low_face is not None:
        spread = tuple(a - l for a, l in zip(spread, low_face))
    keep = 1.0 - DTIME / RELAX
    return (
        rho - half * spread[0],
        keep * mx + rho * wish[0] - half * spread[1],
        keep * my + rho * wish[1] - half * spread[2],
    )


def half_copies(arrays, targets, odd, upper, sems):
    kinds = []
    for low in range(2):
        copies = []
        for t, target in enumerate(targets):
            base = 0
            for whole in arrays:
                lines, rows = whole.shape[:2]
                source = whole.at[:, pl.ds(low * (rows // 2), rows // 2), pl.ds(t * LANES, LANES)]
                copies.append((source, target.at[pl.ds(base, lines)]))
                base += lines
        kinds.append([
            pltpu.make_async_copy(source, target, sems.at[i])
            for i, (source, target) in enumerate(copies)
        ])
    for kind in range(2):

        @pl.when(odd == kind)
        def _():
            for copy in kinds[kind if upper else 1 - kind]:
                copy.start()

    return kinds[0]


def far_kernel(d, m, w, far, sems):
    odd = lax.rem(lax.axis_index("gx"), 2)
    targets = [far.at[t] for t in range(far.shape[0])]
    for copy in half_copies((d, m, w), targets, odd, 1, sems):
        copy.wait()


def own_kernel(d, m, w, fy, fx, far, own_d, own_m, own_w, own_fy, own_fx, near, half_sems, sems):
    tiles = own_d.shape[0]
    odd = lax.rem(lax.axis_index("gx"), 2)
    copies = half_copies((d, m, w), near, odd, 0, half_sems)
    wholes = []
    for whole, cut in ((d, own_d), (m, own_m), (w, own_w)):
        for t in range(tiles):
            wholes.append((whole.at[:, :, pl.ds(t * LANES, LANES)], cut.at[t]))
    wholes += [(fy, own_fy), (fx, own_fx)]
    wholes = [
        pltpu.make_async_copy(source, target, sems.at[i])
        for i, (source, target) in enumerate(wholes)
    ]
    for copy in wholes:
        copy.start()
    for copy in copies + wholes:
        copy.wait()


class Strip:
    def __init__(self, group, own, near, far, width=SUBLANES):
        self.width = width
        self.rows = own[2].shape[1] // 2
        self.half = self.rows // 2
        self.members = own[0].shape[1] // self.rows
        self.tiles = own[0].shape[0]
        cut = lambda ref: [ref.at[t] for t in range(self.tiles)]
        self.first, self.own = pl.multiple_of(group * width, SUBLANES), tuple(cut(a) for a in own)
        self.near = near
        self.far = None if far is None else cut(far)
        self.odd = lax.rem(lax.axis_index("gx"), 2)
        self.sign = (1 - 2 * self.odd).astype(jnp.float32)

    def every(self, ref, first, count, stride):
        parts = [ref[t][pl.ds(first, count, stride=stride), :] for t in range(self.tiles)]
        return jnp.concatenate(parts, axis=1)

    def place(self, x):
        if x < self.half:
            ref, at, lines = self.far, x, self.half
        elif x < self.half + self.rows:
            ref, at, lines = self.own, x - self.half, self.rows
        else:
            ref, at, lines = self.near, x - self.half - self.rows, self.half
        return ref, self.odd * (lines - 1) + (1 - 2 * self.odd) * at, lines

    def load(self, x):
        ref, at, lines = self.place(x)
        if ref is self.own:
            d, m = ref[0], ref[1]
            base = 0
        else:
            d = m = ref
            base = self.members * lines
        first = self.first
        rho = self.every(d, first * lines + at, self.width, lines)
        mx = self.every(m, base + first * 2 * lines + at, self.width, 2 * lines)
        my = self.every(m, base + (first * 2 + 1) * lines + at, self.width, 2 * lines)
        return rho, self.sign * mx, my

    def wish(self, x):
        ref, at, lines = self.place(x)
        if ref is self.own:
            ref, base = ref[2], 0
        else:
            base = 3 * self.members * lines
        line = [self.every(ref, base + c * lines + at, 1, 1) for c in range(2)]
        rate = DTIME / RELAX
        line = [(rate * self.sign) * line[0], rate * line[1]]
        return tuple(jnp.broadcast_to(a, (self.width, a.shape[1])) for a in line)

    def keep(self, state, x, q):
        for c, a in enumerate((q[0], self.sign * q[1], q[2])):
            at = (3 * x + c) * self.members + self.first
            state[pl.ds(at, self.width), :] = a


def march(computed, fetch, wish, emit, hook=None, bound=None):
    sections = len(computed) - 1
    known, terms, faces = {}, {}, {}

    def value(s, x):
        if (s, x) not in known:
            if x not in computed[s]:
                new = fetch(s, x)
            elif bound is not None and x == computed[s][-1]:
                share = 0.5 * DTIME * (0.5 if s % 2 == 0 else 1.0)
                new = tuple(
                    a + share * b for a, b in zip(bound(s - 1, x)["next"], face(s - 1, x - 1))
                )
            else:
                new = advanced(s, x, face(s - 1, x - 1))
            if x in computed[s]:
                emit(s, x, new)
            known[s, x] = new
        return known[s, x]

    def advanced(s, x, low):
        new = section(cell(s - 1, x), low, face(s - 1, x), wish(x))
        if s % 2 == 0:
            new = tuple(0.5 * (a + b) for a, b in zip(value(s - 2, x), new))
        return new

    def cell(s, x):
        if (s, x) not in terms:
            if bound is not None and x == computed[s + 1][-1]:
                terms[s, x] = bound(s, x)
            else:
                terms[s, x] = cell_terms(value(s, x))
        return terms[s, x]

    def face(s, x):
        if (s, x) not in faces:
            faces[s, x] = x_face(cell(s, x), cell(s, x + 1))
        return faces[s, x]

    for t in range(computed[1][0], computed[-1][-1] + sections + 1):
        for s in range(1, sections + 1):
            if t - s in computed[s]:
                value(s, t - s)
        if hook is not None:
            for s in range(sections):
                hook(s, t - s - 1, cell, advanced)


def edge_line(s, members):
    return s * 9 * members


def deal_columns(state, turned_fy, devices, members, lines):
    turned = lax.dot_general(
        turned_fy,
        state[...],
        (((1,), (1,)), ((), ())),
        precision=HIGH,
        preferred_element_type=jnp.float32,
    )
    shares = turned_fy.shape[0] // devices
    firsts, thirds = [], []
    for x in range(lines):
        at = 3 * x * members
        cut = lambda low, high: jnp.concatenate(
            [
                turned[r * devices : (r + 1) * devices, at + low : at + high]
                for r in range(shares)
            ],
            axis=1,
        )
        firsts.append(cut(0, 2 * members))
        thirds.append(cut(2 * members, 3 * members))
    return firsts, thirds


def member_kernel(near, fm, out):
    out[...] = jnp.concatenate([fm[...]] * (LANES // fm.shape[1]), axis=1)


def inner_kernel(own_d, own_m, own_w, fy, *rest):
    *near, edges, early, fy_out, state = rest
    rows = own_w.shape[1] // 2
    half = rows // 2
    members = own_d.shape[1] // rows
    sections = 2 * STEPS
    count = 2 * rows

    @pl.loop(0, members // SUBLANES)
    def _(group):
        strip = Strip(group, (own_d, own_m, own_w), near, None)

        def emit(s, x, q):
            if s == sections:
                strip.keep(state, x - rows, q)

        def hook(s, x, cell, advanced):
            if x == half + s:
                row = cell(s, x)
                arrays = (*row["q"], *row["f"][1:], row["ax"], *advanced(s + 1, x, None))
                for c, a in enumerate(arrays):
                    at = edge_line(s, members) + c * members + strip.first
                    edges[pl.ds(at, SUBLANES), :] = a

        computed = [range(0)] + [range(half + s, count - s) for s in range(1, sections + 1)]
        march(computed, lambda s, x: strip.load(x), strip.wish, emit, hook)

    devices = early.shape[0] // (2 * half)
    fy_out[...] = fy[...].T
    firsts, thirds = deal_columns(state, fy_out[...], devices, members, half)
    for i in range(half):
        early[pl.ds(i * devices, devices), :] = firsts[i]
        early[pl.ds((half + i) * devices, devices), :] = jnp.concatenate([thirds[i]] * 2, axis=1)


def outer_kernel(
    n_gx, own_d, own_m, own_w, far, fy, edges, early, fx, other_fm, out, state
):
    rows = own_w.shape[1] // 2
    half = rows // 2
    members = own_d.shape[1] // rows
    sections = 2 * STEPS
    strip = Strip(0, (own_d, own_m, own_w), None, far, members)

    @functools.cache
    def bound(s, x):
        at = edge_line(s, members) + strip.first
        a = [edges[pl.ds(at + c * members, members), :] for c in range(9)]
        return dict(q=tuple(a[:3]), f=(a[1], a[3], a[4]), ax=a[5], next=tuple(a[6:]))

    def fetch(s, x):
        return strip.load(x) if x < half else bound(s, x)["q"]

    def emit(s, x, q):
        if s == sections:
            strip.keep(state, x - half, q)

    computed = [range(0)] + [range(s, half + s) for s in range(1, sections + 1)]
    march(computed, fetch, strip.wish, emit, bound=bound)

    devices = 2 * n_gx
    height = out.shape[0] // devices
    firsts, thirds = deal_columns(state, fy[...], devices, members, half)
    middle = LANES // 2
    for i in range(half):
        out[pl.ds(i, devices, stride=height), :] = firsts[i]
        out[pl.ds(half + i, devices, stride=height), :] = early[pl.ds(i * devices, devices), :]
        other = early[pl.ds((half + i) * devices, devices), :]
        out[pl.ds(rows + i, devices, stride=height), :] = jnp.concatenate(
            [thirds[i], other[:, middle:]], axis=1
        )
    mem = lax.axis_index("mem")
    for r in range(half):
        line = fx[pl.ds(mem * half + r, 1), :]
        out[pl.ds(rows + half + r, devices, stride=height), :] = jnp.broadcast_to(
            line, (devices, line.shape[1])
        )


def project_kernel(n_gx, rows, rm, inp, own_fm, other_fm, out, tall):
    devices = 2 * n_gx
    members = n_gx
    height = inp.shape[0] // devices
    half = rows // 2
    middle = LANES // 2
    low_rank = rm // 2
    line = lambda j: inp[pl.ds(j, devices, stride=height), :]
    swap = lambda a: pltpu.roll(a, middle, 1)
    lane = lax.broadcasted_iota(jnp.int32, (members, LANES), 1)
    firsts = [line(x) for x in range(rows)]
    firsts = jnp.concatenate(
        [
            jnp.concatenate([a[mem * n_gx : (mem + 1) * n_gx] for a in firsts], axis=0)
            for mem in range(2)
        ],
        axis=1,
    )
    thirds = [line(rows + i) for i in range(half)]
    pairs = [(a[:n_gx], a[n_gx:]) for a in thirds]
    thirds = jnp.concatenate(
        [jnp.where(lane < middle, a, swap(b)) for a, b in pairs]
        + [jnp.where(lane < middle, swap(a), b) for a, b in pairs],
        axis=0,
    )
    first = lax.axis_index("mem") == 0
    a, b = own_fm[...], other_fm[...]
    fm = jnp.concatenate([jnp.where(first, a, b), jnp.where(first, b, a)], axis=0)
    wide = lax.broadcasted_iota(jnp.int32, fm.shape, 1)
    first_half = wide % rm < low_rank
    repeated = (
        jnp.where(first_half, fm, pltpu.roll(fm, low_rank, 1)),
        jnp.where(first_half, pltpu.roll(fm, LANES - low_rank, 1), fm),
    )
    block = lane // low_rank
    part = lambda k, mem: repeated[k][mem * members : (mem + 1) * members]
    count = LANES // members
    diagonal = jnp.concatenate(
        [
            jnp.concatenate(
                [jnp.where(block == p, part(k, mem), 0.0) for mem in range(2) for p in range(count)],
                axis=0,
            )
            for k in range(2)
        ],
        axis=1,
    )
    small = jnp.concatenate(
        [
            jnp.where(
                block == p,
                part(0, mem),
                jnp.where(block == count // 2 + p, part(1, mem), 0.0),
            )
            for mem in range(2)
            for p in range(count // 2)
        ],
        axis=0,
    )
    product = functools.partial(jnp.dot, precision=HIGH, preferred_element_type=jnp.float32)
    halves = [line(rows + half + r) for r in range(half)]
    lines = [a[:n_gx] for a in halves] + [a[n_gx:] for a in halves]
    odd = lax.broadcasted_iota(jnp.int32, (n_gx, LANES), 0) >= n_gx // 2
    lines = [jnp.where(odd, lines[rows - 1 - r], lines[r]) for r in range(rows)]
    fx = jnp.concatenate(lines, axis=0)
    turned_fx = fx.T
    both = product(turned_fx, jnp.concatenate([firsts, thirds], axis=1))
    firsts = product(both[:, : 2 * LANES], diagonal)
    thirds = product(both[:, 2 * LANES :], small)
    high = out.shape[0] // devices
    for t, part in enumerate((firsts[:, :LANES], thirds, firsts[:, LANES:])):
        tall[t] = part
    pairs = n_gx // 2
    lane = lax.broadcasted_iota(jnp.int32, (pairs, LANES), 1)
    for odd in range(2):
        share = lambda t, a: tall[t, pl.ds(odd * SUBLANES + a, pairs, stride=2 * SUBLANES), :]
        spot = lambda k, i: pl.ds((k * n_gx + odd * pairs) * high + i, pairs, stride=high)
        for a in range(SUBLANES):
            for k in range(2):
                out[spot(k, a), :] = share(2 * k, a)
        for i in range(SUBLANES // 2):
            upper = share(1, i)
            lower = share(1, i + SUBLANES // 2)
            first = jnp.where(lane < middle, upper, swap(lower))
            second = jnp.where(lane < middle, swap(upper), lower)
            out[spot(0, SUBLANES + i), :] = first
            out[spot(1, SUBLANES + i), :] = second


def gather_kernel(shares, lows, inp, core, out, sems):
    devices = LANES // shares
    high = inp.shape[0] // devices
    quarter = SUBLANES // 2

    def turn(first):
        return jnp.concatenate(
            [inp[pl.ds(first + i, devices, stride=high), :] for i in range(quarter)], axis=0
        ).T

    def place(turned, base, apart, c, a0):
        for i in range(quarter):
            line = jnp.concatenate(
                [
                    turned[base + r * apart : base + r * apart + lows, i * devices : (i + 1) * devices]
                    for r in range(shares)
                ],
                axis=1,
            )
            out[c, :, a0 + i, :] = line

    def send(c):
        return pltpu.make_async_copy(out.at[c], core.at[:, c], sems.at[c])

    turned = [turn(h * quarter) for h in range(2)]
    for c in range(2):
        for h in range(2):
            place(turned[h], c * lows, 2 * lows, c, h * quarter)
        send(c).start()
    turned = turn(SUBLANES)
    for h in range(2):
        place(turned, h * shares * lows, lows, 2, h * quarter)
    send(2).start()
    for c in range(3):
        send(c).wait()


def exchange(chunks, devices):
    block = chunks.reshape(devices, chunks.shape[0] // devices, 1, chunks.shape[1])
    n_gx = lax.axis_size("gx")
    order = [mem * n_gx + i for mem in range(devices // n_gx) for odd in range(2) for i in range(odd, n_gx, 2)]
    moved = lax.all_to_all(
        block, ("mem", "gx"), split_axis=0, concat_axis=0, axis_index_groups=[order], tiled=True
    )
    return moved.reshape(chunks.shape)


def laid_out(density, factor_x, factor_y, factor_m):
    members, rows, cells_y = density.shape
    n_mem, n_gx = lax.axis_size("mem"), lax.axis_size("gx")
    rx, ry, rm = factor_x.shape[1], factor_y.shape[1], factor_m.shape[1]
    shares = ry // (n_mem * n_gx)
    return (
        n_mem == 2
        and rows == 4 * STEPS == SUBLANES
        and members == n_gx
        and n_gx % 2 == 0
        and members * rows == LANES
        and members % SUBLANES == 0
        and cells_y % LANES == 0
        and rx == LANES == n_gx * SUBLANES
        and ry == LANES == shares * n_mem * n_gx
        and shares * rm == LANES
        and shares * rm // 2 * 2 == LANES
        and 2 * shares * members == LANES
        and 2 * members == rm
    )


def on_device(density, momenta, desired, factor_x, factor_y, factor_m):
    if not laid_out(density, factor_x, factor_y, factor_m):
        return plain(density, momenta, desired, factor_x, factor_y, factor_m)
    members, rows, cells_y = density.shape
    n_gx = lax.axis_size("gx")
    devices = 2 * n_gx
    rx, ry, rm = factor_x.shape[1], factor_y.shape[1], factor_m.shape[1]
    shares = ry // devices
    params = pltpu.CompilerParams(vmem_limit_bytes=32 * 1024 * 1024)
    vmem = pl.BlockSpec(memory_space=pltpu.VMEM)
    anywhere = pl.BlockSpec(memory_space=pl.ANY)
    tiles = cells_y // LANES
    half = rows // 2
    shape = lambda *dims: jax.ShapeDtypeStruct(dims, jnp.float32)
    held = lambda *arrays: [pltpu.with_memory_space_constraint(a, pltpu.HBM) for a in arrays]
    own = [a.reshape(-1, rows, cells_y) for a in (density, momenta, desired)]
    lines = [a.shape[0] for a in own]
    packed = (sum(lines), half, LANES)
    far = pl.pallas_call(
        far_kernel,
        out_shape=shape(tiles, *packed),
        in_specs=[anywhere] * 3,
        out_specs=vmem,
        scratch_shapes=[pltpu.SemaphoreType.DMA((3 * tiles,))],
        compiler_params=params,
        name="far",
    )(*held(*own))
    *own, fy, fx, near = pl.pallas_call(
        own_kernel,
        out_shape=[shape(tiles, n, rows, LANES) for n in lines]
        + [shape(*factor_y.shape), shape(*factor_x.shape), [shape(*packed)] * tiles],
        in_specs=[anywhere] * 6,
        out_specs=[vmem] * 5 + [[vmem] * tiles],
        scratch_shapes=[
            pltpu.SemaphoreType.DMA((3 * tiles,)),
            pltpu.SemaphoreType.DMA((3 * tiles + 2,)),
        ],
        compiler_params=params,
        name="own",
    )(*held(*own, factor_y, factor_x), far)
    own = [a.reshape(tiles, -1, LANES) for a in own]
    far = far.reshape(tiles, -1, LANES)
    near = [a.reshape(-1, LANES) for a in near]
    far = lax.ppermute(far, "gx", [(i, (i - 1 + i % 2 * 2) % n_gx) for i in range(n_gx)])
    near = [lax.ppermute(a, "gx", [(i, i ^ 1) for i in range(n_gx)]) for a in near]
    own_fm = pl.pallas_call(
        member_kernel,
        out_shape=shape(members, LANES),
        in_specs=[anywhere, vmem],
        out_specs=vmem,
        compiler_params=params,
        name="member",
    )(near[-1], factor_m)
    other_fm = lax.ppermute(own_fm, "mem", [(0, 1), (1, 0)])
    sections = 2 * STEPS
    edges, early, turned_fy = pl.pallas_call(
        inner_kernel,
        out_shape=[
            shape(sections * 9 * members, cells_y),
            shape(2 * half * devices, LANES),
            shape(ry, cells_y),
        ],
        scratch_shapes=[pltpu.VMEM((3 * half * members, cells_y), jnp.float32)],
        compiler_params=params,
        name="inner",
    )(*own, fy, *near)
    height = rows + 2 * half
    sent = pl.pallas_call(
        functools.partial(outer_kernel, n_gx),
        out_shape=shape(devices * height, LANES),
        in_specs=[vmem] * 8 + [anywhere],
        out_specs=vmem,
        scratch_shapes=[pltpu.VMEM((3 * half * members, cells_y), jnp.float32)],
        compiler_params=params,
        name="outer",
    )(*own, far, turned_fy, edges, early, fx, other_fm)
    got = exchange(sent, devices)
    lows = rm // 2
    high = 3 * shares * lows * SUBLANES // LANES
    sent = pl.pallas_call(
        functools.partial(project_kernel, n_gx, rows, rm),
        out_shape=jax.ShapeDtypeStruct((devices * high, LANES), jnp.float32),
        scratch_shapes=[pltpu.VMEM((3, rx, LANES), jnp.float32)],
        compiler_params=params,
        name="project",
    )(got, own_fm, other_fm)
    got = exchange(sent, devices)
    core = pl.pallas_call(
        functools.partial(gather_kernel, shares, lows),
        out_shape=shape(lows, 3, SUBLANES, LANES),
        out_specs=anywhere,
        scratch_shapes=[
            pltpu.VMEM((3, lows, SUBLANES, LANES), jnp.float32),
            pltpu.SemaphoreType.DMA((3,)),
        ],
        compiler_params=params,
        name="gather",
    )(got)
    return core


def solution(mesh):
    return jax.shard_map(
        on_device,
        mesh=mesh,
        in_specs=(
            P("mem", "gx", None),
            P("mem", None, "gx", None),
            P(None, "gx", None),
            P("gx", None),
            P(),
            P("mem", None),
        ),
        out_specs=P("mem", None, "gx", None),
        check_vma=False,
    )
```
